32 devices in a mesh: ctx: 2 (over y), exp: 16 (over z, x, core).
Axes of the slice: x: 2, y: 2, z: 4, core: 2. Of those that a mesh axis runs over, the one named last changes fastest.
Arguments:
- tokens: bfloat16 [16, 256, 2048], P('exp', 'ctx'), may hold values from -6 to 6
- queries: bfloat16 [16, 256, 1024], P('exp', 'ctx'), may hold values from -60 to 60
- keys: bfloat16 [16, 256, 1024], P('exp', 'ctx'), may hold values from -4 to 4
- values: bfloat16 [16, 256, 1024], P('exp', 'ctx'), may hold values from -12 to 12
- out_proj: bfloat16 [1024, 2048], replicated, may hold values from -0.1875 to 0.1875
- mod_scale: float32 [16, 2048], P('exp'), may hold values from -2.5 to 2.5
- mod_shift: float32 [16, 2048], P('exp'), may hold values from -2.5 to 2.5
- expert_ids: int32 [16, 256, 2], P('exp', 'ctx'), may hold values from 0 to 7, all different within a row; in each aligned block of 128 rows (0 to 127, 128 to 255, ..., all dimensions but the last counted through in order) at most 48 rows name the same one
- gates: float32 [16, 256, 2], P('exp', 'ctx'), may hold values from 0.2 to 1
- w_gate: bfloat16 [8192, 2048], P(('ctx', 'exp')), may hold values from -0.125 to 0.125
- w_up: bfloat16 [8192, 2048], P(('ctx', 'exp')), may hold values from -0.125 to 0.125
- w_down: bfloat16 [8192, 2048], P(('ctx', 'exp')), may hold values from -0.1875 to 0.1875
- out_grad: bfloat16 [16, 256, 2048], P('exp', 'ctx'), may hold values from -0.1875 to 0.1875
Outputs:
- layer_out: bfloat16 [16, 256, 2048], P('exp', 'ctx')
- grad_gate: bfloat16 [8192, 2048], P(('ctx', 'exp'))
- grad_up: bfloat16 [8192, 2048], P(('ctx', 'exp'))
- grad_down: bfloat16 [8192, 2048], P(('ctx', 'exp'))
The draws below stay inside these ranges and needn't reach their ends.
Inputs may be any that keep to these rules, and one draw needn't show every extreme that they name: `expert_ids`: the two ids of a token differ. Among the 128 tokens of one device no expert is named more than 48 times, and in some device some expert exactly 48 times.
All inputs are finite; a program needn't handle non-finite values.
Results may differ from the reference program's by a relative error of at most 0.0075.
Values may be sent and summed in bfloat16 or wider, within the bound.
No kernel may reach another device: no remote copies, remote signals or barrier semaphores. Data moves between devices by JAX's collectives and lax.ppermute only.
A program may use at most 128 MiB of HBM per device.

```python
import math
import jax
import jax.numpy as jnp
import numpy as np
from jax import lax

D = 2048
F = 1024
HEADS = 8
HD = 128
SHARDS = 4
TOK_DEV = 128
SEQS = 16
LENGTH = 256
EXPERTS = 8
CAP = 48
FS = 256
N_CTX = 2


def attention_pair(key):
    shape = (SEQS, LENGTH, HEADS * HD)
    key_base = jax.random.fold_in(key, 101)
    query_base = jax.random.fold_in(key, 202)
    key_draw = jax.random.truncated_normal(key_base, -4.0, 4.0, shape, jnp.float32)
    query_draw = jax.random.truncated_normal(query_base, -4.0, 4.0, shape, jnp.float32)
    return (query_draw, key_draw)


def draw_queries(key, part):
    return attention_pair(key)[0].astype(jnp.bfloat16)


def draw_keys(key, part):
    return attention_pair(key)[1].astype(jnp.bfloat16)


def levels(key, extent, cuts, smallest, top_value):
    gain, own = 1.0, jax.random.fold_in(key, 6)
    for dim, shards_of in cuts:
        steps = jnp.exp(jax.random.uniform(jax.random.fold_in(own, dim), (shards_of,), jnp.float32, smallest / len(cuts), top_value / len(cuts)))
        gain = gain * jnp.repeat(steps, extent[dim] // shards_of).reshape([-1 if axis == dim else 1 for axis in range(len(extent))])
    return gain


def routed_block(key, own, number, rows, number_of, top, most, slope):
    order = jax.random.permutation(key, number_of)
    heavy_load, common = load_shares(number_of, rows * top, most, slope, True), load_shares(number_of, rows * top, most, slope, False)
    places = jnp.arange(number_of)

    def named(lengths, rotation):
        used = int((lengths > 0).sum())
        fixed = max(1, used // 4)
        shifted = fixed + (places - fixed + rotation * (used - fixed)) % max(1, number_of - fixed)
        return jnp.zeros((number_of,), jnp.int32).at[order[jnp.where(places < fixed, places, shifted)]].set(jnp.asarray(lengths, jnp.int32))

    lengths = jnp.where(number % 4 == 0, named(heavy_load, number // 4), named(common, number - number // 4 - 1))
    mixed = jax.random.permutation(jax.random.fold_in(own, 3), number_of)
    giver, receiver = mixed[0:number_of // 2 * 2:2], mixed[1:number_of // 2 * 2:2]
    slack = jnp.minimum(lengths[giver] - 1, most - lengths[receiver]) // 2
    slack = jnp.where((giver == order[0]) | (receiver == order[0]) | (lengths[receiver] == 0), 0, jnp.maximum(slack, 0))
    shifted = jax.random.randint(jax.random.fold_in(own, 4), (number_of // 2,), 0, 1 << 20) % (slack + 1)
    lengths = lengths.at[giver].add(-shifted).at[receiver].add(shifted)
    members = jnp.searchsorted(jnp.cumsum(lengths), jnp.arange(rows * top), side="right").astype(jnp.int32)
    grid = members.reshape(top, rows).T
    grid = grid[jax.random.permutation(jax.random.fold_in(own, 1), rows)]
    rotation = jax.random.randint(jax.random.fold_in(own, 2), (rows, 1), 0, top)
    return jnp.take_along_axis(grid, (jnp.arange(top)[None, :] + rotation) % top, axis=1)


def load_shares(count, total, bound, slope, full):
    loads = [(1 << 20) // math.isqrt(rank ** slope) + 1 for rank in range(1, count + 1)]
    largest = bound if full else min(bound, max(-(-total // count), total * loads[0] // sum(loads)))
    least = 1 if total - largest >= count - 1 else 0
    holding, surplus = [largest] + [least] * (count - 1), total - largest - least * (count - 1)
    while surplus > 0:
        candidates = [i for i in range(1, count) if holding[i] < largest] or [i for i in range(1, count) if holding[i] < bound]
        pool, remaining = sum([loads[i] for i in candidates]), surplus
        for i in candidates:
            more = min(bound - holding[i], max(1, remaining * loads[i] // pool), surplus)
            holding[i] = holding[i] + more
            surplus = surplus - more
    return np.array(holding)


def gaussian(stream_key, extent, deviation, most, split=(), held_as=jnp.bfloat16):
    level = levels(stream_key, extent, split, -0.22, 0.18) if split else 1.0
    values = jax.random.normal(stream_key, extent, jnp.float32) * deviation * level
    return jnp.minimum(jnp.maximum(values, -most), most).astype(held_as)


def setup_inputs(seed: int = 0) -> dict:
    key_of = jax.random.split(jax.random.key(seed), 14)
    tokens = gaussian(key_of[0], (SEQS, LENGTH, D), 1.0, 6.0, ((0, 16), (1, 2)))
    queries = draw_queries(jax.random.fold_in(key_of[13], 71), 0)
    keys = draw_keys(jax.random.fold_in(key_of[13], 71), 0)
    values = gaussian(key_of[3], (SEQS, LENGTH, HEADS * HD), 3.0, 12.0, ((0, 16), (1, 2)))
    out_proj = gaussian(key_of[4], (HEADS * HD, D), (HEADS * HD) ** -0.5, 0.1875)
    mod_scale = gaussian(key_of[5], (SEQS, D), 0.3, 2.5, ((0, 16),), jnp.float32)
    mod_shift = gaussian(key_of[6], (SEQS, D), 0.5, 2.5, ((0, 16),), jnp.float32)
    expert_ids_keys = jax.random.split(jax.random.fold_in(key_of[7], 1), SEQS * LENGTH // TOK_DEV)
    expert_ids_turns = jax.random.permutation(jax.random.fold_in(key_of[7], 3), SEQS * LENGTH // TOK_DEV)
    expert_ids = jax.vmap(lambda own, number: routed_block(jax.random.fold_in(key_of[7], 2), own, number, TOK_DEV, EXPERTS, 2, CAP, 2))(expert_ids_keys, expert_ids_turns).reshape((SEQS, LENGTH, 2))
    gates = jnp.clip(jnp.exp(math.log(1.0) - 1.609438 * jax.random.uniform(key_of[8], (SEQS, LENGTH, 2), jnp.float32) ** levels(key_of[8], (SEQS, LENGTH, 2), ((0, 16), (1, 2)), -0.2, 0.2)), 0.2, 1.0)
    w_gate = gaussian(key_of[9], (EXPERTS * F, D), D ** -0.5, 0.125, ((0, 32),))
    w_up = gaussian(key_of[10], (EXPERTS * F, D), D ** -0.5, 0.125, ((0, 32),))
    w_down = gaussian(key_of[11], (EXPERTS * F, D), F ** -0.5, 0.1875, ((0, 32),))
    out_grad = gaussian(key_of[12], (SEQS, LENGTH, D), 0.03, 0.1875, ((0, 16), (1, 2)))
    return {"tokens": tokens, "queries": queries, "keys": keys, "values": values, "out_proj": out_proj, "mod_scale": mod_scale, "mod_shift": mod_shift, "expert_ids": expert_ids, "gates": gates, "w_gate": w_gate, "w_up": w_up, "w_down": w_down, "out_grad": out_grad}


def attend(bundle):
    query_seq, key_seq, value_seq = bundle
    length = query_seq.shape[0]
    query_heads = query_seq.astype(jnp.float32).reshape(length, HEADS, HD)
    key_heads = key_seq.astype(jnp.float32).reshape(length, HEADS, HD)
    value_heads = value_seq.astype(jnp.float32).reshape(length, HEADS, HD)
    scores = jnp.einsum('qhd,khd->hqk', query_heads, key_heads) * HD ** (-0.5)
    row_top = lax.optimization_barrier(jnp.max(scores, axis=-1, keepdims=True))
    exponent = jnp.exp(scores - row_top)
    denominator = lax.optimization_barrier(jnp.sum(exponent, axis=-1))
    rounded = lax.optimization_barrier(exponent.astype(jnp.bfloat16))
    mixed_heads = jnp.einsum('hqk,khd->hqd', rounded.astype(jnp.float32), value_heads) / denominator[..., None]
    return jnp.transpose(mixed_heads, (1, 0, 2)).reshape(length, HEADS * HD).astype(jnp.bfloat16)

def by_device(source_array):
    trailing = source_array.shape[2:]
    shaped = source_array.reshape((SEQS, N_CTX, TOK_DEV) + trailing)
    return jnp.swapaxes(shaped, 0, 1).reshape((N_CTX * SEQS, TOK_DEV) + trailing)

def expert_pass(bundle):
    expert_rows, row_grads, weight_gate, weight_up, weight_down = bundle
    gate_pre = jnp.dot(expert_rows, weight_gate.T, preferred_element_type=jnp.float32)
    up_pre = jnp.dot(expert_rows, weight_up.T, preferred_element_type=jnp.float32)
    sigmoid_gate = jax.nn.sigmoid(gate_pre)
    activation = gate_pre * sigmoid_gate
    hidden = (activation * up_pre).astype(jnp.bfloat16)
    expert_out = jnp.zeros((expert_rows.shape[0], D), jnp.float32)
    for shard_index in range(SHARDS):
        lower = shard_index * FS
        piece_out = jnp.dot(hidden[:, lower:lower + FS], weight_down[lower:lower + FS], preferred_element_type=jnp.float32)
        piece_out = lax.optimization_barrier(piece_out.astype(jnp.bfloat16))
        expert_out = expert_out + piece_out.astype(jnp.float32)
    hidden_grad = jnp.dot(row_grads, weight_down.T, preferred_element_type=jnp.float32)
    gate_cot = (hidden_grad * up_pre * sigmoid_gate * (1.0 + gate_pre * (1.0 - sigmoid_gate))).astype(jnp.bfloat16)
    up_cot = (hidden_grad * activation).astype(jnp.bfloat16)
    grad_down = jnp.dot(hidden.T, row_grads, preferred_element_type=jnp.float32).astype(jnp.bfloat16)
    grad_gate = jnp.dot(gate_cot.T, expert_rows, preferred_element_type=jnp.float32).astype(jnp.bfloat16)
    grad_up = jnp.dot(up_cot.T, expert_rows, preferred_element_type=jnp.float32).astype(jnp.bfloat16)
    return (expert_out, grad_gate, grad_up, grad_down)

def reference(tokens, queries, keys, values, out_proj, mod_scale, mod_shift, expert_ids, gates, w_gate, w_up, w_down, out_grad):
    attended = lax.map(attend, (queries, keys, values))
    projected = jnp.dot(attended.reshape(SEQS * LENGTH, HEADS * HD), out_proj, preferred_element_type=jnp.float32)
    mixed = tokens.astype(jnp.float32) + projected.reshape(SEQS, LENGTH, D)
    mean_square = lax.optimization_barrier(jnp.mean(mixed * mixed, axis=-1, keepdims=True))
    normed = (mixed * lax.rsqrt(mean_square + 1e-06) * (1.0 + mod_scale[:, None, :]) + mod_shift[:, None, :]).astype(jnp.bfloat16)
    devices = N_CTX * SEQS
    chosen = by_device(expert_ids).reshape(devices, 2 * TOK_DEV)
    one_hot = (chosen[:, :, None] == jnp.arange(EXPERTS, dtype=jnp.int32)[None, None, :]).astype(jnp.int32)
    before = jnp.cumsum(one_hot, axis=1) - one_hot
    slot_index = lax.optimization_barrier(jnp.sum(one_hot * before, axis=2))
    sources = jnp.broadcast_to(jnp.arange(devices, dtype=jnp.int32)[:, None], chosen.shape)
    flat_pos = ((chosen * devices + sources) * CAP + slot_index).reshape(-1).astype(jnp.int32)
    normed_rows = jnp.repeat(by_device(normed).reshape(devices * TOK_DEV, D), 2, axis=0)
    gate_flat = by_device(gates).reshape(-1)
    cot_rows = jnp.repeat(by_device(out_grad).reshape(devices * TOK_DEV, D), 2, axis=0)
    grad_rows = (gate_flat[:, None] * cot_rows.astype(jnp.float32)).astype(jnp.bfloat16)
    slot_count = EXPERTS * devices * CAP
    inputs = jnp.zeros((slot_count, D), jnp.bfloat16).at[flat_pos].set(normed_rows).reshape(EXPERTS, devices * CAP, D)
    cotangents = jnp.zeros((slot_count, D), jnp.bfloat16).at[flat_pos].set(grad_rows).reshape(EXPERTS, devices * CAP, D)
    expert_results = lax.map(expert_pass, (inputs, cotangents, w_gate.reshape(EXPERTS, F, D), w_up.reshape(EXPERTS, F, D), w_down.reshape(EXPERTS, F, D)))
    expert_out = expert_results[0].reshape(slot_count, D)
    picked = jnp.take(expert_out, flat_pos, axis=0)
    weighted = lax.optimization_barrier(jnp.sum((gate_flat[:, None] * picked).reshape(devices, TOK_DEV, 2, D), axis=2))
    weighted = jnp.swapaxes(weighted.reshape(N_CTX, SEQS, TOK_DEV, D), 0, 1).reshape(SEQS, LENGTH, D)
    layer_out = (mixed + weighted).astype(jnp.bfloat16)
    return (layer_out, expert_results[1].reshape(EXPERTS * F, D), expert_results[2].reshape(EXPERTS * F, D), expert_results[3].reshape(EXPERTS * F, D))
```

```python
import functools

import jax
import jax.numpy as jnp
from jax import lax
from jax.experimental import pallas as pl
from jax.experimental.pallas import tpu as pltpu
from jax.sharding import PartitionSpec as P

HEADS = 8
HD = 128
SHARDS = 4
UNIT = 48
VMEM_LIMIT = 48 * 1024 * 1024
AXES = ("ctx", "exp")

NT = (((1,), (1,)), ((), ()))
TN = (((0,), (0,)), ((), ()))


def dot(a, b, dims=(((1,), (0,)), ((), ()))):
    return lax.dot_general(a, b, dims, preferred_element_type=jnp.float32)


def params():
    return pltpu.CompilerParams(vmem_limit_bytes=VMEM_LIMIT)


VMEM = functools.partial(pl.BlockSpec, memory_space=pltpu.VMEM)
SMEM = functools.partial(pl.BlockSpec, memory_space=pltpu.SMEM)
ANY = functools.partial(pl.BlockSpec, memory_space=pl.ANY)


def choosers(pos, slots):
    tokens = pos.shape[0]
    line = lax.broadcasted_iota(jnp.int32, (tokens, slots), 1)
    return [(pos[:, k : k + 1] == line).astype(jnp.bfloat16) for k in range(2)]


def slot_kernel(capacity, slots, me_ref, ids_ref, gates_ref, grad_ref, pos_ref, *unit_refs):
    ids = ids_ref[...]
    tokens = ids.shape[0]
    lanes = lax.broadcasted_iota(jnp.int32, (tokens, 128), 1)
    hot = [(ids[:, k : k + 1] == lanes).astype(jnp.float32) for k in range(2)]
    later = lax.broadcasted_iota(jnp.int32, (tokens, tokens), 0)
    earlier = lax.broadcasted_iota(jnp.int32, (tokens, tokens), 1)
    lower = (later > earlier).astype(jnp.bfloat16)
    before = dot(lower, (hot[0] + hot[1]).astype(jnp.bfloat16))
    me = me_ref[0]
    pos = []
    for k in range(2):
        slot = jnp.sum(hot[k] * before, axis=1, keepdims=True).astype(jnp.int32)
        pos.append((ids[:, k : k + 1] ^ me) * capacity + slot)
    pair = lax.broadcasted_iota(jnp.int32, (tokens, 2), 1)
    pos = jnp.where(pair == 0, pos[0], pos[1])
    pos_ref[...] = pos
    pick = choosers(pos, slots)
    grad = grad_ref[...].astype(jnp.float32)
    gates = gates_ref[...]
    placed = 0.0
    for k in range(2):
        rows = (gates[:, k : k + 1] * grad).astype(jnp.bfloat16)
        placed = placed + dot(pick[k], rows, TN)
    store_units(placed, unit_refs)


def store_units(placed, unit_refs):
    placed = placed.astype(jnp.bfloat16)
    rows = unit_refs[0].shape[0]
    for n, ref in enumerate(unit_refs):
        ref[...] = placed[n * rows : (n + 1) * rows]


def attend_kernel(pieces, *refs):
    query_ref = refs[0]
    key_refs = refs[1 : 1 + pieces]
    value_refs = refs[1 + pieces : 1 + 2 * pieces]
    token_ref, proj_ref, scale_ref, shift_ref, pos_ref = refs[1 + 2 * pieces : 6 + 2 * pieces]
    mixed_ref = refs[6 + 2 * pieces]
    unit_refs = refs[7 + 2 * pieces : -1]
    attended_ref = refs[-1]
    for head in range(HEADS):
        cols = slice(head * HD, (head + 1) * HD)
        query = query_ref[:, cols]
        scores = [dot(query, ref[:, cols], NT) * (HD ** (-0.5)) for ref in key_refs]
        top = functools.reduce(
            jnp.maximum, [jnp.max(piece, axis=1, keepdims=True) for piece in scores]
        )
        weights = [jnp.exp(piece - top) for piece in scores]
        total = functools.reduce(
            jnp.add, [jnp.sum(piece, axis=1, keepdims=True) for piece in weights]
        )
        accum = functools.reduce(
            jnp.add,
            [
                dot(piece.astype(jnp.bfloat16), ref[:, cols])
                for piece, ref in zip(weights, value_refs)
            ],
        )
        attended_ref[:, cols] = (accum / total).astype(jnp.bfloat16)
    mixed = token_ref[...].astype(jnp.float32) + dot(attended_ref[...], proj_ref[...])
    mixed_ref[...] = mixed
    mean_square = jnp.mean(mixed * mixed, axis=1, keepdims=True)
    normed = mixed * lax.rsqrt(mean_square + 1e-06) * (1.0 + scale_ref[...]) + shift_ref[...]
    normed = normed.astype(jnp.bfloat16)
    slots = len(unit_refs) * unit_refs[0].shape[0]
    pick = choosers(pos_ref[...], slots)
    store_units(dot(pick[0] + pick[1], normed, TN), unit_refs)


def load_rows(block_refs, rows_ref, sem):
    copies = []
    for n, ref in enumerate(block_refs):
        rows = ref.shape[0]
        copies.append(
            pltpu.make_async_copy(ref, rows_ref.at[pl.ds(n * rows, rows)], sem.at[n])
        )
    for copy in copies:
        copy.start()
    return copies


def forward_kernel(count, *refs):
    blocks = refs[:count]
    gate_ref, up_ref, down_ref, keep_ref, send_ref, gate_pre_ref, up_pre_ref, rows_ref, sem = refs[
        count:
    ]
    for copy in load_rows(blocks, rows_ref, sem):
        copy.wait()
    rows = rows_ref[...]
    gate_pre = dot(rows, gate_ref[...], NT)
    up_pre = dot(rows, up_ref[...], NT)
    gate_pre_ref[...] = gate_pre
    up_pre_ref[...] = up_pre
    hidden = (gate_pre * jax.nn.sigmoid(gate_pre) * up_pre).astype(jnp.bfloat16)
    half = rows.shape[0] // 2
    send_ref[...] = dot(hidden[half:], down_ref[...]).astype(jnp.bfloat16)
    keep_ref[...] = dot(hidden[:half], down_ref[...]).astype(jnp.bfloat16)


def forward(blocks, w_gate, w_up, w_down):
    rows = sum(block.shape[0] for block in blocks)
    fs, width = w_gate.shape
    half = jax.ShapeDtypeStruct((rows // 2, width), jnp.bfloat16)
    pre = jax.ShapeDtypeStruct((rows, fs), jnp.float32)
    return pl.pallas_call(
        functools.partial(forward_kernel, len(blocks)),
        out_shape=(half, half, pre, pre),
        in_specs=[ANY()] * len(blocks) + [VMEM()] * 3,
        out_specs=[VMEM()] * 4,
        scratch_shapes=[
            pltpu.VMEM((rows, width), jnp.bfloat16),
            pltpu.SemaphoreType.DMA((len(blocks),)),
        ],
        compiler_params=params(),
        cost_estimate=pl.CostEstimate(
            flops=6 * rows * fs * width, bytes_accessed=8 * rows * width, transcendentals=0
        ),
        name="forward",
    )(*blocks, w_gate, w_up, w_down)


def backward_kernel(chunks, count, *refs):
    gate_pre_refs = refs[:chunks]
    up_pre_refs = refs[chunks : 2 * chunks]
    rows_in = refs[2 * chunks : 2 * chunks + count]
    cots_in = refs[2 * chunks + count : 2 * chunks + 2 * count]
    down_ref, gate_out, up_out, down_out, rows_ref, cots_ref, side_ref, sem, cot_sem = refs[
        2 * chunks + 2 * count :
    ]
    row_copies = load_rows(rows_in, rows_ref, sem)
    cot_copies = load_rows(cots_in, cots_ref, cot_sem)
    for copy in cot_copies:
        copy.wait()
    done = 0
    for n in range(chunks):
        rows = gate_pre_refs[n].shape[0]
        part = pl.ds(done, rows)
        done += rows
        gate_pre = gate_pre_refs[n][...]
        up_pre = up_pre_refs[n][...]
        hidden_grad = dot(cots_ref[part], down_ref[...], NT)
        sigmoid = jax.nn.sigmoid(gate_pre)
        active = gate_pre * sigmoid
        side_ref[0, part] = (active * up_pre).astype(jnp.bfloat16)
        side_ref[1, part] = (
            hidden_grad * up_pre * sigmoid * (1.0 + gate_pre * (1.0 - sigmoid))
        ).astype(jnp.bfloat16)
        side_ref[2, part] = (hidden_grad * active).astype(jnp.bfloat16)
    down_out[...] = dot(side_ref[0], cots_ref[...], TN).astype(jnp.bfloat16)
    for copy in row_copies:
        copy.wait()
    gate_out[...] = dot(side_ref[1], rows_ref[...], TN).astype(jnp.bfloat16)
    up_out[...] = dot(side_ref[2], rows_ref[...], TN).astype(jnp.bfloat16)


def backward(gate_pres, up_pres, rows_in, cots_in, w_down):
    rows = sum(block.shape[0] for block in rows_in)
    fs, width = w_down.shape
    count = len(rows_in)
    out = jax.ShapeDtypeStruct((fs, width), jnp.bfloat16)
    return pl.pallas_call(
        functools.partial(backward_kernel, len(gate_pres), count),
        out_shape=(out, out, out),
        in_specs=[VMEM()] * (2 * len(gate_pres)) + [ANY()] * (2 * count) + [VMEM()],
        out_specs=[VMEM()] * 3,
        scratch_shapes=[
            pltpu.VMEM((rows, width), jnp.bfloat16),
            pltpu.VMEM((rows, width), jnp.bfloat16),
            pltpu.VMEM((3, rows, fs), jnp.bfloat16),
            pltpu.SemaphoreType.DMA((count,)),
            pltpu.SemaphoreType.DMA((count,)),
        ],
        compiler_params=params(),
        cost_estimate=pl.CostEstimate(
            flops=8 * rows * fs * width, bytes_accessed=6 * rows * width, transcendentals=0
        ),
        name="backward",
    )(*gate_pres, *up_pres, *rows_in, *cots_in, w_down)


def combine_kernel(count, *refs):
    mixed_ref, gates_ref, pos_ref = refs[:3]
    units = refs[3 : 3 + count]
    out_ref, rows_ref = refs[3 + count :]
    size = units[0].shape[0]
    for n, ref in enumerate(units):
        rows_ref[n * size : (n + 1) * size] = ref[...]
    pick = choosers(pos_ref[...], count * size)
    gates = gates_ref[...]
    rows = rows_ref[...]
    total = gates[:, 0:1] * dot(pick[0], rows) + gates[:, 1:2] * dot(pick[1], rows)
    out_ref[...] = (mixed_ref[...] + total).astype(jnp.bfloat16)


def per_device(
    tokens,
    queries,
    keys,
    values,
    out_proj,
    mod_scale,
    mod_shift,
    expert_ids,
    gates,
    w_gate,
    w_up,
    w_down,
    out_grad,
):
    n_ctx = lax.axis_size("ctx")
    n_exp = lax.axis_size("exp")
    groups = n_exp // SHARDS
    experts = n_ctx * groups
    local = tokens.shape[1]
    width = tokens.shape[2]
    capacity = 3 * local // experts
    slots = experts * capacity
    bundle = max(1, UNIT // capacity)
    units = experts // bundle
    unit_rows = bundle * capacity
    assert n_ctx & (n_ctx - 1) == 0 and groups & (groups - 1) == 0

    def shifted(value, ctx=0, group=0, shard=0):
        moves = []
        for c in range(n_ctx):
            for e in range(n_exp):
                moves.append((c * n_exp + e, (c ^ ctx) * n_exp + (e ^ (group * SHARDS + shard))))
        return lax.ppermute(value, AXES, moves)

    def exchanged(blocks):
        got = []
        for n, block in enumerate(blocks):
            parts = []
            for m in range(bundle):
                offset = n * bundle + m
                part = block if bundle == 1 else block[m * capacity : (m + 1) * capacity]
                if offset:
                    part = shifted(part, offset // groups, offset % groups)
                parts.append(part)
            got.append(parts[0] if bundle == 1 else jnp.concatenate(parts, axis=0))
        return got

    def spread(block):
        across = shifted(block, shard=2)
        return [block, across, shifted(block, shard=1), shifted(across, shard=1)]

    key_pieces = [keys[0]]
    value_pieces = [values[0]]
    for step in range(1, n_ctx):
        key_pieces.append(shifted(keys[0], ctx=step))
        value_pieces.append(shifted(values[0], ctx=step))

    me = lax.axis_index("ctx") * groups + lax.axis_index("exp") // SHARDS
    me = me.astype(jnp.int32).reshape(1)
    unit_shape = [jax.ShapeDtypeStruct((unit_rows, width), jnp.bfloat16)] * units
    pos, *cot_units = pl.pallas_call(
        functools.partial(slot_kernel, capacity, slots),
        out_shape=[jax.ShapeDtypeStruct((local, 2), jnp.int32)] + unit_shape,
        in_specs=[SMEM()] + [VMEM()] * 3,
        out_specs=[VMEM()] * (1 + units),
        compiler_params=params(),
        name="slots",
    )(me, expert_ids[0], gates[0], out_grad[0])

    cots = [spread(block) for block in exchanged(cot_units)]

    mixed, *row_units = pl.pallas_call(
        functools.partial(attend_kernel, n_ctx),
        out_shape=[jax.ShapeDtypeStruct((local, width), jnp.float32)] + unit_shape,
        in_specs=[VMEM()] * (6 + 2 * n_ctx),
        out_specs=[VMEM()] * (1 + units),
        scratch_shapes=[pltpu.VMEM((local, HEADS * HD), jnp.bfloat16)],
        compiler_params=params(),
        name="attend",
    )(
        queries[0],
        *key_pieces,
        *value_pieces,
        tokens[0],
        out_proj,
        mod_scale,
        mod_shift,
        pos,
    )

    rows = [spread(block) for block in exchanged(row_units)]

    per_chunk = 2
    gate_pres, up_pres, row_blocks, cot_blocks, results = [], [], [], [], []
    for first in range(0, units, per_chunk):
        some = range(first, first + per_chunk)
        order = [(k, n) for k in range(SHARDS) for n in some]
        blocks = [rows[n][k] for k, n in order]
        keep, send, gate_pre, up_pre = forward(blocks, w_gate, w_up, w_down)
        row_blocks += blocks
        cot_blocks += [cots[n][k] for k, n in order]
        gate_pres.append(gate_pre)
        up_pres.append(up_pre)
        other = shifted(send, shard=1)
        half = keep.shape[0] // 2
        mine = keep[:half].astype(jnp.float32) + other[:half].astype(jnp.float32)
        theirs = keep[half:].astype(jnp.float32) + other[half:].astype(jnp.float32)
        across = shifted(theirs.astype(jnp.bfloat16), shard=2)
        sums = (mine + across.astype(jnp.float32)).astype(jnp.bfloat16)
        results += [sums[n * unit_rows : (n + 1) * unit_rows] for n in range(per_chunk)]
    returned = exchanged(results)

    grad_gate, grad_up, grad_down = backward(gate_pres, up_pres, row_blocks, cot_blocks, w_down)

    layer_out = pl.pallas_call(
        functools.partial(combine_kernel, units),
        out_shape=jax.ShapeDtypeStruct((local, width), jnp.bfloat16),
        in_specs=[VMEM()] * (3 + units),
        out_specs=VMEM(),
        scratch_shapes=[pltpu.VMEM((slots, width), jnp.bfloat16)],
        compiler_params=params(),
        name="combine",
    )(mixed, gates[0], pos, *returned)
    return (layer_out[None], grad_gate, grad_up, grad_down)


def solution(mesh):
    placed = (
        P("exp", "ctx", None),
        P("exp", "ctx", None),
        P("exp", "ctx", None),
        P("exp", "ctx", None),
        P(),
        P("exp", None),
        P("exp", None),
        P("exp", "ctx", None),
        P("exp", "ctx", None),
        P(("ctx", "exp"), None),
        P(("ctx", "exp"), None),
        P(("ctx", "exp"), None),
        P("exp", "ctx", None),
    )
    return jax.shard_map(
        per_device,
        mesh=mesh,
        in_specs=placed,
        out_specs=(
            P("exp", "ctx", None),
            P(("ctx", "exp"), None),
            P(("ctx", "exp"), None),
            P(("ctx", "exp"), None),
        ),
        check_vma=False,
    )
```

```python
import functools

import jax
import jax.numpy as jnp
from jax import lax
from jax.experimental import pallas as pl
from jax.experimental.pallas import tpu as pltpu
from jax.sharding import PartitionSpec as P

HEADS = 8
HD = 128
SHARDS = 4
PIECE = 16
VMEM_LIMIT = 48 * 1024 * 1024
EXP = ("group", "side", "core")

NT = (((1,), (1,)), ((), ()))
TN = (((0,), (0,)), ((), ()))


def dot(a, b, dims=(((1,), (0,)), ((), ()))):
    return lax.dot_general(a, b, dims, preferred_element_type=jnp.float32)


def params():
    return pltpu.CompilerParams(vmem_limit_bytes=VMEM_LIMIT)


VMEM = functools.partial(pl.BlockSpec, memory_space=pltpu.VMEM)
SMEM = functools.partial(pl.BlockSpec, memory_space=pltpu.SMEM)
ANY = functools.partial(pl.BlockSpec, memory_space=pl.ANY)


def choosers(pos, slots):
    tokens = pos.shape[0]
    line = lax.broadcasted_iota(jnp.int32, (tokens, slots), 1)
    return [(pos[:, k : k + 1] == line).astype(jnp.bfloat16) for k in range(2)]


def slot_kernel(capacity, piece, ids_ref, gates_ref, grad_ref, pos_ref, *chunk_refs):
    ids = ids_ref[...]
    tokens = ids.shape[0]
    lanes = lax.broadcasted_iota(jnp.int32, (tokens, 128), 1)
    hot = [(ids[:, k : k + 1] == lanes).astype(jnp.float32) for k in range(2)]
    later = lax.broadcasted_iota(jnp.int32, (tokens, tokens), 0)
    earlier = lax.broadcasted_iota(jnp.int32, (tokens, tokens), 1)
    lower = (later > earlier).astype(jnp.bfloat16)
    before = dot(lower, (hot[0] + hot[1]).astype(jnp.bfloat16))
    block = chunk_refs[0].shape[0]
    pos = []
    for k in range(2):
        slot = jnp.sum(hot[k] * before, axis=1, keepdims=True).astype(jnp.int32)
        chunk = slot // piece
        pos.append(chunk * block + ids[:, k : k + 1] * piece + (slot - chunk * piece))
    pair = lax.broadcasted_iota(jnp.int32, (tokens, 2), 1)
    pos = jnp.where(pair == 0, pos[0], pos[1])
    pos_ref[...] = pos
    pick = choosers(pos, block * len(chunk_refs))
    grad = grad_ref[...].astype(jnp.float32)
    gates = gates_ref[...]
    placed = 0.0
    for k in range(2):
        rows = (gates[:, k : k + 1] * grad).astype(jnp.bfloat16)
        placed = placed + dot(pick[k], rows, TN)
    store_units(placed, chunk_refs)


def store_units(placed, unit_refs):
    placed = placed.astype(jnp.bfloat16)
    rows = unit_refs[0].shape[0]
    for n, ref in enumerate(unit_refs):
        ref[...] = placed[n * rows : (n + 1) * rows]


def attend_kernel(pieces, *refs):
    query_ref = refs[0]
    key_refs = refs[1 : 1 + pieces]
    value_refs = refs[1 + pieces : 1 + 2 * pieces]
    token_ref, proj_ref, scale_ref, shift_ref, pos_ref = refs[1 + 2 * pieces : 6 + 2 * pieces]
    mixed_ref = refs[6 + 2 * pieces]
    unit_refs = refs[7 + 2 * pieces : -1]
    attended_ref = refs[-1]
    for head in range(HEADS):
        cols = slice(head * HD, (head + 1) * HD)
        query = query_ref[:, cols]
        scores = [dot(query, ref[:, cols], NT) * (HD ** (-0.5)) for ref in key_refs]
        top = functools.reduce(
            jnp.maximum, [jnp.max(piece, axis=1, keepdims=True) for piece in scores]
        )
        weights = [jnp.exp(piece - top) for piece in scores]
        total = functools.reduce(
            jnp.add, [jnp.sum(piece, axis=1, keepdims=True) for piece in weights]
        )
        accum = functools.reduce(
            jnp.add,
            [
                dot(piece.astype(jnp.bfloat16), ref[:, cols])
                for piece, ref in zip(weights, value_refs)
            ],
        )
        attended_ref[:, cols] = (accum / total).astype(jnp.bfloat16)
    mixed = token_ref[...].astype(jnp.float32) + dot(attended_ref[...], proj_ref[...])
    mixed_ref[...] = mixed
    mean_square = jnp.mean(mixed * mixed, axis=1, keepdims=True)
    normed = mixed * lax.rsqrt(mean_square + 1e-06) * (1.0 + scale_ref[...]) + shift_ref[...]
    normed = normed.astype(jnp.bfloat16)
    slots = len(unit_refs) * unit_refs[0].shape[0]
    pick = choosers(pos_ref[...], slots)
    store_units(dot(pick[0] + pick[1], normed, TN), unit_refs)


def load_rows(block_refs, rows_ref, sem):
    copies = []
    for n, ref in enumerate(block_refs):
        rows = ref.shape[0]
        copies.append(
            pltpu.make_async_copy(ref, rows_ref.at[pl.ds(n * rows, rows)], sem.at[n])
        )
    for copy in copies:
        copy.start()
    return copies


def forward_kernel(count, *refs):
    blocks = refs[:count]
    gate_ref, up_ref, down_ref, keep_ref, send_ref, gate_pre_ref, up_pre_ref, rows_ref, sem = refs[
        count:
    ]
    for copy in load_rows(blocks, rows_ref, sem):
        copy.wait()
    rows = rows_ref[...]
    gate_pre = dot(rows, gate_ref[...], NT)
    up_pre = dot(rows, up_ref[...], NT)
    gate_pre_ref[...] = gate_pre
    up_pre_ref[...] = up_pre
    hidden = (gate_pre * jax.nn.sigmoid(gate_pre) * up_pre).astype(jnp.bfloat16)
    half = rows.shape[0] // 2
    send_ref[...] = dot(hidden[half:], down_ref[...]).astype(jnp.bfloat16)
    keep_ref[...] = dot(hidden[:half], down_ref[...]).astype(jnp.bfloat16)


def forward(blocks, w_gate, w_up, w_down):
    rows = sum(block.shape[0] for block in blocks)
    fs, width = w_gate.shape
    half = jax.ShapeDtypeStruct((rows // 2, width), jnp.bfloat16)
    pre = jax.ShapeDtypeStruct((rows, fs), jnp.float32)
    return pl.pallas_call(
        functools.partial(forward_kernel, len(blocks)),
        out_shape=(half, half, pre, pre),
        in_specs=[ANY()] * len(blocks) + [VMEM()] * 3,
        out_specs=[VMEM()] * 4,
        scratch_shapes=[
            pltpu.VMEM((rows, width), jnp.bfloat16),
            pltpu.SemaphoreType.DMA((len(blocks),)),
        ],
        compiler_params=params(),
        cost_estimate=pl.CostEstimate(
            flops=6 * rows * fs * width, bytes_accessed=8 * rows * width, transcendentals=0
        ),
        name="forward",
    )(*blocks, w_gate, w_up, w_down)


def backward_kernel(chunks, count, *refs):
    gate_pre_refs = refs[:chunks]
    up_pre_refs = refs[chunks : 2 * chunks]
    rows_in = refs[2 * chunks : 2 * chunks + count]
    cots_in = refs[2 * chunks + count : 2 * chunks + 2 * count]
    down_ref, gate_out, up_out, down_out, rows_ref, cots_ref, side_ref, sem, cot_sem = refs[
        2 * chunks + 2 * count :
    ]
    row_copies = load_rows(rows_in, rows_ref, sem)
    cot_copies = load_rows(cots_in, cots_ref, cot_sem)
    for copy in cot_copies:
        copy.wait()
    done = 0
    for n in range(chunks):
        rows = gate_pre_refs[n].shape[0]
        part = pl.ds(done, rows)
        done += rows
        gate_pre = gate_pre_refs[n][...]
        up_pre = up_pre_refs[n][...]
        hidden_grad = dot(cots_ref[part], down_ref[...], NT)
        sigmoid = jax.nn.sigmoid(gate_pre)
        active = gate_pre * sigmoid
        side_ref[0, part] = (active * up_pre).astype(jnp.bfloat16)
        side_ref[1, part] = (
            hidden_grad * up_pre * sigmoid * (1.0 + gate_pre * (1.0 - sigmoid))
        ).astype(jnp.bfloat16)
        side_ref[2, part] = (hidden_grad * active).astype(jnp.bfloat16)
    down_out[...] = dot(side_ref[0], cots_ref[...], TN).astype(jnp.bfloat16)
    for copy in row_copies:
        copy.wait()
    gate_out[...] = dot(side_ref[1], rows_ref[...], TN).astype(jnp.bfloat16)
    up_out[...] = dot(side_ref[2], rows_ref[...], TN).astype(jnp.bfloat16)


def backward(gate_pres, up_pres, rows_in, cots_in, w_down):
    rows = sum(block.shape[0] for block in rows_in)
    fs, width = w_down.shape
    count = len(rows_in)
    out = jax.ShapeDtypeStruct((fs, width), jnp.bfloat16)
    return pl.pallas_call(
        functools.partial(backward_kernel, len(gate_pres), count),
        out_shape=(out, out, out),
        in_specs=[VMEM()] * (2 * len(gate_pres)) + [ANY()] * (2 * count) + [VMEM()],
        out_specs=[VMEM()] * 3,
        scratch_shapes=[
            pltpu.VMEM((rows, width), jnp.bfloat16),
            pltpu.VMEM((rows, width), jnp.bfloat16),
            pltpu.VMEM((3, rows, fs), jnp.bfloat16),
            pltpu.SemaphoreType.DMA((count,)),
            pltpu.SemaphoreType.DMA((count,)),
        ],
        compiler_params=params(),
        cost_estimate=pl.CostEstimate(
            flops=8 * rows * fs * width, bytes_accessed=6 * rows * width, transcendentals=0
        ),
        name="backward",
    )(*gate_pres, *up_pres, *rows_in, *cots_in, w_down)


def combine_kernel(count, *refs):
    mixed_ref, gates_ref, pos_ref = refs[:3]
    units = refs[3 : 3 + count]
    out_ref, rows_ref = refs[3 + count :]
    size = units[0].shape[0]
    for n, ref in enumerate(units):
        rows_ref[n * size : (n + 1) * size] = ref[...]
    pick = choosers(pos_ref[...], count * size)
    gates = gates_ref[...]
    rows = rows_ref[...]
    total = gates[:, 0:1] * dot(pick[0], rows) + gates[:, 1:2] * dot(pick[1], rows)
    out_ref[...] = (mixed_ref[...] + total).astype(jnp.bfloat16)


def per_device(
    tokens,
    queries,
    keys,
    values,
    out_proj,
    mod_scale,
    mod_shift,
    expert_ids,
    gates,
    w_gate,
    w_up,
    w_down,
    out_grad,
):
    n_ctx = lax.axis_size("ctx")
    experts = n_ctx * lax.axis_size("group")
    local = tokens.shape[1]
    width = tokens.shape[2]
    capacity = 3 * local // experts
    slots = experts * capacity
    piece = PIECE if capacity % PIECE == 0 else capacity
    chunks = capacity // piece
    block = experts * piece

    def swapped(value, axis, step=1):
        size = lax.axis_size(axis)
        return lax.ppermute(value, axis, [(n, n ^ step) for n in range(size)])

    def exchanged(value):
        shaped = value.reshape(experts, piece, width)
        moved = lax.all_to_all(shaped, ("ctx", "group"), split_axis=0, concat_axis=0, tiled=True)
        return moved.reshape(block, width)

    def spread(value):
        across = swapped(value, "side")
        return [value, across, swapped(value, "core"), swapped(across, "core")]

    key_pieces = [keys[0]]
    value_pieces = [values[0]]
    for step in range(1, n_ctx):
        key_pieces.append(swapped(keys[0], "ctx", step))
        value_pieces.append(swapped(values[0], "ctx", step))

    chunk_shape = [jax.ShapeDtypeStruct((block, width), jnp.bfloat16)] * chunks
    pos, *cot_chunks = pl.pallas_call(
        functools.partial(slot_kernel, capacity, piece),
        out_shape=[jax.ShapeDtypeStruct((local, 2), jnp.int32)] + chunk_shape,
        in_specs=[VMEM()] * 3,
        out_specs=[VMEM()] * (1 + chunks),
        compiler_params=params(),
        name="slots",
    )(expert_ids[0], gates[0], out_grad[0])

    cots = [spread(exchanged(value)) for value in cot_chunks]

    mixed, *row_chunks = pl.pallas_call(
        functools.partial(attend_kernel, n_ctx),
        out_shape=[jax.ShapeDtypeStruct((local, width), jnp.float32)] + chunk_shape,
        in_specs=[VMEM()] * (6 + 2 * n_ctx),
        out_specs=[VMEM()] * (1 + chunks),
        scratch_shapes=[pltpu.VMEM((local, HEADS * HD), jnp.bfloat16)],
        compiler_params=params(),
        name="attend",
    )(
        queries[0],
        *key_pieces,
        *value_pieces,
        tokens[0],
        out_proj,
        mod_scale,
        mod_shift,
        pos,
    )

    rows = [spread(exchanged(value)) for value in row_chunks]

    gate_pres, up_pres, returned = [], [], []
    for blocks in rows:
        keep, send, gate_pre, up_pre = forward(blocks, w_gate, w_up, w_down)
        gate_pres.append(gate_pre)
        up_pres.append(up_pre)
        other = swapped(send, "core")
        mine = keep[:block].astype(jnp.float32) + other[:block].astype(jnp.float32)
        theirs = keep[block:].astype(jnp.float32) + other[block:].astype(jnp.float32)
        across = swapped(theirs.astype(jnp.bfloat16), "side")
        returned.append(exchanged((mine + across.astype(jnp.float32)).astype(jnp.bfloat16)))

    grad_gate, grad_up, grad_down = backward(gate_pres, up_pres, sum(rows, []), sum(cots, []), w_down)

    layer_out = pl.pallas_call(
        functools.partial(combine_kernel, chunks),
        out_shape=jax.ShapeDtypeStruct((local, width), jnp.bfloat16),
        in_specs=[VMEM()] * (3 + chunks),
        out_specs=VMEM(),
        scratch_shapes=[pltpu.VMEM((slots, width), jnp.bfloat16)],
        compiler_params=params(),
        name="combine",
    )(mixed, gates[0], pos, *returned)
    return (layer_out[None], grad_gate, grad_up, grad_down)


def solution(mesh):
    n_ctx = mesh.shape["ctx"]
    cut = (n_ctx, mesh.shape["exp"] // SHARDS, SHARDS // 2, 2)
    mesh = jax.sharding.Mesh(mesh.devices.reshape(cut), ("ctx",) + EXP)
    placed = (
        P(EXP, "ctx", None),
        P(EXP, "ctx", None),
        P(EXP, "ctx", None),
        P(EXP, "ctx", None),
        P(),
        P(EXP, None),
        P(EXP, None),
        P(EXP, "ctx", None),
        P(EXP, "ctx", None),
        P(("ctx",) + EXP, None),
        P(("ctx",) + EXP, None),
        P(("ctx",) + EXP, None),
        P(EXP, "ctx", None),
    )
    return jax.shard_map(
        per_device,
        mesh=mesh,
        in_specs=placed,
        out_specs=(
            P(EXP, "ctx", None),
            P(("ctx",) + EXP, None),
            P(("ctx",) + EXP, None),
            P(("ctx",) + EXP, None),
        ),
        check_vma=False,
    )
```

```python
import functools

import jax
import jax.numpy as jnp
from jax import lax
from jax.experimental import pallas as pl
from jax.experimental.pallas import tpu as pltpu
from jax.sharding import PartitionSpec as P

HEADS = 8
HD = 128
SHARDS = 4
UNIT = 48
PER_CHUNK = 2
VMEM_LIMIT = 40 * 1024 * 1024
EXP = ("group", "side", "core")

NT = (((1,), (1,)), ((), ()))
TN = (((0,), (0,)), ((), ()))

VMEM = pl.BlockSpec(memory_space=pltpu.VMEM)
SMEM = pl.BlockSpec(memory_space=pltpu.SMEM)
ANY = pl.BlockSpec(memory_space=pl.ANY)


def dot(a, b, dims=(((1,), (0,)), ((), ()))):
    return lax.dot_general(a, b, dims, preferred_element_type=jnp.float32)


def shape_of(rows, cols, dtype=jnp.bfloat16):
    return jax.ShapeDtypeStruct((rows, cols), dtype)


def call(body, name, small, large, outs, buffers, flops=0, after=()):
    flat = [value for group in large for value in group]
    count = len(flat)
    n_small, n_outs, n_after = len(small), len(outs), len(after)
    group_shapes = [
        pltpu.VMEM((sum(v.shape[0] for v in group), group[0].shape[1]), group[0].dtype)
        for group in large
    ]

    def kernel(*refs):
        small_refs = refs[:n_small]
        sources = refs[n_small : n_small + count]
        out_refs = refs[n_small + count + n_after : n_small + count + n_after + n_outs]
        rest = refs[n_small + count + n_after + n_outs :]
        targets = rest[: len(large)]
        own = rest[len(large) : -1]
        sem = rest[-1]
        waits, at = [], 0
        for group, target in zip(large, targets):
            copies, row = [], 0
            for value in group:
                size = value.shape[0]
                copies.append(
                    pltpu.make_async_copy(sources[at], target.at[pl.ds(row, size)], sem.at[at])
                )
                row += size
                at += 1
            waits.append(copies)
        for copies in waits:
            for copy in copies:
                copy.start()

        def ready(n):
            for copy in waits[n]:
                copy.wait()
            return targets[n]

        body(small_refs, ready, out_refs, own)

    moved = sum(v.size * v.dtype.itemsize for v in flat)
    return pl.pallas_call(
        kernel,
        out_shape=tuple(outs),
        in_specs=[spec for spec, _ in small] + [ANY] * (count + n_after),
        out_specs=(VMEM,) * n_outs,
        scratch_shapes=group_shapes + list(buffers) + [pltpu.SemaphoreType.DMA((count,))],
        compiler_params=pltpu.CompilerParams(vmem_limit_bytes=VMEM_LIMIT),
        cost_estimate=pl.CostEstimate(flops=flops, bytes_accessed=moved, transcendentals=0),
        name=name,
    )(*[value for _, value in small], *flat, *after)


def column(row):
    size = row.shape[1]
    across = lax.broadcasted_iota(jnp.int32, (size, size), 0)
    along = lax.broadcasted_iota(jnp.int32, (size, size), 1)
    return jnp.sum(jnp.where(across == along, row, jnp.zeros_like(row)), axis=1, keepdims=True)


def choosers(pos, slots):
    line = lax.broadcasted_iota(jnp.int32, (pos[0].shape[0], slots), 1)
    return [(place == line).astype(jnp.bfloat16) for place in pos]


def store_units(placed, unit_refs):
    placed = placed.astype(jnp.bfloat16)
    rows = unit_refs[0].shape[0]
    for n, ref in enumerate(unit_refs):
        ref[...] = placed[n * rows : (n + 1) * rows]


def slots_body(n_ctx, groups, capacity, small, ready, outs, own):
    me_ref, ids_ref, gates_ref = small
    pos_ref, *unit_refs = outs
    ids = [column(ids_ref[k : k + 1]) for k in range(2)]
    gates = [column(gates_ref[k : k + 1]) for k in range(2)]
    tokens = ids[0].shape[0]
    lanes = lax.broadcasted_iota(jnp.int32, (tokens, 128), 1)
    hot = [(ids[k] == lanes).astype(jnp.float32) for k in range(2)]
    later = lax.broadcasted_iota(jnp.int32, (tokens, tokens), 0)
    earlier = lax.broadcasted_iota(jnp.int32, (tokens, tokens), 1)
    lower = (later > earlier).astype(jnp.bfloat16)
    before = dot(lower, (hot[0] + hot[1]).astype(jnp.bfloat16))
    shift = groups.bit_length() - 1
    pos = []
    for k in range(2):
        slot = jnp.sum(hot[k] * before, axis=1, keepdims=True).astype(jnp.int32)
        ctx = ((ids[k] >> shift) - me_ref[0]) & (n_ctx - 1)
        group = ((ids[k] & (groups - 1)) - me_ref[1]) & (groups - 1)
        pos.append((group * n_ctx + ctx) * capacity + slot)
    pair = lax.broadcasted_iota(jnp.int32, (tokens, 2), 1)
    pos_ref[...] = jnp.where(pair == 0, pos[0], pos[1])
    pick = choosers(pos, len(unit_refs) * unit_refs[0].shape[0])
    grad = ready(0)[...].astype(jnp.float32)
    placed = 0.0
    for k in range(2):
        placed = placed + dot(pick[k], (gates[k] * grad).astype(jnp.bfloat16), TN)
    store_units(placed, unit_refs)


def attend_body(pieces, small, ready, outs, own):
    scale_ref, shift_ref, pos_ref = small
    mixed_ref, *unit_refs = outs
    (attended_ref,) = own
    query_ref, key_ref, value_ref = ready(0), ready(1), ready(2)
    for head in range(HEADS):
        cols = slice(head * HD, (head + 1) * HD)
        scores = dot(query_ref[:, cols], key_ref[:, cols], NT) * (HD ** (-0.5))
        weights = jnp.exp(scores - jnp.max(scores, axis=1, keepdims=True))
        total = jnp.sum(weights, axis=1, keepdims=True)
        accum = dot(weights.astype(jnp.bfloat16), value_ref[:, cols])
        attended_ref[:, cols] = (accum / total).astype(jnp.bfloat16)
    token_ref, proj_ref = ready(3), ready(4)
    mixed = token_ref[...].astype(jnp.float32) + dot(attended_ref[...], proj_ref[...])
    mixed_ref[...] = mixed
    mean_square = jnp.mean(mixed * mixed, axis=1, keepdims=True)
    normed = mixed * lax.rsqrt(mean_square + 1e-06) * (1.0 + scale_ref[...]) + shift_ref[...]
    slots = len(unit_refs) * unit_refs[0].shape[0]
    pick = choosers([pos_ref[:, 0:1], pos_ref[:, 1:2]], slots)
    store_units(dot(pick[0] + pick[1], normed.astype(jnp.bfloat16), TN), unit_refs)


def forward_body(small, ready, outs, own):
    keep_ref, send_ref, gate_pre_ref, up_pre_ref = outs
    rows = ready(0)[...]
    gate_pre = dot(rows, ready(1)[...], NT)
    gate_pre_ref[...] = gate_pre
    up_pre = dot(rows, ready(2)[...], NT)
    up_pre_ref[...] = up_pre
    hidden = (gate_pre * jax.nn.sigmoid(gate_pre) * up_pre).astype(jnp.bfloat16)
    half = rows.shape[0] // 2
    partial = dot(hidden, ready(3)[...]).astype(jnp.bfloat16)
    keep_ref[...] = partial[:half]
    send_ref[...] = partial[half:]


def add_body(small, ready, outs, own):
    total = ready(0)[...].astype(jnp.float32) + ready(1)[...].astype(jnp.float32)
    store_units(total, outs)


def backward_body(small, ready, outs, own):
    side_refs = outs[:3]
    cot_ref, down_ref = ready(0), ready(1)
    hidden_grad = dot(cot_ref[...], down_ref[...], NT)
    gate_pre = ready(2)[...]
    up_pre = ready(3)[...]
    sigmoid = jax.nn.sigmoid(gate_pre)
    active = gate_pre * sigmoid
    side_refs[0][...] = (
        hidden_grad * up_pre * sigmoid * (1.0 + gate_pre * (1.0 - sigmoid))
    ).astype(jnp.bfloat16)
    side_refs[1][...] = (hidden_grad * active).astype(jnp.bfloat16)
    side_refs[2][...] = (active * up_pre).astype(jnp.bfloat16)
    row_ref = ready(4)
    half = side_refs[0].shape[1] // 2
    for side_ref, with_ref, out_ref in zip(side_refs, (row_ref, row_ref, cot_ref), outs[3:]):
        out_ref[...] = dot(side_ref[:, half:], with_ref[...], TN).astype(jnp.bfloat16)


def finish_body(small, ready, outs, own):
    row_ref, cot_ref = ready(0), ready(1)
    for n, (with_ref, out_ref) in enumerate(zip((row_ref, row_ref, cot_ref), outs)):
        side_ref = ready(2 + n)
        half = side_ref.shape[1] // 2
        grad = dot(side_ref[:, :half], with_ref[...], TN)
        out_ref[...] = (grad + ready(5 + n)[...].astype(jnp.float32)).astype(jnp.bfloat16)


def combine_body(small, ready, outs, own):
    gates_ref, pos_ref = small
    rows_ref, mixed_ref = ready(0), ready(1)
    rows = rows_ref[...]
    pick = choosers([pos_ref[:, 0:1], pos_ref[:, 1:2]], rows.shape[0])
    total = mixed_ref[...]
    for k in range(2):
        total = total + column(gates_ref[k : k + 1]) * dot(pick[k], rows)
    outs[0][...] = total.astype(jnp.bfloat16)


def per_device(
    tokens,
    queries,
    keys,
    values,
    out_proj,
    mod_scale,
    mod_shift,
    expert_ids,
    gates,
    w_gate,
    w_up,
    w_down,
    out_grad,
):
    n_ctx = lax.axis_size("ctx")
    groups = lax.axis_size("group")
    experts = n_ctx * groups
    local = tokens.shape[1]
    width = tokens.shape[2]
    hidden = w_gate.shape[0]
    capacity = 3 * local // experts
    slots = experts * capacity
    bundle = max(1, UNIT // capacity)
    units = experts // bundle
    unit_rows = bundle * capacity
    assert n_ctx & (n_ctx - 1) == 0 and groups & (groups - 1) == 0

    def swapped(value, axis):
        return lax.ppermute(value, axis, [(n, n ^ 1) for n in range(lax.axis_size(axis))])

    def shifted(value, offset, sign):
        group, ctx = offset // n_ctx * sign, offset % n_ctx * sign
        moves = []
        for c in range(n_ctx):
            for g in range(groups):
                target = (c + ctx) % n_ctx * groups + (g + group) % groups
                moves.append((c * groups + g, target))
        return lax.ppermute(value, ("ctx", "group"), moves)

    def exchanged(unit, n, sign):
        parts = []
        for m in range(bundle):
            offset = n * bundle + m
            part = unit if bundle == 1 else unit[m * capacity : (m + 1) * capacity]
            parts.append(shifted(part, offset, sign) if offset else part)
        return parts[0] if bundle == 1 else jnp.concatenate(parts, axis=0)

    key_pieces = [keys[0]]
    value_pieces = [values[0]]
    for step in range(1, n_ctx):
        key_pieces.append(shifted(keys[0], step, 1))
        value_pieces.append(shifted(values[0], step, 1))

    ids_rows = jnp.transpose(expert_ids[0])
    gate_rows = jnp.transpose(gates[0])
    me = jnp.stack([lax.axis_index("ctx"), lax.axis_index("group")]).astype(jnp.int32)
    unit_shape = [shape_of(unit_rows, width)] * units
    pos, *cot_units = call(
        functools.partial(slots_body, n_ctx, groups, capacity),
        "slots",
        [(SMEM, me), (VMEM, ids_rows), (VMEM, gate_rows)],
        [[out_grad[0]]],
        [shape_of(local, 2, jnp.int32)] + unit_shape,
        [],
        flops=8 * slots * local * width,
    )
    cots = [exchanged(unit, n, 1) for n, unit in enumerate(cot_units)]
    cots_across = [swapped(unit, "side") for unit in cots]

    mixed, *row_units = call(
        functools.partial(attend_body, n_ctx),
        "attend",
        [(VMEM, mod_scale), (VMEM, mod_shift), (VMEM, pos)],
        [[queries[0]], key_pieces, value_pieces, [tokens[0]], [out_proj]],
        [shape_of(local, width, jnp.float32)] + unit_shape,
        [pltpu.VMEM((local, HEADS * HD), jnp.bfloat16)],
        flops=4 * local * HEADS * HD * width,
        after=cots[2:4],
    )
    rows = [exchanged(unit, n, 1) for n, unit in enumerate(row_units)]
    rows_across = [swapped(unit, "side") for unit in rows]

    weights = [[weight, swapped(weight, "core")] for weight in (w_gate, w_up, w_down)]
    ahead = {0: cots_across[0:4], PER_CHUNK: cots_across[6:8]}
    gate_pres, up_pres, row_order, cot_order, returned = [], [], [], [], []
    for first in range(0, units, PER_CHUNK):
        last = first + PER_CHUNK
        blocks = rows[first:last] + rows_across[first:last]
        row_order += blocks
        cot_order += cots[first:last] + cots_across[first:last]
        half = PER_CHUNK * unit_rows
        keep, send, gate_pre, up_pre = call(
            forward_body,
            "forward",
            [],
            [blocks] + weights,
            [shape_of(half, width)] * 2 + [shape_of(2 * half, 2 * hidden, jnp.float32)] * 2,
            [],
            flops=24 * half * hidden * width,
            after=ahead.get(first, ()),
        )
        gate_pres.append(gate_pre)
        up_pres.append(up_pre)
        sums = call(
            add_body,
            "add",
            [],
            [[keep], [swapped(send, "side")]],
            [shape_of(unit_rows, width)] * PER_CHUNK,
            [],
        )
        returned += [exchanged(unit, first + n, -1) for n, unit in enumerate(sums)]

    total_rows = 2 * slots
    side = [shape_of(total_rows, 2 * hidden)] * 3
    grad = [shape_of(hidden, width)] * 3
    *sides, other_gate, other_up, other_down = call(
        backward_body,
        "backward",
        [],
        [cot_order, weights[2], gate_pres, up_pres, row_order],
        side + grad,
        [],
        flops=10 * total_rows * hidden * width,
    )
    others = [swapped(value, "core") for value in (other_gate, other_up, other_down)]
    grad_gate, grad_up, grad_down = call(
        finish_body,
        "finish",
        [],
        [row_order, cot_order] + [[value] for value in sides] + [[value] for value in others],
        grad,
        [],
        flops=6 * total_rows * hidden * width,
    )

    (layer_out,) = call(
        combine_body,
        "combine",
        [(VMEM, gate_rows), (VMEM, pos)],
        [returned, [mixed]],
        [shape_of(local, width)],
        [],
    )
    return (layer_out[None], grad_gate, grad_up, grad_down)


def solution(mesh):
    n_ctx = mesh.shape["ctx"]
    cut = (n_ctx, mesh.shape["exp"] // SHARDS, SHARDS // 2, 2)
    mesh = jax.sharding.Mesh(mesh.devices.reshape(cut), ("ctx",) + EXP)
    rows = P(EXP, "ctx", None)
    weight = P(("ctx",) + EXP, None)
    return jax.shard_map(
        per_device,
        mesh=mesh,
        in_specs=(rows, rows, rows, rows, P(), P(EXP, None), P(EXP, None), rows, rows)
        + (weight, weight, weight, rows),
        out_specs=(rows, weight, weight, weight),
        check_vma=False,
    )
```

```python
import functools

import jax
import jax.numpy as jnp
from jax import lax
from jax.experimental import pallas as pl
from jax.experimental.pallas import tpu as pltpu
from jax.sharding import PartitionSpec as P

HEADS = 8
HD = 128
SHARDS = 4
PIECE = 16
VMEM_LIMIT = 60 * 1024 * 1024
EXP = ("group", "side", "core")

NT = (((1,), (1,)), ((), ()))
TN = (((0,), (0,)), ((), ()))

VMEM = pl.BlockSpec(memory_space=pltpu.VMEM)
ANY = pl.BlockSpec(memory_space=pl.ANY)


def dot(a, b, dims=(((1,), (0,)), ((), ()))):
    return lax.dot_general(a, b, dims, preferred_element_type=jnp.float32)


def shape_of(*shape, dtype=jnp.bfloat16):
    return jax.ShapeDtypeStruct(shape, dtype)


def call(body, name, operands, outs, flops=0, after=()):
    pieces = [piece for group, _ in operands for piece in group]
    values = []
    for value, _, _ in pieces:
        if not any(value is known for known in values):
            values.append(value)
    where = [[value is known for known in values].index(True) for value, _, _ in pieces]
    n_in, n_outs = len(values) + len(after), len(outs)

    def kernel(*refs):
        out_refs = refs[n_in : n_in + n_outs]
        targets = refs[n_in + n_outs : -1]
        sem = refs[-1]
        waits, at = [], 0
        for (group, _), target in zip(operands, targets):
            copies = []
            for _, source_index, target_index in group:
                source = refs[where[at]]
                copies.append(
                    pltpu.make_async_copy(
                        source if source_index is None else source.at[source_index],
                        target if target_index is None else target.at[target_index],
                        sem.at[at],
                    )
                )
                at += 1
            waits.append(copies)
        for copies in waits:
            for copy in copies:
                copy.start()

        def ready(n):
            for copy in waits[n]:
                copy.wait()
            return targets[n]

        body(ready, out_refs)

    moved = sum(v.size * v.dtype.itemsize for v in values)
    return pl.pallas_call(
        kernel,
        out_shape=tuple(outs),
        in_specs=[ANY] * n_in,
        out_specs=(VMEM,) * n_outs,
        scratch_shapes=[pltpu.VMEM(shape, group[0][0].dtype) for group, shape in operands]
        + [pltpu.SemaphoreType.DMA((len(pieces),))],
        compiler_params=pltpu.CompilerParams(vmem_limit_bytes=VMEM_LIMIT),
        cost_estimate=pl.CostEstimate(flops=flops, bytes_accessed=moved, transcendentals=0),
        name=name,
    )(*values, *after)


def whole(value):
    return [(value, None, None)], value.shape


def rows_of(values):
    pieces, row = [], 0
    for value in values:
        pieces.append((value, None, pl.ds(row, value.shape[0])))
        row += value.shape[0]
    return pieces, (row, values[0].shape[1])


def column(row):
    size = row.shape[1]
    across = lax.broadcasted_iota(jnp.int32, (size, size), 0)
    along = lax.broadcasted_iota(jnp.int32, (size, size), 1)
    return jnp.sum(jnp.where(across == along, row, jnp.zeros_like(row)), axis=1, keepdims=True)


def choosers(pos, slots):
    line = lax.broadcasted_iota(jnp.int32, (pos[0].shape[0], slots), 1)
    return [(place == line).astype(jnp.bfloat16) for place in pos]


def positions(capacity, ids):
    tokens = ids[0].shape[0]
    lanes = lax.broadcasted_iota(jnp.int32, (tokens, 128), 1)
    hot = [(ids[k] == lanes).astype(jnp.float32) for k in range(2)]
    later = lax.broadcasted_iota(jnp.int32, (tokens, tokens), 0)
    earlier = lax.broadcasted_iota(jnp.int32, (tokens, tokens), 1)
    lower = (later > earlier).astype(jnp.bfloat16)
    before = dot(lower, (hot[0] + hot[1]).astype(jnp.bfloat16))
    pos = []
    for k in range(2):
        slot = jnp.sum(hot[k] * before, axis=1, keepdims=True).astype(jnp.int32)
        pos.append(ids[k] * capacity + slot)
    return pos


def chunk_position(pos, capacity, first, count):
    expert = pos // capacity
    slot = pos - expert * capacity - first
    return jnp.where((slot >= 0) & (slot < count), expert * count + slot, -1)


def place_cots(capacity, first, ready, grad_at, gates, pos, out_ref):
    blocks, count, _ = out_ref.shape
    piece = count if blocks > 1 else capacity
    pick = choosers(
        [chunk_position(place, capacity, first, piece) for place in pos], blocks * count
    )
    grad = ready(grad_at)[...].astype(jnp.float32)
    placed = 0.0
    for k in range(2):
        placed = placed + dot(pick[k], (gates[k] * grad).astype(jnp.bfloat16), TN)
    out_ref[...] = placed.astype(jnp.bfloat16).reshape(out_ref.shape)


def slots_body(capacity, ready, outs):
    pos_ref, cot_ref = outs
    ids_ref = ready(0)
    pos = positions(capacity, [column(ids_ref[k : k + 1]) for k in range(2)])
    pair = lax.broadcasted_iota(jnp.int32, (pos[0].shape[0], 2), 1)
    pos_ref[...] = jnp.where(pair == 0, pos[0], pos[1])
    gates_ref = ready(1)
    gates = [column(gates_ref[k : k + 1]) for k in range(2)]
    place_cots(capacity, 0, ready, 2, gates, pos, cot_ref)


def late_slots_body(capacity, first, ready, outs):
    pos_ref, gates_ref = ready(0), ready(1)
    gates = [column(gates_ref[k : k + 1]) for k in range(2)]
    pos = [pos_ref[:, k : k + 1] for k in range(2)]
    place_cots(capacity, first, ready, 2, gates, pos, outs[0])


def attend_body(ready, outs):
    mixed_ref, normed_ref = outs
    query_ref, key_ref, value_ref = ready(0), ready(1), ready(2)
    parts = []
    for head in range(HEADS):
        cols = slice(head * HD, (head + 1) * HD)
        scores = dot(query_ref[:, cols], key_ref[:, cols], NT) * (HD ** (-0.5))
        weights = jnp.exp(scores - jnp.max(scores, axis=1, keepdims=True))
        total = jnp.sum(weights, axis=1, keepdims=True)
        accum = dot(weights.astype(jnp.bfloat16), value_ref[:, cols])
        parts.append((accum / total).astype(jnp.bfloat16))
    attended = jnp.concatenate(parts, axis=1)
    token_ref, proj_ref = ready(3), ready(4)
    mixed = token_ref[...].astype(jnp.float32) + dot(attended, proj_ref[...])
    mixed_ref[...] = mixed
    mean_square = jnp.mean(mixed * mixed, axis=1, keepdims=True)
    scale_ref, shift_ref = ready(5), ready(6)
    normed = mixed * lax.rsqrt(mean_square + 1e-06) * (1.0 + scale_ref[...]) + shift_ref[...]
    normed_ref[...] = normed.astype(jnp.bfloat16)


def place_body(capacity, firsts, ready, outs):
    pos_ref = ready(0)
    pos = [pos_ref[:, k : k + 1] for k in range(2)]
    normed = ready(1)[...]
    for first, out_ref in zip(firsts, outs):
        blocks, count, _ = out_ref.shape
        piece = count if blocks > 1 else capacity
        pick = choosers(
            [chunk_position(place, capacity, first, piece) for place in pos], blocks * count
        )
        placed = dot(pick[0] + pick[1], normed, TN).astype(jnp.bfloat16)
        out_ref[...] = placed.reshape(out_ref.shape)


def forward_body(ready, outs):
    keep_ref, send_ref, gate_pre_ref, up_pre_ref = outs
    row_ref = ready(0)
    rows = row_ref[...].reshape(-1, row_ref.shape[-1])
    gate_pre = dot(ready(1)[...], rows, NT)
    gate_pre_ref[...] = gate_pre
    up_pre = dot(ready(2)[...], rows, NT)
    up_pre_ref[...] = up_pre
    hidden = (gate_pre * jax.nn.sigmoid(gate_pre) * up_pre).astype(jnp.bfloat16)
    half = rows.shape[0] // 2
    partial = dot(hidden, ready(3)[...], TN).astype(jnp.bfloat16)
    keep_ref[...] = partial[:half]
    send_ref[...] = partial[half:]


def add_body(ready, outs):
    for n, out_ref in enumerate(outs):
        total = ready(2 * n)[...].astype(jnp.float32) + ready(2 * n + 1)[...].astype(jnp.float32)
        out_ref[...] = total.astype(jnp.bfloat16).reshape(out_ref.shape)


def backward_body(ready, outs):
    kept, sent = outs[:3], outs[3:]
    cot_ref, down_ref = ready(0), ready(1)
    cots = cot_ref[...]
    hidden_grad = dot(down_ref[...], cots, NT)
    gate_pre = ready(2)[...]
    up_pre = ready(3)[...]
    sigmoid = jax.nn.sigmoid(gate_pre)
    active = gate_pre * sigmoid
    gate_cot = hidden_grad * up_pre * sigmoid * (1.0 + gate_pre * (1.0 - sigmoid))
    up_cot = hidden_grad * active
    half = kept[0].shape[0]
    both = jnp.concatenate([gate_cot.astype(jnp.bfloat16), up_cot.astype(jnp.bfloat16)], axis=0)
    grads = dot(both, ready(4)[...])
    for n in range(2):
        kept[n][...] = grads[2 * n * half : (2 * n + 1) * half]
        sent[n][...] = grads[(2 * n + 1) * half : (2 * n + 2) * half].astype(jnp.bfloat16)
    grads = dot((active * up_pre).astype(jnp.bfloat16), cots)
    kept[2][...] = grads[:half]
    sent[2][...] = grads[half:].astype(jnp.bfloat16)


def combine_body(ready, outs):
    pos_ref, gates_ref = ready(0), ready(1)
    row_ref = ready(2)
    rows = row_ref[...].reshape(-1, row_ref.shape[-1])
    pick = choosers([pos_ref[:, 0:1], pos_ref[:, 1:2]], rows.shape[0])
    picked = dot(jnp.concatenate(pick, axis=0), rows)
    total = ready(3)[...]
    tokens = total.shape[0]
    for k in range(2):
        total = total + column(gates_ref[k : k + 1]) * picked[k * tokens : (k + 1) * tokens]
    outs[0][...] = total.astype(jnp.bfloat16)


def per_device(
    tokens,
    queries,
    keys,
    values,
    out_proj,
    mod_scale,
    mod_shift,
    expert_ids,
    gates,
    w_gate,
    w_up,
    w_down,
    out_grad,
):
    n_ctx = lax.axis_size("ctx")
    experts = n_ctx * lax.axis_size("group")
    local = tokens.shape[1]
    width = tokens.shape[2]
    hidden = w_gate.shape[0]
    capacity = 3 * local // experts
    slots = experts * capacity
    if capacity % PIECE == 0 and capacity > PIECE:
        blocks, height = experts, capacity
        row_cuts = [(0, capacity - PIECE), (capacity - PIECE, PIECE)]
        cot_cuts = [(0, PIECE), (PIECE, capacity - PIECE)]
    else:
        blocks, height = 1, slots
        row_cuts = cot_cuts = [(0, slots)]

    def swapped(value, axis):
        return lax.ppermute(value, axis, [(n, n ^ 1) for n in range(lax.axis_size(axis))])

    def exchanged(value):
        shaped = value if blocks > 1 else value.reshape(experts, capacity, width)
        moved = lax.all_to_all(shaped, ("ctx", "group"), split_axis=0, concat_axis=0, tiled=True)
        return moved.reshape(value.shape)

    def turned(value, step):
        size = lax.axis_size("ctx")
        return lax.ppermute(value, "ctx", [(n, (n + step) % size) for n in range(size)])

    def chunk_shapes(cuts):
        return [shape_of(blocks, count, width) for _, count in cuts]

    key_pieces = [keys[0]] + [turned(keys[0], step) for step in range(1, n_ctx)]
    value_pieces = [values[0]] + [turned(values[0], step) for step in range(1, n_ctx)]

    ids_rows = jnp.transpose(expert_ids[0])
    gate_rows = jnp.transpose(gates[0])
    pos, first_cots = call(
        functools.partial(slots_body, capacity),
        "slots",
        [whole(ids_rows), whole(gate_rows), whole(out_grad[0])],
        [shape_of(local, 2, dtype=jnp.int32)] + chunk_shapes(cot_cuts[:1]),
        flops=4 * slots * local * width,
    )
    cots = [exchanged(first_cots)]
    cots_across = [swapped(cots[0], "side")]

    mixed, normed = call(
        attend_body,
        "attend",
        [
            whole(queries[0]),
            rows_of(key_pieces),
            rows_of(value_pieces),
            whole(tokens[0]),
            whole(out_proj),
            whole(mod_scale),
            whole(mod_shift),
        ],
        [shape_of(local, width, dtype=jnp.float32), shape_of(local, width)],
        flops=4 * local * HEADS * HD * width,
    )
    placed = call(
        functools.partial(place_body, capacity, [first for first, _ in row_cuts]),
        "place",
        [whole(pos), whole(normed)],
        chunk_shapes(row_cuts),
        flops=2 * slots * local * width,
        after=cots,
    )
    rows = [exchanged(value) for value in placed]
    rows_across = [swapped(value, "side") for value in rows]

    for first, count in cot_cuts[1:]:
        (late_cots,) = call(
            functools.partial(late_slots_body, capacity, first),
            "late_slots",
            [whole(pos), whole(gate_rows), whole(out_grad[0])],
            [shape_of(blocks, count, width)],
            flops=4 * slots * local * width,
            after=rows,
        )
        cots.append(exchanged(late_cots))
        cots_across.append(swapped(cots[-1], "side"))

    pairs = [[weight, swapped(weight, "core")] for weight in (w_gate, w_up, w_down)]
    gate_pres, up_pres, returned = [], [], []
    after = cots_across[:1]
    for (_, count), own, across in zip(row_cuts, rows, rows_across):
        half = blocks * count
        pre = shape_of(2 * hidden, 2 * half, dtype=jnp.float32)
        keep, send, gate_pre, up_pre = call(
            forward_body,
            "forward",
            [([(own, None, 0), (across, None, 1)], (2,) + own.shape)]
            + [rows_of(pair) for pair in pairs],
            [shape_of(half, width)] * 2 + [pre] * 2,
            flops=24 * half * hidden * width,
            after=after,
        )
        after = [keep]
        gate_pres.append(gate_pre)
        up_pres.append(up_pre)
        (sums,) = call(
            add_body,
            "add",
            [whole(keep), whole(swapped(send, "side"))],
            [shape_of(blocks, count, width)],
        )
        returned.append(exchanged(sums))

    total_rows = 2 * slots
    row_pieces, cot_pieces, pre_pieces, line = [], [], [[], []], 0
    for n, (first, count) in enumerate(row_cuts):
        for side, both in enumerate(((rows, cots), (rows_across, cots_across))):
            for block in range(blocks):
                start = line + (side * blocks + block) * count
                row_pieces.append((both[0][n], block, pl.ds(start, count)))
                for (cot_first, cot_count), value in zip(cot_cuts, both[1]):
                    low = max(first, cot_first)
                    high = min(first + count, cot_first + cot_count)
                    if low < high:
                        source = (block, pl.ds(low - cot_first, high - low))
                        cot_pieces.append((value, source, pl.ds(start + low - first, high - low)))
        for pieces, pres in zip(pre_pieces, (gate_pres, up_pres)):
            target = (slice(None), pl.ds(line, 2 * blocks * count))
            pieces.append((pres[n], None, target))
        line += 2 * blocks * count
    grads = call(
        backward_body,
        "backward",
        [
            (cot_pieces, (total_rows, width)),
            rows_of(pairs[2]),
            (pre_pieces[0], (2 * hidden, total_rows)),
            (pre_pieces[1], (2 * hidden, total_rows)),
            (row_pieces, (total_rows, width)),
        ],
        [shape_of(hidden, width, dtype=jnp.float32)] * 3 + [shape_of(hidden, width)] * 3,
        flops=16 * total_rows * hidden * width,
    )
    operands = []
    for kept, sent in zip(grads[:3], grads[3:]):
        operands += [whole(kept), whole(swapped(sent, "core"))]
    grad_gate, grad_up, grad_down = call(
        add_body, "finish", operands, [shape_of(hidden, width)] * 3
    )

    returned_pieces = []
    for (first, count), value in zip(row_cuts, returned):
        returned_pieces.append((value, None, (slice(None), pl.ds(first, count))))
    (layer_out,) = call(
        combine_body,
        "combine",
        [
            whole(pos),
            whole(gate_rows),
            (returned_pieces, (blocks, height, width)),
            whole(mixed),
        ],
        [shape_of(local, width)],
        flops=4 * slots * local * width,
    )
    return (layer_out[None], grad_gate, grad_up, grad_down)


def solution(mesh):
    n_ctx = mesh.shape["ctx"]
    cut = (n_ctx, mesh.shape["exp"] // SHARDS, SHARDS // 2, 2)
    mesh = jax.sharding.Mesh(mesh.devices.reshape(cut), ("ctx",) + EXP)
    rows = P(EXP, "ctx", None)
    weight = P(("ctx",) + EXP, None)
    return jax.shard_map(
        per_device,
        mesh=mesh,
        in_specs=(rows, rows, rows, rows, P(), P(EXP, None), P(EXP, None), rows, rows)
        + (weight, weight, weight, rows),
        out_specs=(rows, weight, weight, weight),
        check_vma=False,
    )
```

```python
import functools

import jax
import jax.numpy as jnp
from jax import lax
from jax.experimental import pallas as pl
from jax.experimental.pallas import tpu as pltpu
from jax.sharding import PartitionSpec as P

HEADS = 8
HD = 128
SHARDS = 4
UNIT = 48
VMEM_LIMIT = 63 * 1024 * 1024
EXP = ("group", "side", "core")

NT = (((1,), (1,)), ((), ()))
TN = (((0,), (0,)), ((), ()))

VMEM = pl.BlockSpec(memory_space=pltpu.VMEM)
ANY = pl.BlockSpec(memory_space=pl.ANY)


def dot(a, b, dims=(((1,), (0,)), ((), ()))):
    return lax.dot_general(a, b, dims, preferred_element_type=jnp.float32)


def shape_of(*shape, dtype=jnp.bfloat16):
    return jax.ShapeDtypeStruct(shape, dtype)


def call(body, name, operands, outs, micros=1, after=(), copied=()):
    pieces = [piece for group, _ in operands for piece in group]
    values = []
    for value, _, _ in pieces:
        if not any(value is known for known in values):
            values.append(value)
    where = [[value is known for known in values].index(True) for value, _, _ in pieces]
    n_values, n_outs = len(values), len(outs)
    n_in = n_values + len(copied) + len(after)
    packs = [shape_of(sum(v.shape[0] for v in copied), copied[0].shape[1])] if copied else []

    def kernel(*refs):
        out_refs = refs[n_in : n_in + n_outs]
        targets = refs[n_in + n_outs + len(packs) : -1]
        sem = refs[-1]
        waits, at = [], 0
        for (group, _), target in zip(operands, targets):
            copies = []
            for _, source_index, target_index in group:
                source = refs[where[at]]
                if callable(source_index):
                    source_index = source_index()
                copies.append(
                    pltpu.make_async_copy(
                        source if source_index is None else source.at[source_index],
                        target if target_index is None else target.at[target_index],
                        sem.at[at],
                    )
                )
                at += 1
            waits.append(copies)
        for copies in waits:
            for copy in copies:
                copy.start()

        extra, row = [], 0
        for n, value in enumerate(copied):
            size = value.shape[0]
            target = refs[n_in + n_outs].at[pl.ds(row, size)]
            row += size
            extra.append(pltpu.make_async_copy(refs[n_values + n], target, sem.at[at + n]))
            extra[-1].start()

        def ready(n):
            for copy in waits[n]:
                copy.wait()
            return targets[n]

        body(ready, out_refs)
        for copy in extra:
            copy.wait()

    return pl.pallas_call(
        kernel,
        out_shape=tuple(outs) + tuple(packs),
        in_specs=[ANY] * n_in,
        out_specs=(VMEM,) * n_outs + (ANY,) * len(packs),
        scratch_shapes=[pltpu.VMEM(shape, group[0][0].dtype) for group, shape in operands]
        + [pltpu.SemaphoreType.DMA((len(pieces) + len(copied),))],
        compiler_params=pltpu.CompilerParams(vmem_limit_bytes=VMEM_LIMIT),
        cost_estimate=pl.CostEstimate(
            flops=int(micros * 1.15e9), bytes_accessed=0, transcendentals=0
        ),
        name=name,
    )(*values, *copied, *after)


def whole(value):
    return [(value, None, None)], value.shape


def rows_of(values):
    pieces, row = [], 0
    for value in values:
        pieces.append((value, None, pl.ds(row, value.shape[0])))
        row += value.shape[0]
    return pieces, (row, values[0].shape[1])


def column(row):
    size = row.shape[1]
    across = lax.broadcasted_iota(jnp.int32, (size, size), 0)
    along = lax.broadcasted_iota(jnp.int32, (size, size), 1)
    return jnp.sum(jnp.where(across == along, row, jnp.zeros_like(row)), axis=1, keepdims=True)


def choosers(pos, slots):
    line = lax.broadcasted_iota(jnp.int32, (pos[0].shape[0], slots), 1)
    return [(place == line).astype(jnp.bfloat16) for place in pos]


def unit_place(n_ctx, groups, capacity, ids, slot):
    me_ctx, me_group = lax.axis_index("ctx"), lax.axis_index("group")
    ctx = ((ids >> (groups.bit_length() - 1)) - me_ctx) & (n_ctx - 1)
    group = ((ids & (groups - 1)) - me_group) & (groups - 1)
    return ((group ^ (group >> 1)) * n_ctx + ctx) * capacity + slot


def slots_body(n_ctx, groups, capacity, ready, outs):
    pos_ref, cot_ref = outs
    ids_ref = ready(0)
    ids = [column(ids_ref[k : k + 1]) for k in range(2)]
    tokens = ids[0].shape[0]
    lanes = lax.broadcasted_iota(jnp.int32, (tokens, 128), 1)
    hot = [(ids[k] == lanes).astype(jnp.float32) for k in range(2)]
    later = lax.broadcasted_iota(jnp.int32, (tokens, tokens), 0)
    earlier = lax.broadcasted_iota(jnp.int32, (tokens, tokens), 1)
    lower = (later > earlier).astype(jnp.bfloat16)
    before = dot(lower, (hot[0] + hot[1]).astype(jnp.bfloat16))
    slot = [
        jnp.sum(hot[k] * before, axis=1, keepdims=True).astype(jnp.int32) for k in range(2)
    ]
    pos = [unit_place(n_ctx, groups, capacity, ids[k], slot[k]) for k in range(2)]
    pair = lax.broadcasted_iota(jnp.int32, (tokens, 2), 1)
    pos_ref[...] = jnp.where(pair == 0, pos[0], pos[1])
    gates_ref = ready(1)
    pick = choosers([ids[k] * capacity + slot[k] for k in range(2)], cot_ref.shape[0])
    grad = ready(2)[...].astype(jnp.float32)
    placed = 0.0
    for k in range(2):
        gate = column(gates_ref[k : k + 1])
        placed = placed + dot(pick[k], (gate * grad).astype(jnp.bfloat16), TN)
    cot_ref[...] = placed.astype(jnp.bfloat16)


def store_units(placed, unit_refs):
    placed = placed.astype(jnp.bfloat16)
    rows = unit_refs[0].shape[0]
    for n, ref in enumerate(unit_refs):
        ref[...] = placed[n * rows : (n + 1) * rows]


def attend_body(ready, outs):
    mixed_ref, *unit_refs = outs
    query_ref, key_ref, value_ref = ready(0), ready(1), ready(2)
    parts = []
    for head in range(HEADS):
        cols = slice(head * HD, (head + 1) * HD)
        scores = dot(query_ref[:, cols], key_ref[:, cols], NT) * (HD ** (-0.5))
        weights = jnp.exp(scores - jnp.max(scores, axis=1, keepdims=True))
        total = jnp.sum(weights, axis=1, keepdims=True)
        accum = dot(weights.astype(jnp.bfloat16), value_ref[:, cols])
        parts.append((accum / total).astype(jnp.bfloat16))
    attended = jnp.concatenate(parts, axis=1)
    token_ref, proj_ref = ready(3), ready(4)
    mixed = token_ref[...].astype(jnp.float32) + dot(attended, proj_ref[...])
    mixed_ref[...] = mixed
    mean_square = jnp.mean(mixed * mixed, axis=1, keepdims=True)
    scale_ref, shift_ref = ready(5), ready(6)
    normed = mixed * lax.rsqrt(mean_square + 1e-06) * (1.0 + scale_ref[...]) + shift_ref[...]
    pos_ref = ready(7)
    pick = choosers(
        [pos_ref[:, 0:1], pos_ref[:, 1:2]], len(unit_refs) * unit_refs[0].shape[0]
    )
    store_units(dot(pick[0] + pick[1], normed.astype(jnp.bfloat16), TN), unit_refs)


def forward_body(pieces, ready, outs):
    keep_refs, send_refs = outs[:pieces], outs[pieces : 2 * pieces]
    gate_pre_ref, up_pre_ref = outs[2 * pieces :]
    rows = ready(0)[...]
    gate_pre = dot(ready(1)[...], rows, NT)
    gate_pre_ref[...] = gate_pre
    up_pre = dot(ready(2)[...], rows, NT)
    up_pre_ref[...] = up_pre
    hidden = (gate_pre * jax.nn.sigmoid(gate_pre) * up_pre).astype(jnp.bfloat16)
    half = rows.shape[0] // 2
    partial = dot(hidden, ready(3)[...], TN)
    store_units(partial[:half], keep_refs)
    store_units(partial[half:], send_refs)


def add_body(ready, outs):
    store_units(ready(0)[...].astype(jnp.float32) + ready(1)[...].astype(jnp.float32), outs)


def finish_body(ready, outs):
    sent_ref = ready(3)
    size = outs[0].shape[0]
    for n, out_ref in enumerate(outs):
        total = ready(n)[...] + sent_ref[n * size : (n + 1) * size].astype(jnp.float32)
        out_ref[...] = total.astype(jnp.bfloat16)


def backward_body(ready, outs):
    kept, sent_ref = outs[:3], outs[3]
    cot_ref, down_ref = ready(0), ready(1)
    cots = cot_ref[...]
    hidden_grad = dot(down_ref[...], cots, NT)
    gate_pre = ready(2)[...]
    up_pre = ready(3)[...]
    sigmoid = jax.nn.sigmoid(gate_pre)
    active = gate_pre * sigmoid
    gate_cot = hidden_grad * up_pre * sigmoid * (1.0 + gate_pre * (1.0 - sigmoid))
    up_cot = hidden_grad * active
    half = kept[0].shape[0]
    both = jnp.concatenate([gate_cot.astype(jnp.bfloat16), up_cot.astype(jnp.bfloat16)], axis=0)
    grads = dot(both, ready(4)[...])
    for n in range(2):
        kept[n][...] = grads[2 * n * half : (2 * n + 1) * half]
        sent = grads[(2 * n + 1) * half : (2 * n + 2) * half].astype(jnp.bfloat16)
        sent_ref[n * half : (n + 1) * half] = sent
    grads = dot((active * up_pre).astype(jnp.bfloat16), cots)
    kept[2][...] = grads[:half]
    sent_ref[2 * half :] = grads[half:].astype(jnp.bfloat16)


def combine_body(ready, outs):
    pos_ref, gates_ref = ready(0), ready(1)
    rows = ready(2)[...]
    pick = choosers([pos_ref[:, 0:1], pos_ref[:, 1:2]], rows.shape[0])
    picked = dot(jnp.concatenate(pick, axis=0), rows)
    total = ready(3)[...]
    tokens = total.shape[0]
    for k in range(2):
        total = total + column(gates_ref[k : k + 1]) * picked[k * tokens : (k + 1) * tokens]
    outs[0][...] = total.astype(jnp.bfloat16)


def per_device(
    tokens,
    queries,
    keys,
    values,
    out_proj,
    mod_scale,
    mod_shift,
    expert_ids,
    gates,
    w_gate,
    w_up,
    w_down,
    out_grad,
):
    n_ctx = lax.axis_size("ctx")
    groups = lax.axis_size("group")
    experts = n_ctx * groups
    local = tokens.shape[1]
    width = tokens.shape[2]
    hidden = w_gate.shape[0]
    capacity = 3 * local // experts
    slots = experts * capacity
    bundle = max(1, UNIT // capacity)
    units = experts // bundle
    unit_rows = bundle * capacity
    assert n_ctx & (n_ctx - 1) == 0 and groups & (groups - 1) == 0
    gray = sorted(range(groups), key=lambda group: group ^ (group >> 1))
    distances = [(group, ctx) for group in gray for ctx in range(n_ctx)]

    def swapped(value, axis):
        return lax.ppermute(value, axis, [(n, n ^ 1) for n in range(lax.axis_size(axis))])

    def shifted(value, group, ctx):
        moves = []
        for c in range(n_ctx):
            for g in range(groups):
                target = (c + ctx) % n_ctx * groups + (g + group) % groups
                moves.append((c * groups + g, target))
        return lax.ppermute(value, ("ctx", "group"), moves)

    def exchanged(unit, n, sign):
        parts = []
        for m in range(bundle):
            group, ctx = distances[n * bundle + m]
            part = unit if bundle == 1 else unit[m * capacity : (m + 1) * capacity]
            moved = shifted(part, sign * group, sign * ctx) if group or ctx else part
            parts.append(moved)
        return parts[0] if bundle == 1 else jnp.concatenate(parts, axis=0)

    key_pieces = [keys[0]] + [shifted(keys[0], 0, step) for step in range(1, n_ctx)]
    value_pieces = [values[0]] + [shifted(values[0], 0, step) for step in range(1, n_ctx)]

    ids_rows = jnp.transpose(expert_ids[0])
    gate_rows = jnp.transpose(gates[0])
    pos, cots, packed = call(
        functools.partial(slots_body, n_ctx, groups, capacity),
        "slots",
        [whole(ids_rows), whole(gate_rows), whole(out_grad[0])],
        [shape_of(local, 2, dtype=jnp.int32), shape_of(slots, width)],
        3,
        copied=[w_gate, w_up, w_down],
    )
    other_weights = swapped(packed, "core")
    cots = lax.all_to_all(
        cots.reshape(experts, capacity, width), ("ctx", "group"), 0, 0, tiled=True
    )
    sources = [
        (lax.axis_index("ctx") - ctx) % n_ctx * groups
        + (lax.axis_index("group") - group) % groups
        for group, ctx in distances
    ]
    if bundle > 1:
        cots = jnp.take(cots, jnp.stack(sources), axis=0).reshape(units, unit_rows, width)
    cots_across = swapped(cots, "side")

    mixed, *row_units = call(
        attend_body,
        "attend",
        [
            whole(queries[0]),
            rows_of(key_pieces),
            rows_of(value_pieces),
            whole(tokens[0]),
            whole(out_proj),
            whole(mod_scale),
            whole(mod_shift),
            whole(pos),
        ],
        [shape_of(local, width, dtype=jnp.float32)] + [shape_of(unit_rows, width)] * units,
        6,
        after=[other_weights],
    )
    rows = [exchanged(unit, n, 1) for n, unit in enumerate(row_units)]
    rows_across = [swapped(unit, "side") for unit in rows]

    pairs = []
    for n, weight in enumerate((w_gate, w_up, w_down)):
        second = (other_weights, pl.ds(n * hidden, hidden), pl.ds(hidden, hidden))
        pairs.append(([(weight, None, pl.ds(0, hidden)), second], (2 * hidden, width)))
    gate_pres, up_pres, returned, row_order, unit_order = [], [], [], [], []
    per_call = units // 2
    pieces = per_call // 2
    for first in range(0, units, per_call):
        some = range(first, first + per_call)
        half = per_call * unit_rows
        blocks = [rows[n] for n in some] + [rows_across[n] for n in some]
        row_order += blocks
        unit_order += [(0, n) for n in some] + [(1, n) for n in some]
        *partials, gate_pre, up_pre = call(
            functools.partial(forward_body, pieces),
            "forward",
            [rows_of(blocks)] + pairs,
            [shape_of(half // pieces, width)] * (2 * pieces)
            + [shape_of(2 * hidden, 2 * half, dtype=jnp.float32)] * 2,
            7,
            after=[cots_across] if first else [],
        )
        gate_pres.append(gate_pre)
        up_pres.append(up_pre)
        for piece in range(pieces):
            keep, send = partials[piece], partials[pieces + piece]
            sums = call(
                add_body,
                "add",
                [whole(keep), whole(swapped(send, "side"))],
                [shape_of(unit_rows, width)] * (per_call // pieces),
                2,
            )
            for n, unit in enumerate(sums):
                returned.append(exchanged(unit, first + piece * (per_call // pieces) + n, -1))

    def source_block(n):
        if bundle > 1:
            return n
        group, ctx = distances[n]
        ctx = (lax.axis_index("ctx") - ctx) & (n_ctx - 1)
        return ctx * groups + ((lax.axis_index("group") - group) & (groups - 1))

    total_rows = 2 * slots
    cot_pieces = []
    for at, (side, n) in enumerate(unit_order):
        block = functools.partial(source_block, n)
        cot_pieces.append(((cots, cots_across)[side], block, pl.ds(at * unit_rows, unit_rows)))
    pre_pieces = [[], []]
    for line, pres in zip(pre_pieces, (gate_pres, up_pres)):
        for n, pre in enumerate(pres):
            size = pre.shape[1]
            line.append((pre, None, (slice(None), pl.ds(n * size, size))))
    *kept, sent = call(
        backward_body,
        "backward",
        [
            (cot_pieces, (total_rows, width)),
            pairs[2],
            (pre_pieces[0], (2 * hidden, total_rows)),
            (pre_pieces[1], (2 * hidden, total_rows)),
            rows_of(row_order),
        ],
        [shape_of(hidden, width, dtype=jnp.float32)] * 3 + [shape_of(3 * hidden, width)],
        15,
    )
    grad_gate, grad_up, grad_down = call(
        finish_body,
        "finish",
        [whole(value) for value in kept] + [whole(swapped(sent, "core"))],
        [shape_of(hidden, width)] * 3,
        5,
    )

    (layer_out,) = call(
        combine_body,
        "combine",
        [whole(pos), whole(gate_rows), rows_of(returned), whole(mixed)],
        [shape_of(local, width)],
        3,
    )
    return (layer_out[None], grad_gate, grad_up, grad_down)


def solution(mesh):
    n_ctx = mesh.shape["ctx"]
    cut = (n_ctx, mesh.shape["exp"] // SHARDS, SHARDS // 2, 2)
    mesh = jax.sharding.Mesh(mesh.devices.reshape(cut), ("ctx",) + EXP)
    rows = P(EXP, "ctx", None)
    weight = P(("ctx",) + EXP, None)
    return jax.shard_map(
        per_device,
        mesh=mesh,
        in_specs=(rows, rows, rows, rows, P(), P(EXP, None), P(EXP, None), rows, rows)
        + (weight, weight, weight, rows),
        out_specs=(rows, weight, weight, weight),
        check_vma=False,
    )
```

```python
import functools

import jax
import jax.numpy as jnp
from jax import lax
from jax.experimental import pallas as pl
from jax.experimental.pallas import tpu as pltpu
from jax.sharding import PartitionSpec as P

HEADS = 8
HD = 128
SHARDS = 4
VMEM_LIMIT = 63 * 1024 * 1024
EXP = ("group", "side", "core")

NT = (((1,), (1,)), ((), ()))
TN = (((0,), (0,)), ((), ()))

VMEM = pl.BlockSpec(memory_space=pltpu.VMEM)
ANY = pl.BlockSpec(memory_space=pl.ANY)


def dot(a, b, dims=(((1,), (0,)), ((), ()))):
    return lax.dot_general(a, b, dims, preferred_element_type=jnp.float32)


def shape_of(*shape, dtype=jnp.bfloat16):
    return jax.ShapeDtypeStruct(shape, dtype)


def call(body, name, operands, outs, micros=1, after=()):
    pieces = [piece for group, _ in operands for piece in group]
    values = []
    for value, _, _ in pieces:
        if not any(value is known for known in values):
            values.append(value)
    where = [[value is known for known in values].index(True) for value, _, _ in pieces]
    n_values, n_outs = len(values), len(outs)
    n_in = n_values + len(after)

    def kernel(*refs):
        out_refs = refs[n_in : n_in + n_outs]
        targets = refs[n_in + n_outs : -1]
        sem = refs[-1]
        waits, at = [], 0
        for (group, _), target in zip(operands, targets):
            copies = []
            for _, source_index, target_index in group:
                source = refs[where[at]]
                copies.append(
                    pltpu.make_async_copy(
                        source if source_index is None else source.at[source_index],
                        target if target_index is None else target.at[target_index],
                        sem.at[at],
                    )
                )
                at += 1
            waits.append(copies)
        for copies in waits:
            for copy in copies:
                copy.start()

        def ready(n):
            for copy in waits[n]:
                copy.wait()
            return targets[n]

        body(ready, out_refs)

    return pl.pallas_call(
        kernel,
        out_shape=tuple(outs),
        in_specs=[ANY] * n_in,
        out_specs=(VMEM,) * n_outs,
        scratch_shapes=[pltpu.VMEM(shape, group[0][0].dtype) for group, shape in operands]
        + [pltpu.SemaphoreType.DMA((len(pieces),))],
        compiler_params=pltpu.CompilerParams(vmem_limit_bytes=VMEM_LIMIT),
        cost_estimate=pl.CostEstimate(
            flops=int(micros * 1.15e9), bytes_accessed=0, transcendentals=0
        ),
        name=name,
    )(*values, *after)


def whole(value):
    return [(value, None, None)], value.shape


def rows_of(values):
    pieces, row = [], 0
    for value in values:
        pieces.append((value, None, pl.ds(row, value.shape[0])))
        row += value.shape[0]
    return pieces, (row, values[0].shape[1])


def column(row):
    size = row.shape[1]
    across = lax.broadcasted_iota(jnp.int32, (size, size), 0)
    along = lax.broadcasted_iota(jnp.int32, (size, size), 1)
    return jnp.sum(jnp.where(across == along, row, jnp.zeros_like(row)), axis=1, keepdims=True)


def choosers(pos, slots):
    line = lax.broadcasted_iota(jnp.int32, (pos[0].shape[0], slots), 1)
    return [(place == line).astype(jnp.bfloat16) for place in pos]


def earlier_count(hot):
    tokens = hot.shape[0]
    later = lax.broadcasted_iota(jnp.int32, (tokens, tokens), 0)
    earlier = lax.broadcasted_iota(jnp.int32, (tokens, tokens), 1)
    return dot((later > earlier).astype(jnp.bfloat16), hot.astype(jnp.bfloat16))


def begin_body(n_ctx, groups, capacity, ready, outs):
    pos_ref, packed_ref = outs
    info_ref = ready(0)
    ids = [column(info_ref[k : k + 1]).astype(jnp.int32) for k in range(2)]
    lanes = lax.broadcasted_iota(jnp.int32, (ids[0].shape[0], 128), 1)
    hot = [(ids[k] == lanes).astype(jnp.float32) for k in range(2)]
    before = earlier_count(hot[0] + hot[1])
    me_ctx, me_group = lax.axis_index("ctx"), lax.axis_index("group")
    pos = []
    for k in range(2):
        slot = jnp.sum(hot[k] * before, axis=1, keepdims=True).astype(jnp.int32)
        ctx = ((ids[k] >> (groups.bit_length() - 1)) - me_ctx) & (n_ctx - 1)
        group = ((ids[k] & (groups - 1)) - me_group) & (groups - 1)
        pos.append((ctx * groups + group) * capacity + slot)
    pair = lax.broadcasted_iota(jnp.int32, (pos[0].shape[0], 2), 1)
    pos_ref[...] = jnp.where(pair == 0, pos[0], pos[1])
    size = packed_ref.shape[0] // 3
    for n in range(3):
        packed_ref[n * size : (n + 1) * size] = ready(1 + n)[...]


def select_body(n_ctx, groups, capacity, gated, ready, outs):
    info_ref = ready(0)
    me_ctx, me_group = lax.axis_index("ctx"), lax.axis_index("group")
    shift = groups.bit_length() - 1
    picks = [[] for _ in range(n_ctx)]
    gates = [[] for _ in range(n_ctx)]
    for source in range(groups):
        info = [column(info_ref[source, k : k + 1]) for k in range(4)]
        ids = [info[k].astype(jnp.int32) for k in range(2)]
        tokens = ids[0].shape[0]
        lanes = lax.broadcasted_iota(jnp.int32, (tokens, 128), 1)
        expert = (((me_ctx + lanes) & (n_ctx - 1)) << shift) + me_group
        hot = [((ids[k] == expert) & (lanes < n_ctx)).astype(jnp.float32) for k in range(2)]
        named = hot[0] + hot[1]
        before = earlier_count(named)
        gate = hot[0] * info[2] + hot[1] * info[3]
        line = lax.broadcasted_iota(jnp.int32, (tokens, groups * capacity), 1)
        start = ((me_group - source) & (groups - 1)) * capacity
        for step in range(n_ctx):
            place = before[:, step : step + 1].astype(jnp.int32) + start
            place = jnp.where(named[:, step : step + 1] > 0.0, place, -1)
            picks[step].append((place == line).astype(jnp.bfloat16))
            gates[step].append(gate[:, step : step + 1])
    rows = ready(1)[...]
    if gated:
        grads = rows.astype(jnp.float32)
        for step, out_ref in enumerate(outs):
            scaled = (jnp.concatenate(gates[step], axis=0) * grads).astype(jnp.bfloat16)
            out_ref[...] = dot(jnp.concatenate(picks[step], axis=0), scaled, TN).astype(
                jnp.bfloat16
            )
    else:
        pick = jnp.concatenate([jnp.concatenate(step, axis=0) for step in picks], axis=1)
        store_units(dot(pick, rows, TN), outs)


def store_units(placed, unit_refs):
    placed = placed.astype(jnp.bfloat16)
    rows = unit_refs[0].shape[0]
    for n, ref in enumerate(unit_refs):
        ref[...] = placed[n * rows : (n + 1) * rows]


def attend_body(ready, outs):
    mixed_ref, normed_ref = outs
    query_ref, key_ref, value_ref = ready(0), ready(1), ready(2)
    parts = []
    for head in range(HEADS):
        cols = slice(head * HD, (head + 1) * HD)
        scores = dot(query_ref[:, cols], key_ref[:, cols], NT) * (HD ** (-0.5))
        weights = jnp.exp(scores - jnp.max(scores, axis=1, keepdims=True))
        total = jnp.sum(weights, axis=1, keepdims=True)
        accum = dot(weights.astype(jnp.bfloat16), value_ref[:, cols])
        parts.append((accum / total).astype(jnp.bfloat16))
    attended = jnp.concatenate(parts, axis=1)
    token_ref, proj_ref = ready(3), ready(4)
    mixed = token_ref[...].astype(jnp.float32) + dot(attended, proj_ref[...])
    mixed_ref[...] = mixed
    mean_square = jnp.mean(mixed * mixed, axis=1, keepdims=True)
    scale_ref, shift_ref = ready(5), ready(6)
    normed = mixed * lax.rsqrt(mean_square + 1e-06) * (1.0 + scale_ref[...]) + shift_ref[...]
    normed_ref[...] = normed.astype(jnp.bfloat16)


def forward_body(ready, outs):
    keep_ref, send_ref, gate_pre_ref, up_pre_ref = outs
    rows = ready(0)[...]
    gate_pre = dot(ready(1)[...], rows, NT)
    gate_pre_ref[...] = gate_pre
    up_pre = dot(ready(2)[...], rows, NT)
    up_pre_ref[...] = up_pre
    hidden = (gate_pre * jax.nn.sigmoid(gate_pre) * up_pre).astype(jnp.bfloat16)
    half = rows.shape[0] // 2
    partial = dot(hidden, ready(3)[...], TN).astype(jnp.bfloat16)
    keep_ref[...] = partial[:half]
    send_ref[...] = partial[half:]


def add_body(ready, outs):
    store_units(ready(0)[...].astype(jnp.float32) + ready(1)[...].astype(jnp.float32), outs)


def finish_body(ready, outs):
    sent_ref = ready(3)
    size = outs[0].shape[0]
    for n, out_ref in enumerate(outs):
        total = ready(n)[...] + sent_ref[n * size : (n + 1) * size].astype(jnp.float32)
        out_ref[...] = total.astype(jnp.bfloat16)


def backward_body(ready, outs):
    kept, sent_ref = outs[:3], outs[3]
    cot_ref, down_ref = ready(0), ready(1)
    cots = cot_ref[...]
    hidden_grad = dot(down_ref[...], cots, NT)
    gate_pre = ready(2)[...]
    up_pre = ready(3)[...]
    sigmoid = jax.nn.sigmoid(gate_pre)
    active = gate_pre * sigmoid
    gate_cot = hidden_grad * up_pre * sigmoid * (1.0 + gate_pre * (1.0 - sigmoid))
    up_cot = hidden_grad * active
    half = kept[0].shape[0]
    both = jnp.concatenate([gate_cot.astype(jnp.bfloat16), up_cot.astype(jnp.bfloat16)], axis=0)
    grads = dot(both, ready(4)[...])
    for n in range(2):
        kept[n][...] = grads[2 * n * half : (2 * n + 1) * half]
        sent = grads[(2 * n + 1) * half : (2 * n + 2) * half].astype(jnp.bfloat16)
        sent_ref[n * half : (n + 1) * half] = sent
    grads = dot((active * up_pre).astype(jnp.bfloat16), cots)
    kept[2][...] = grads[:half]
    sent_ref[2 * half :] = grads[half:].astype(jnp.bfloat16)


def combine_body(ready, outs):
    pos_ref, gates_ref = ready(0), ready(1)
    rows = ready(2)[...]
    pick = choosers([pos_ref[:, 0:1], pos_ref[:, 1:2]], rows.shape[0])
    picked = dot(jnp.concatenate(pick, axis=0), rows)
    total = ready(3)[...]
    tokens = total.shape[0]
    for k in range(2):
        total = total + column(gates_ref[k : k + 1]) * picked[k * tokens : (k + 1) * tokens]
    outs[0][...] = total.astype(jnp.bfloat16)


def per_device(
    tokens,
    queries,
    keys,
    values,
    out_proj,
    mod_scale,
    mod_shift,
    expert_ids,
    gates,
    w_gate,
    w_up,
    w_down,
    out_grad,
):
    n_ctx = lax.axis_size("ctx")
    groups = lax.axis_size("group")
    experts = n_ctx * groups
    local = tokens.shape[1]
    width = tokens.shape[2]
    hidden = w_gate.shape[0]
    capacity = 3 * local // experts
    slots = experts * capacity
    part = groups * capacity
    assert n_ctx & (n_ctx - 1) == 0 and groups & (groups - 1) == 0

    def swapped(value, axis):
        return lax.ppermute(value, axis, [(n, n ^ 1) for n in range(lax.axis_size(axis))])

    def shifted(value, ctx, group):
        if not ctx and not group:
            return value
        moves = []
        for c in range(n_ctx):
            for g in range(groups):
                target = (c + ctx) % n_ctx * groups + (g + group) % groups
                moves.append((c * groups + g, target))
        return lax.ppermute(value, ("ctx", "group"), moves)

    key_pieces = [shifted(keys[0], step, 0) for step in range(n_ctx)]
    value_pieces = [shifted(values[0], step, 0) for step in range(n_ctx)]

    gate_rows = jnp.transpose(gates[0])
    info = jnp.concatenate(
        [jnp.transpose(expert_ids[0]).astype(jnp.float32), gate_rows, jnp.zeros((4, local))]
    )
    pos, packed = call(
        functools.partial(begin_body, n_ctx, groups, capacity),
        "begin",
        [whole(info), whole(w_gate), whole(w_up), whole(w_down)],
        [shape_of(local, 2, dtype=jnp.int32), shape_of(3 * hidden, width)],
        4,
    )
    other_weights = swapped(packed, "core")
    infos = lax.all_gather(info, "group")
    all_grads = lax.all_gather(out_grad[0], "group", tiled=True)

    mixed, normed = call(
        attend_body,
        "attend",
        [
            whole(queries[0]),
            rows_of(key_pieces),
            rows_of(value_pieces),
            whole(tokens[0]),
            whole(out_proj),
            whole(mod_scale),
            whole(mod_shift),
        ],
        [shape_of(local, width, dtype=jnp.float32), shape_of(local, width)],
        6,
        after=[other_weights, infos],
    )
    all_tokens = lax.all_gather(normed, "group", tiled=True)

    def selected(name, values, gated, after):
        parts = call(
            functools.partial(select_body, n_ctx, groups, capacity, gated),
            name,
            [whole(infos), whole(values)],
            [shape_of(part, width)] * n_ctx,
            3,
            after=after,
        )
        own = [shifted(value, step, 0) for step, value in enumerate(parts)]
        return own, [swapped(value, "side") for value in own]

    rows, rows_across = selected("select", all_tokens, False, [])
    cots, cots_across = selected("select_cots", all_grads, True, rows)

    pairs = []
    for n, weight in enumerate((w_gate, w_up, w_down)):
        second = (other_weights, pl.ds(n * hidden, hidden), pl.ds(hidden, hidden))
        pairs.append(([(weight, None, pl.ds(0, hidden)), second], (2 * hidden, width)))
    gate_pres, up_pres, returned, row_order, cot_order, totals = [], [], [], [], [], []
    per_call = n_ctx // 2
    for first in range(0, n_ctx, per_call):
        some = slice(first, first + per_call)
        half = per_call * part
        blocks = rows[some] + rows_across[some]
        row_order += blocks
        cot_order += cots[some] + cots_across[some]
        pre = shape_of(2 * hidden, 2 * half, dtype=jnp.float32)
        keep, send, gate_pre, up_pre = call(
            forward_body,
            "forward",
            [rows_of(blocks)] + pairs,
            [shape_of(half, width)] * 2 + [pre] * 2,
            7,
        )
        gate_pres.append(gate_pre)
        up_pres.append(up_pre)
        count = per_call * groups
        aligned = capacity % 16 == 0
        sums = call(
            add_body,
            "add",
            [whole(keep), whole(swapped(send, "side"))],
            [shape_of(capacity, width)] * count if aligned else [shape_of(half, width)],
            2,
        )
        totals += sums
        if not aligned:
            sums = [sums[0][n * capacity : (n + 1) * capacity] for n in range(count)]
        for n, unit in enumerate(sums):
            returned.append(shifted(unit, -(first + n // groups), -(n % groups)))
    if not aligned:
        returned = [jnp.concatenate(returned, axis=0)]

    total_rows = 2 * slots
    pre_pieces = [[], []]
    for line, pres in zip(pre_pieces, (gate_pres, up_pres)):
        for n, pre in enumerate(pres):
            size = pre.shape[1]
            line.append((pre, None, (slice(None), pl.ds(n * size, size))))
    *kept, sent = call(
        backward_body,
        "backward",
        [
            rows_of(cot_order),
            pairs[2],
            (pre_pieces[0], (2 * hidden, total_rows)),
            (pre_pieces[1], (2 * hidden, total_rows)),
            rows_of(row_order),
        ],
        [shape_of(hidden, width, dtype=jnp.float32)] * 3 + [shape_of(3 * hidden, width)],
        15,
        after=totals,
    )
    grad_gate, grad_up, grad_down = call(
        finish_body,
        "finish",
        [whole(value) for value in kept] + [whole(swapped(sent, "core"))],
        [shape_of(hidden, width)] * 3,
        5,
    )

    (layer_out,) = call(
        combine_body,
        "combine",
        [whole(pos), whole(gate_rows), rows_of(returned), whole(mixed)],
        [shape_of(local, width)],
        3,
    )
    return (layer_out[None], grad_gate, grad_up, grad_down)


def solution(mesh):
    n_ctx = mesh.shape["ctx"]
    cut = (n_ctx, mesh.shape["exp"] // SHARDS, SHARDS // 2, 2)
    mesh = jax.sharding.Mesh(mesh.devices.reshape(cut), ("ctx",) + EXP)
    rows = P(EXP, "ctx", None)
    weight = P(("ctx",) + EXP, None)
    return jax.shard_map(
        per_device,
        mesh=mesh,
        in_specs=(rows, rows, rows, rows, P(), P(EXP, None), P(EXP, None), rows, rows)
        + (weight, weight, weight, rows),
        out_specs=(rows, weight, weight, weight),
        check_vma=False,
    )
```

```python
import functools

import jax
import jax.numpy as jnp
from jax import lax
from jax.experimental import pallas as pl
from jax.experimental.pallas import tpu as pltpu
from jax.sharding import PartitionSpec as P

HEADS = 8
HD = 128
SHARDS = 4
PIECE = 16
VMEM_LIMIT = 63 * 1024 * 1024
EXP = ("group", "side", "core")

NT = (((1,), (1,)), ((), ()))
TN = (((0,), (0,)), ((), ()))

VMEM = pl.BlockSpec(memory_space=pltpu.VMEM)
ANY = pl.BlockSpec(memory_space=pl.ANY)


def dot(a, b, dims=(((1,), (0,)), ((), ()))):
    return lax.dot_general(a, b, dims, preferred_element_type=jnp.float32)


def shape_of(*shape, dtype=jnp.bfloat16):
    return jax.ShapeDtypeStruct(shape, dtype)


def call(body, name, operands, outs, micros=1, after=()):
    pieces = [piece for group, _ in operands for piece in group]
    values = []
    for value, _, _ in pieces:
        if not any(value is known for known in values):
            values.append(value)
    where = [[value is known for known in values].index(True) for value, _, _ in pieces]
    n_in, n_outs = len(values) + len(after), len(outs)

    def kernel(*refs):
        out_refs = refs[n_in : n_in + n_outs]
        targets = refs[n_in + n_outs : -1]
        sem = refs[-1]
        waits, at = [], 0
        for (group, _), target in zip(operands, targets):
            copies = []
            for _, source_index, target_index in group:
                source = refs[where[at]]
                copies.append(
                    pltpu.make_async_copy(
                        source if source_index is None else source.at[source_index],
                        target if target_index is None else target.at[target_index],
                        sem.at[at],
                    )
                )
                at += 1
            waits.append(copies)
        for copies in waits:
            for copy in copies:
                copy.start()

        def ready(n):
            for copy in waits[n]:
                copy.wait()
            return targets[n]

        body(ready, out_refs)

    return pl.pallas_call(
        kernel,
        out_shape=tuple(outs),
        in_specs=[ANY] * n_in,
        out_specs=(VMEM,) * n_outs,
        scratch_shapes=[pltpu.VMEM(shape, group[0][0].dtype) for group, shape in operands]
        + [pltpu.SemaphoreType.DMA((len(pieces),))],
        compiler_params=pltpu.CompilerParams(vmem_limit_bytes=VMEM_LIMIT),
        cost_estimate=pl.CostEstimate(
            flops=int(micros * 1.15e9), bytes_accessed=0, transcendentals=0
        ),
        name=name,
    )(*values, *after)


def whole(value):
    return [(value, None, None)], value.shape


def rows_of(values):
    pieces, row = [], 0
    for value in values:
        pieces.append((value, None, pl.ds(row, value.shape[0])))
        row += value.shape[0]
    return pieces, (row, values[0].shape[1])


def column(row):
    size = row.shape[1]
    across = lax.broadcasted_iota(jnp.int32, (size, size), 0)
    along = lax.broadcasted_iota(jnp.int32, (size, size), 1)
    return jnp.sum(jnp.where(across == along, row, jnp.zeros_like(row)), axis=1, keepdims=True)


def choosers(pos, slots):
    line = lax.broadcasted_iota(jnp.int32, (pos[0].shape[0], slots), 1)
    return [(place == line).astype(jnp.bfloat16) for place in pos]


def positions(capacity, ids):
    tokens = ids[0].shape[0]
    lanes = lax.broadcasted_iota(jnp.int32, (tokens, 128), 1)
    hot = [(ids[k] == lanes).astype(jnp.float32) for k in range(2)]
    later = lax.broadcasted_iota(jnp.int32, (tokens, tokens), 0)
    earlier = lax.broadcasted_iota(jnp.int32, (tokens, tokens), 1)
    lower = (later > earlier).astype(jnp.bfloat16)
    before = dot(lower, (hot[0] + hot[1]).astype(jnp.bfloat16))
    pos = []
    for k in range(2):
        slot = jnp.sum(hot[k] * before, axis=1, keepdims=True).astype(jnp.int32)
        pos.append(ids[k] * capacity + slot)
    return pos


def chunk_position(pos, capacity, first, count):
    expert = pos // capacity
    slot = pos - expert * capacity - first
    return jnp.where((slot >= 0) & (slot < count), expert * count + slot, -1)


def place_cots(capacity, first, ready, grad_at, gates, pos, out_ref):
    blocks, count, _ = out_ref.shape
    piece = count if blocks > 1 else capacity
    pick = choosers(
        [chunk_position(place, capacity, first, piece) for place in pos], blocks * count
    )
    grad = ready(grad_at)[...].astype(jnp.float32)
    placed = 0.0
    for k in range(2):
        placed = placed + dot(pick[k], (gates[k] * grad).astype(jnp.bfloat16), TN)
    out_ref[...] = placed.astype(jnp.bfloat16).reshape(out_ref.shape)


def slots_body(capacity, ready, outs):
    pos_ref, cot_ref = outs
    ids_ref = ready(0)
    pos = positions(capacity, [column(ids_ref[k : k + 1]) for k in range(2)])
    pair = lax.broadcasted_iota(jnp.int32, (pos[0].shape[0], 2), 1)
    pos_ref[...] = jnp.where(pair == 0, pos[0], pos[1])
    gates_ref = ready(1)
    gates = [column(gates_ref[k : k + 1]) for k in range(2)]
    place_cots(capacity, 0, ready, 2, gates, pos, cot_ref)


def late_slots_body(capacity, first, ready, outs):
    pos_ref, gates_ref = ready(0), ready(1)
    gates = [column(gates_ref[k : k + 1]) for k in range(2)]
    pos = [pos_ref[:, k : k + 1] for k in range(2)]
    place_cots(capacity, first, ready, 2, gates, pos, outs[0])


def attend_body(ready, outs):
    mixed_ref, normed_ref = outs
    query_ref, key_ref, value_ref = ready(0), ready(1), ready(2)
    parts = []
    for head in range(HEADS):
        cols = slice(head * HD, (head + 1) * HD)
        scores = dot(query_ref[:, cols], key_ref[:, cols], NT) * (HD ** (-0.5))
        weights = jnp.exp(scores - jnp.max(scores, axis=1, keepdims=True))
        total = jnp.sum(weights, axis=1, keepdims=True)
        accum = dot(weights.astype(jnp.bfloat16), value_ref[:, cols])
        parts.append((accum / total).astype(jnp.bfloat16))
    attended = jnp.concatenate(parts, axis=1)
    token_ref, proj_ref = ready(3), ready(4)
    mixed = token_ref[...].astype(jnp.float32) + dot(attended, proj_ref[...])
    mixed_ref[...] = mixed
    mean_square = jnp.mean(mixed * mixed, axis=1, keepdims=True)
    scale_ref, shift_ref = ready(5), ready(6)
    normed = mixed * lax.rsqrt(mean_square + 1e-06) * (1.0 + scale_ref[...]) + shift_ref[...]
    normed_ref[...] = normed.astype(jnp.bfloat16)


def place_body(capacity, firsts, ready, outs):
    pos_ref = ready(0)
    pos = [pos_ref[:, k : k + 1] for k in range(2)]
    normed = ready(1)[...]
    for first, out_ref in zip(firsts, outs):
        blocks, count, _ = out_ref.shape
        piece = count if blocks > 1 else capacity
        pick = choosers(
            [chunk_position(place, capacity, first, piece) for place in pos], blocks * count
        )
        placed = dot(pick[0] + pick[1], normed, TN).astype(jnp.bfloat16)
        out_ref[...] = placed.reshape(out_ref.shape)


def forward_body(ready, outs):
    keep_ref, send_ref, gate_pre_ref, up_pre_ref = outs
    row_ref = ready(0)
    rows = row_ref[...].reshape(-1, row_ref.shape[-1])
    gate_pre = dot(ready(1)[...], rows, NT)
    gate_pre_ref[...] = gate_pre
    up_pre = dot(ready(2)[...], rows, NT)
    up_pre_ref[...] = up_pre
    hidden = (gate_pre * jax.nn.sigmoid(gate_pre) * up_pre).astype(jnp.bfloat16)
    half = rows.shape[0] // 2
    partial = dot(hidden, ready(3)[...], TN).astype(jnp.bfloat16)
    keep_ref[...] = partial[:half]
    send_ref[...] = partial[half:]


def add_body(ready, outs):
    for n, out_ref in enumerate(outs):
        total = ready(2 * n)[...].astype(jnp.float32) + ready(2 * n + 1)[...].astype(jnp.float32)
        out_ref[...] = total.astype(jnp.bfloat16).reshape(out_ref.shape)


def finish_body(ready, outs):
    sent_ref = ready(3)
    size = outs[0].shape[0]
    for n, out_ref in enumerate(outs):
        total = ready(n)[...] + sent_ref[n * size : (n + 1) * size].astype(jnp.float32)
        out_ref[...] = total.astype(jnp.bfloat16)


def backward_body(ready, outs):
    kept, sent_ref = outs[:3], outs[3]
    cot_ref, down_ref = ready(0), ready(1)
    cots = cot_ref[...]
    hidden_grad = dot(down_ref[...], cots, NT)
    gate_pre = ready(2)[...]
    up_pre = ready(3)[...]
    sigmoid = jax.nn.sigmoid(gate_pre)
    active = gate_pre * sigmoid
    gate_cot = hidden_grad * up_pre * sigmoid * (1.0 + gate_pre * (1.0 - sigmoid))
    up_cot = hidden_grad * active
    half = kept[0].shape[0]
    both = jnp.concatenate([gate_cot.astype(jnp.bfloat16), up_cot.astype(jnp.bfloat16)], axis=0)
    grads = dot(both, ready(4)[...])
    for n in range(2):
        kept[n][...] = grads[2 * n * half : (2 * n + 1) * half]
        sent = grads[(2 * n + 1) * half : (2 * n + 2) * half].astype(jnp.bfloat16)
        sent_ref[n * half : (n + 1) * half] = sent
    grads = dot((active * up_pre).astype(jnp.bfloat16), cots)
    kept[2][...] = grads[:half]
    sent_ref[2 * half :] = grads[half:].astype(jnp.bfloat16)


def pack_body(ready, outs):
    size = outs[0].shape[0] // 3
    for n in range(3):
        outs[0][n * size : (n + 1) * size] = ready(n)[...]


def combine_body(ready, outs):
    pos_ref, gates_ref = ready(0), ready(1)
    row_ref = ready(2)
    rows = row_ref[...].reshape(-1, row_ref.shape[-1])
    pick = choosers([pos_ref[:, 0:1], pos_ref[:, 1:2]], rows.shape[0])
    picked = dot(jnp.concatenate(pick, axis=0), rows)
    total = ready(3)[...]
    tokens = total.shape[0]
    for k in range(2):
        total = total + column(gates_ref[k : k + 1]) * picked[k * tokens : (k + 1) * tokens]
    outs[0][...] = total.astype(jnp.bfloat16)


def per_device(
    tokens,
    queries,
    keys,
    values,
    out_proj,
    mod_scale,
    mod_shift,
    expert_ids,
    gates,
    w_gate,
    w_up,
    w_down,
    out_grad,
):
    n_ctx = lax.axis_size("ctx")
    experts = n_ctx * lax.axis_size("group")
    local = tokens.shape[1]
    width = tokens.shape[2]
    hidden = w_gate.shape[0]
    capacity = 3 * local // experts
    slots = experts * capacity
    if capacity % PIECE == 0 and capacity > PIECE:
        blocks, height = experts, capacity
        row_cuts = [(0, capacity - PIECE), (capacity - PIECE, PIECE)]
        cot_cuts = [(0, PIECE), (PIECE, capacity - PIECE)]
    else:
        blocks, height = 1, slots
        row_cuts = cot_cuts = [(0, slots)]

    def swapped(value, axis):
        return lax.ppermute(value, axis, [(n, n ^ 1) for n in range(lax.axis_size(axis))])

    def exchanged(value):
        shaped = value if blocks > 1 else value.reshape(experts, capacity, width)
        moved = lax.all_to_all(shaped, ("ctx", "group"), split_axis=0, concat_axis=0, tiled=True)
        return moved.reshape(value.shape)

    def turned(value, step):
        size = lax.axis_size("ctx")
        return lax.ppermute(value, "ctx", [(n, (n + step) % size) for n in range(size)])

    def chunk_shapes(cuts):
        return [shape_of(blocks, count, width) for _, count in cuts]

    key_pieces = [keys[0]] + [turned(keys[0], step) for step in range(1, n_ctx)]
    value_pieces = [values[0]] + [turned(values[0], step) for step in range(1, n_ctx)]

    ids_rows = jnp.transpose(expert_ids[0])
    gate_rows = jnp.transpose(gates[0])
    pos, first_cots = call(
        functools.partial(slots_body, capacity),
        "slots",
        [whole(ids_rows), whole(gate_rows), whole(out_grad[0])],
        [shape_of(local, 2, dtype=jnp.int32)] + chunk_shapes(cot_cuts[:1]),
        3,
    )
    cots = [exchanged(first_cots)]
    cots_across = [swapped(cots[0], "side")]

    (packed,) = call(
        pack_body,
        "pack",
        [whole(w_gate), whole(w_up), whole(w_down)],
        [shape_of(3 * hidden, width)],
        3,
    )
    other_weights = swapped(packed, "core")

    mixed, normed = call(
        attend_body,
        "attend",
        [
            whole(queries[0]),
            rows_of(key_pieces),
            rows_of(value_pieces),
            whole(tokens[0]),
            whole(out_proj),
            whole(mod_scale),
            whole(mod_shift),
        ],
        [shape_of(local, width, dtype=jnp.float32), shape_of(local, width)],
        60,
    )
    placed = call(
        functools.partial(place_body, capacity, [first for first, _ in row_cuts]),
        "place",
        [whole(pos), whole(normed)],
        chunk_shapes(row_cuts),
        3,
        after=cots + [other_weights],
    )
    rows = [exchanged(value) for value in placed]
    rows_across = [swapped(value, "side") for value in rows]

    for first, count in cot_cuts[1:]:
        (late_cots,) = call(
            functools.partial(late_slots_body, capacity, first),
            "late_slots",
            [whole(pos), whole(gate_rows), whole(out_grad[0])],
            [shape_of(blocks, count, width)],
            3,
            after=rows + cots_across[:1],
        )
        cots.append(exchanged(late_cots))
        cots_across.append(swapped(cots[-1], "side"))

    pairs = []
    for n, weight in enumerate((w_gate, w_up, w_down)):
        second = (other_weights, pl.ds(n * hidden, hidden), pl.ds(hidden, hidden))
        pairs.append(([(weight, None, pl.ds(0, hidden)), second], (2 * hidden, width)))
    gate_pres, up_pres, partials = [], [], []
    after = []
    for (_, count), own, across in zip(row_cuts, rows, rows_across):
        half = blocks * count
        pre = shape_of(2 * hidden, 2 * half, dtype=jnp.float32)
        keep, send, gate_pre, up_pre = call(
            forward_body,
            "forward",
            [([(own, None, 0), (across, None, 1)], (2,) + own.shape)]
            + pairs,
            [shape_of(half, width)] * 2 + [pre] * 2,
            7,
            after=after,
        )
        after = [keep]
        gate_pres.append(gate_pre)
        up_pres.append(up_pre)
        partials.append((keep, swapped(send, "side"), count))

    def summed(keep, other, count, after):
        (sums,) = call(
            add_body,
            "add",
            [whole(keep), whole(other)],
            [shape_of(blocks, count, width)],
            2,
            after=after,
        )
        return sums

    totals = [summed(*partial, []) for partial in partials[:-1]]

    total_rows = 2 * slots
    row_pieces, cot_pieces, pre_pieces, line = [], [], [[], []], 0
    for n, (first, count) in enumerate(row_cuts):
        for side, both in enumerate(((rows, cots), (rows_across, cots_across))):
            for block in range(blocks):
                start = line + (side * blocks + block) * count
                row_pieces.append((both[0][n], block, pl.ds(start, count)))
                for (cot_first, cot_count), value in zip(cot_cuts, both[1]):
                    low = max(first, cot_first)
                    high = min(first + count, cot_first + cot_count)
                    if low < high:
                        source = (block, pl.ds(low - cot_first, high - low))
                        cot_pieces.append((value, source, pl.ds(start + low - first, high - low)))
        for pieces, pres in zip(pre_pieces, (gate_pres, up_pres)):
            target = (slice(None), pl.ds(line, 2 * blocks * count))
            pieces.append((pres[n], None, target))
        line += 2 * blocks * count
    *kept, sent = call(
        backward_body,
        "backward",
        [
            (cot_pieces, (total_rows, width)),
            pairs[2],
            (pre_pieces[0], (2 * hidden, total_rows)),
            (pre_pieces[1], (2 * hidden, total_rows)),
            (row_pieces, (total_rows, width)),
        ],
        [shape_of(hidden, width, dtype=jnp.float32)] * 3 + [shape_of(3 * hidden, width)],
        40,
        after=totals,
    )
    totals.append(summed(*partials[-1], kept[:1] if totals else []))
    returned = [exchanged(total) for total in totals]
    grad_gate, grad_up, grad_down = call(
        finish_body,
        "finish",
        [whole(value) for value in kept] + [whole(swapped(sent, "core"))],
        [shape_of(hidden, width)] * 3,
        5,
    )

    returned_pieces = []
    for (first, count), value in zip(row_cuts, returned):
        returned_pieces.append((value, None, (slice(None), pl.ds(first, count))))
    (layer_out,) = call(
        combine_body,
        "combine",
        [
            whole(pos),
            whole(gate_rows),
            (returned_pieces, (blocks, height, width)),
            whole(mixed),
        ],
        [shape_of(local, width)],
        3,
        after=[grad_gate],
    )
    return (layer_out[None], grad_gate, grad_up, grad_down)


def solution(mesh):
    n_ctx = mesh.shape["ctx"]
    cut = (n_ctx, mesh.shape["exp"] // SHARDS, SHARDS // 2, 2)
    mesh = jax.sharding.Mesh(mesh.devices.reshape(cut), ("ctx",) + EXP)
    rows = P(EXP, "ctx", None)
    weight = P(("ctx",) + EXP, None)
    return jax.shard_map(
        per_device,
        mesh=mesh,
        in_specs=(rows, rows, rows, rows, P(), P(EXP, None), P(EXP, None), rows, rows)
        + (weight, weight, weight, rows),
        out_specs=(rows, weight, weight, weight),
        check_vma=False,
    )
```

```python
import functools

import jax
import jax.numpy as jnp
from jax import lax
from jax.experimental import pallas as pl
from jax.experimental.pallas import tpu as pltpu
from jax.sharding import PartitionSpec as P

HEADS = 8
HD = 128
SHARDS = 4
PIECE = 16
VMEM_LIMIT = 63 * 1024 * 1024
EXP = ("group", "side", "core")

NT = (((1,), (1,)), ((), ()))
TN = (((0,), (0,)), ((), ()))

VMEM = pl.BlockSpec(memory_space=pltpu.VMEM)
ANY = pl.BlockSpec(memory_space=pl.ANY)


def dot(a, b, dims=(((1,), (0,)), ((), ()))):
    return lax.dot_general(a, b, dims, preferred_element_type=jnp.float32)


def shape_of(*shape, dtype=jnp.bfloat16):
    return jax.ShapeDtypeStruct(shape, dtype)


def call(body, name, operands, outs, micros=1, after=()):
    pieces = [piece for group, _ in operands for piece in group]
    values = []
    for value, _, _ in pieces:
        if not any(value is known for known in values):
            values.append(value)
    where = [[value is known for known in values].index(True) for value, _, _ in pieces]
    n_in, n_outs = len(values) + len(after), len(outs)

    def kernel(*refs):
        out_refs = refs[n_in : n_in + n_outs]
        targets = refs[n_in + n_outs : -1]
        sem = refs[-1]
        waits, at = [], 0
        for (group, _), target in zip(operands, targets):
            copies = []
            for _, source_index, target_index in group:
                source = refs[where[at]]
                if callable(target_index):
                    target_index = target_index()
                copies.append(
                    pltpu.make_async_copy(
                        source if source_index is None else source.at[source_index],
                        target if target_index is None else target.at[target_index],
                        sem.at[at],
                    )
                )
                at += 1
            waits.append(copies)
        for copies in waits:
            for copy in copies:
                copy.start()

        def ready(n):
            for copy in waits[n]:
                copy.wait()
            return targets[n]

        body(ready, out_refs)

    return pl.pallas_call(
        kernel,
        out_shape=tuple(outs),
        in_specs=[ANY] * n_in,
        out_specs=(VMEM,) * n_outs,
        scratch_shapes=[pltpu.VMEM(shape, group[0][0].dtype) for group, shape in operands]
        + [pltpu.SemaphoreType.DMA((len(pieces),))],
        compiler_params=pltpu.CompilerParams(vmem_limit_bytes=VMEM_LIMIT),
        cost_estimate=pl.CostEstimate(
            flops=int(micros * 1.15e9), bytes_accessed=0, transcendentals=0
        ),
        name=name,
    )(*values, *after)


def whole(value):
    return [(value, None, None)], value.shape


def rows_of(values):
    pieces, row = [], 0
    for value in values:
        pieces.append((value, None, pl.ds(row, value.shape[0])))
        row += value.shape[0]
    return pieces, (row, values[0].shape[1])


def column(row):
    size = row.shape[1]
    across = lax.broadcasted_iota(jnp.int32, (size, size), 0)
    along = lax.broadcasted_iota(jnp.int32, (size, size), 1)
    return jnp.sum(jnp.where(across == along, row, jnp.zeros_like(row)), axis=1, keepdims=True)


def choosers(pos, slots):
    line = lax.broadcasted_iota(jnp.int32, (pos[0].shape[0], slots), 1)
    return [(place == line).astype(jnp.bfloat16) for place in pos]


def earlier_count(hot):
    tokens = hot.shape[0]
    later = lax.broadcasted_iota(jnp.int32, (tokens, tokens), 0)
    earlier = lax.broadcasted_iota(jnp.int32, (tokens, tokens), 1)
    return dot((later > earlier).astype(jnp.bfloat16), hot.astype(jnp.bfloat16))


def select_body(n_ctx, groups, capacity, ready, outs):
    info_ref = ready(0)
    me_ctx, me_group = lax.axis_index("ctx"), lax.axis_index("group")
    shift = groups.bit_length() - 1
    picks = [[] for _ in range(n_ctx)]
    gates = [[] for _ in range(n_ctx)]
    for source in range(groups):
        info = [column(info_ref[source, k : k + 1]) for k in range(4)]
        ids = [info[k].astype(jnp.int32) for k in range(2)]
        tokens = ids[0].shape[0]
        lanes = lax.broadcasted_iota(jnp.int32, (tokens, 128), 1)
        expert = (((me_ctx + lanes) & (n_ctx - 1)) << shift) + me_group
        hot = [((ids[k] == expert) & (lanes < n_ctx)).astype(jnp.float32) for k in range(2)]
        named = hot[0] + hot[1]
        before = earlier_count(named)
        gate = hot[0] * info[2] + hot[1] * info[3]
        line = lax.broadcasted_iota(jnp.int32, (tokens, groups * capacity), 1)
        start = source * capacity
        for step in range(n_ctx):
            place = before[:, step : step + 1].astype(jnp.int32) + start
            place = jnp.where(named[:, step : step + 1] > 0.0, place, -1)
            picks[step].append((place == line).astype(jnp.bfloat16))
            gates[step].append(gate[:, step : step + 1])
    rows = ready(1)[...]
    grads = rows.astype(jnp.float32)
    for step, out_ref in enumerate(outs):
        scaled = (jnp.concatenate(gates[step], axis=0) * grads).astype(jnp.bfloat16)
        placed = dot(jnp.concatenate(picks[step], axis=0), scaled, TN)
        out_ref[...] = placed.astype(jnp.bfloat16)


def chunk_position(pos, capacity, first, count):
    expert = pos // capacity
    slot = pos - expert * capacity - first
    return jnp.where((slot >= 0) & (slot < count), expert * count + slot, -1)


def begin_body(capacity, ready, outs):
    pos_ref, packed_ref = outs
    info_ref = ready(0)
    ids = [column(info_ref[k : k + 1]).astype(jnp.int32) for k in range(2)]
    lanes = lax.broadcasted_iota(jnp.int32, (ids[0].shape[0], 128), 1)
    hot = [(ids[k] == lanes).astype(jnp.float32) for k in range(2)]
    before = earlier_count(hot[0] + hot[1])
    pos = []
    for k in range(2):
        slot = jnp.sum(hot[k] * before, axis=1, keepdims=True).astype(jnp.int32)
        pos.append(ids[k] * capacity + slot)
    pair = lax.broadcasted_iota(jnp.int32, (pos[0].shape[0], 2), 1)
    pos_ref[...] = jnp.where(pair == 0, pos[0], pos[1])
    size = packed_ref.shape[0] // 3
    for n in range(3):
        packed_ref[n * size : (n + 1) * size] = ready(1 + n)[...]


def attend_body(capacity, firsts, ready, outs):
    mixed_ref, *chunk_refs = outs
    query_ref, key_ref, value_ref = ready(0), ready(1), ready(2)
    parts = []
    for head in range(HEADS):
        cols = slice(head * HD, (head + 1) * HD)
        scores = dot(query_ref[:, cols], key_ref[:, cols], NT) * (HD ** (-0.5))
        weights = jnp.exp(scores - jnp.max(scores, axis=1, keepdims=True))
        total = jnp.sum(weights, axis=1, keepdims=True)
        accum = dot(weights.astype(jnp.bfloat16), value_ref[:, cols])
        parts.append((accum / total).astype(jnp.bfloat16))
    attended = jnp.concatenate(parts, axis=1)
    token_ref, proj_ref = ready(3), ready(4)
    mixed = token_ref[...].astype(jnp.float32) + dot(attended, proj_ref[...])
    mixed_ref[...] = mixed
    mean_square = jnp.mean(mixed * mixed, axis=1, keepdims=True)
    scale_ref, shift_ref = ready(5), ready(6)
    normed = mixed * lax.rsqrt(mean_square + 1e-06) * (1.0 + scale_ref[...]) + shift_ref[...]
    normed = normed.astype(jnp.bfloat16)
    pos_ref = ready(7)
    pos = [pos_ref[:, k : k + 1] for k in range(2)]
    for first, out_ref in zip(firsts, chunk_refs):
        blocks, count, _ = out_ref.shape
        piece = count if blocks > 1 else capacity
        pick = choosers(
            [chunk_position(place, capacity, first, piece) for place in pos], blocks * count
        )
        placed = dot(pick[0] + pick[1], normed, TN).astype(jnp.bfloat16)
        out_ref[...] = placed.reshape(out_ref.shape)


def forward_body(ready, outs):
    keep_ref, send_ref, gate_pre_ref, up_pre_ref = outs
    row_ref = ready(0)
    rows = row_ref[...].reshape(-1, row_ref.shape[-1])
    gate_pre = dot(ready(1)[...], rows, NT)
    gate_pre_ref[...] = gate_pre
    up_pre = dot(ready(2)[...], rows, NT)
    up_pre_ref[...] = up_pre
    hidden = (gate_pre * jax.nn.sigmoid(gate_pre) * up_pre).astype(jnp.bfloat16)
    half = rows.shape[0] // 2
    partial = dot(hidden, ready(3)[...], TN).astype(jnp.bfloat16)
    keep_ref[...] = partial[:half]
    send_ref[...] = partial[half:]


def add_body(ready, outs):
    for n, out_ref in enumerate(outs):
        total = ready(2 * n)[...].astype(jnp.float32) + ready(2 * n + 1)[...].astype(jnp.float32)
        out_ref[...] = total.astype(jnp.bfloat16).reshape(out_ref.shape)


def finish_body(ready, outs):
    sent_ref = ready(3)
    size = outs[0].shape[0]
    for n, out_ref in enumerate(outs):
        total = ready(n)[...] + sent_ref[n * size : (n + 1) * size].astype(jnp.float32)
        out_ref[...] = total.astype(jnp.bfloat16)


def backward_body(ready, outs):
    kept, sent_ref = outs[:3], outs[3]
    cot_ref, down_ref = ready(0), ready(1)
    cots = cot_ref[...]
    hidden_grad = dot(down_ref[...], cots, NT)
    gate_pre = ready(2)[...]
    up_pre = ready(3)[...]
    sigmoid = jax.nn.sigmoid(gate_pre)
    active = gate_pre * sigmoid
    gate_cot = hidden_grad * up_pre * sigmoid * (1.0 + gate_pre * (1.0 - sigmoid))
    up_cot = hidden_grad * active
    half = kept[0].shape[0]
    both = jnp.concatenate([gate_cot.astype(jnp.bfloat16), up_cot.astype(jnp.bfloat16)], axis=0)
    grads = dot(both, ready(4)[...])
    for n in range(2):
        kept[n][...] = grads[2 * n * half : (2 * n + 1) * half]
        sent = grads[(2 * n + 1) * half : (2 * n + 2) * half].astype(jnp.bfloat16)
        sent_ref[n * half : (n + 1) * half] = sent
    grads = dot((active * up_pre).astype(jnp.bfloat16), cots)
    kept[2][...] = grads[:half]
    sent_ref[2 * half :] = grads[half:].astype(jnp.bfloat16)


def combine_body(ready, outs):
    pos_ref, gates_ref = ready(0), ready(1)
    row_ref = ready(2)
    rows = row_ref[...].reshape(-1, row_ref.shape[-1])
    pick = choosers([pos_ref[:, 0:1], pos_ref[:, 1:2]], rows.shape[0])
    picked = dot(jnp.concatenate(pick, axis=0), rows)
    total = ready(3)[...]
    tokens = total.shape[0]
    for k in range(2):
        total = total + column(gates_ref[k : k + 1]) * picked[k * tokens : (k + 1) * tokens]
    outs[0][...] = total.astype(jnp.bfloat16)


def per_device(
    tokens,
    queries,
    keys,
    values,
    out_proj,
    mod_scale,
    mod_shift,
    expert_ids,
    gates,
    w_gate,
    w_up,
    w_down,
    out_grad,
):
    n_ctx = lax.axis_size("ctx")
    groups = lax.axis_size("group")
    experts = n_ctx * groups
    local = tokens.shape[1]
    width = tokens.shape[2]
    hidden = w_gate.shape[0]
    capacity = 3 * local // experts
    slots = experts * capacity
    if capacity % PIECE == 0 and capacity > PIECE:
        blocks, height = experts, capacity
        row_cuts = [(0, capacity - PIECE), (capacity - PIECE, PIECE)]
    else:
        blocks, height = 1, slots
        row_cuts = [(0, slots)]

    def swapped(value, axis):
        return lax.ppermute(value, axis, [(n, n ^ 1) for n in range(lax.axis_size(axis))])

    def exchanged(value):
        shaped = value if blocks > 1 else value.reshape(experts, capacity, width)
        moved = lax.all_to_all(shaped, ("ctx", "group"), split_axis=0, concat_axis=0, tiled=True)
        return moved.reshape(value.shape)

    def turned(value, step):
        size = lax.axis_size("ctx")
        return lax.ppermute(value, "ctx", [(n, (n + step) % size) for n in range(size)])

    def chunk_shapes(cuts):
        return [shape_of(blocks, count, width) for _, count in cuts]

    key_pieces = [keys[0]] + [turned(keys[0], step) for step in range(1, n_ctx)]
    value_pieces = [values[0]] + [turned(values[0], step) for step in range(1, n_ctx)]

    gate_rows = jnp.transpose(gates[0])
    info = jnp.concatenate(
        [jnp.transpose(expert_ids[0]).astype(jnp.float32), gate_rows, jnp.zeros((4, local))]
    )
    all_grads = lax.all_gather(out_grad[0], "group", tiled=True)
    infos = lax.all_gather(info, "group")
    pos, packed = call(
        functools.partial(begin_body, capacity),
        "begin",
        [whole(info), whole(w_gate), whole(w_up), whole(w_down)],
        [shape_of(local, 2, dtype=jnp.int32), shape_of(3 * hidden, width)],
        4,
    )
    other_weights = swapped(packed, "core")

    mixed, *placed = call(
        functools.partial(attend_body, capacity, [first for first, _ in row_cuts]),
        "attend",
        [
            whole(queries[0]),
            rows_of(key_pieces),
            rows_of(value_pieces),
            whole(tokens[0]),
            whole(out_proj),
            whole(mod_scale),
            whole(mod_shift),
            whole(pos),
        ],
        [shape_of(local, width, dtype=jnp.float32)] + chunk_shapes(row_cuts),
        7,
    )
    rows = [exchanged(value) for value in placed]
    rows_across = [swapped(value, "side") for value in rows]

    picked = call(
        functools.partial(select_body, n_ctx, groups, capacity),
        "select",
        [whole(infos), whole(all_grads)],
        [shape_of(groups * capacity, width)] * n_ctx,
        4,
    )
    cots = [picked[0]] + [turned(value, step) for step, value in enumerate(picked) if step]
    cots_across = [swapped(value, "side") for value in cots]

    pairs = []
    for n, weight in enumerate((w_gate, w_up, w_down)):
        second = (other_weights, pl.ds(n * hidden, hidden), pl.ds(hidden, hidden))
        pairs.append(([(weight, None, pl.ds(0, hidden)), second], (2 * hidden, width)))
    gate_pres, up_pres, partials = [], [], []
    after = []
    for (_, count), own, across in zip(row_cuts, rows, rows_across):
        half = blocks * count
        pre = shape_of(2 * hidden, 2 * half, dtype=jnp.float32)
        keep, send, gate_pre, up_pre = call(
            forward_body,
            "forward",
            [([(own, None, 0), (across, None, 1)], (2,) + own.shape)]
            + pairs,
            [shape_of(half, width)] * 2 + [pre] * 2,
            7,
            after=after,
        )
        after = [keep]
        gate_pres.append(gate_pre)
        up_pres.append(up_pre)
        partials.append((keep, swapped(send, "side"), count))

    def summed(keep, other, count):
        (sums,) = call(
            add_body,
            "add",
            [whole(keep), whole(other)],
            [shape_of(blocks, count, width)],
            2,
        )
        return sums

    totals = [summed(*partial) for partial in partials]

    total_rows = 2 * slots
    row_pieces, cot_pieces, pre_pieces, line = [], [], [[], []], 0

    def cot_target(start, size, stride, step):
        ctx = (lax.axis_index("ctx") - step) & (n_ctx - 1)
        return pl.ds(pl.multiple_of(start + ctx * stride, 16), size)

    for n, (first, count) in enumerate(row_cuts):
        for side, (own, other) in enumerate(((rows, cots), (rows_across, cots_across))):
            start = line + side * blocks * count
            for block in range(blocks):
                row_pieces.append((own[n], block, pl.ds(start + block * count, count)))
            for step, value in enumerate(other):
                if blocks == 1:
                    size = groups * capacity
                    target = functools.partial(cot_target, start, size, size, step)
                    cot_pieces.append((value, None, target))
                    continue
                for group in range(groups):
                    target = functools.partial(
                        cot_target, start + group * count, count, groups * count, step
                    )
                    source = pl.ds(group * capacity + first, count)
                    cot_pieces.append((value, source, target))
        for pieces, pres in zip(pre_pieces, (gate_pres, up_pres)):
            target = (slice(None), pl.ds(line, 2 * blocks * count))
            pieces.append((pres[n], None, target))
        line += 2 * blocks * count
    *kept, sent = call(
        backward_body,
        "backward",
        [
            (cot_pieces, (total_rows, width)),
            pairs[2],
            (pre_pieces[0], (2 * hidden, total_rows)),
            (pre_pieces[1], (2 * hidden, total_rows)),
            (row_pieces, (total_rows, width)),
        ],
        [shape_of(hidden, width, dtype=jnp.float32)] * 3 + [shape_of(3 * hidden, width)],
        15,
    )
    returned = [exchanged(total) for total in totals]
    grad_gate, grad_up, grad_down = call(
        finish_body,
        "finish",
        [whole(value) for value in kept] + [whole(swapped(sent, "core"))],
        [shape_of(hidden, width)] * 3,
        5,
    )

    returned_pieces = []
    for (first, count), value in zip(row_cuts, returned):
        returned_pieces.append((value, None, (slice(None), pl.ds(first, count))))
    (layer_out,) = call(
        combine_body,
        "combine",
        [
            whole(pos),
            whole(gate_rows),
            (returned_pieces, (blocks, height, width)),
            whole(mixed),
        ],
        [shape_of(local, width)],
        3,
        after=[grad_gate],
    )
    return (layer_out[None], grad_gate, grad_up, grad_down)


def solution(mesh):
    n_ctx = mesh.shape["ctx"]
    cut = (n_ctx, mesh.shape["exp"] // SHARDS, SHARDS // 2, 2)
    mesh = jax.sharding.Mesh(mesh.devices.reshape(cut), ("ctx",) + EXP)
    rows = P(EXP, "ctx", None)
    weight = P(("ctx",) + EXP, None)
    return jax.shard_map(
        per_device,
        mesh=mesh,
        in_specs=(rows, rows, rows, rows, P(), P(EXP, None), P(EXP, None), rows, rows)
        + (weight, weight, weight, rows),
        out_specs=(rows, weight, weight, weight),
        check_vma=False,
    )
```

```python
import functools

import jax
import jax.numpy as jnp
from jax import lax
from jax.experimental import pallas as pl
from jax.experimental.pallas import tpu as pltpu
from jax.sharding import PartitionSpec as P

HEADS = 8
HD = 128
SHARDS = 4
PIECE = 16
VMEM_LIMIT = 63 * 1024 * 1024
EXP = ("group", "side", "core")

NT = (((1,), (1,)), ((), ()))
TN = (((0,), (0,)), ((), ()))

VMEM = pl.BlockSpec(memory_space=pltpu.VMEM)
ANY = pl.BlockSpec(memory_space=pl.ANY)


def dot(a, b, dims=(((1,), (0,)), ((), ()))):
    return lax.dot_general(a, b, dims, preferred_element_type=jnp.float32)


def shape_of(*shape, dtype=jnp.bfloat16):
    return jax.ShapeDtypeStruct(shape, dtype)


def call(body, name, operands, outs, micros=1, after=()):
    pieces = [piece for group, _ in operands for piece in group]
    values = []
    for value, _, _ in pieces:
        if not any(value is known for known in values):
            values.append(value)
    where = [[value is known for known in values].index(True) for value, _, _ in pieces]
    n_in, n_outs = len(values) + len(after), len(outs)

    def kernel(*refs):
        out_refs = refs[n_in : n_in + n_outs]
        targets = refs[n_in + n_outs : -1]
        sem = refs[-1]
        waits, at = [], 0
        for (group, _), target in zip(operands, targets):
            copies = []
            for _, source_index, target_index in group:
                source = refs[where[at]]
                if callable(target_index):
                    target_index = target_index()
                copies.append(
                    pltpu.make_async_copy(
                        source if source_index is None else source.at[source_index],
                        target if target_index is None else target.at[target_index],
                        sem.at[at],
                    )
                )
                at += 1
            waits.append(copies)
        for copies in waits:
            for copy in copies:
                copy.start()

        def ready(n):
            for copy in waits[n]:
                copy.wait()
            return targets[n]

        body(ready, out_refs)

    return pl.pallas_call(
        kernel,
        out_shape=tuple(outs),
        in_specs=[ANY] * n_in,
        out_specs=(VMEM,) * n_outs,
        scratch_shapes=[pltpu.VMEM(shape, group[0][0].dtype) for group, shape in operands]
        + [pltpu.SemaphoreType.DMA((len(pieces),))],
        compiler_params=pltpu.CompilerParams(vmem_limit_bytes=VMEM_LIMIT),
        cost_estimate=pl.CostEstimate(
            flops=int(micros * 1.15e9), bytes_accessed=0, transcendentals=0
        ),
        name=name,
    )(*values, *after)


def whole(value):
    return [(value, None, None)], value.shape


def rows_of(values):
    pieces, row = [], 0
    for value in values:
        pieces.append((value, None, pl.ds(row, value.shape[0])))
        row += value.shape[0]
    return pieces, (row, values[0].shape[1])


def column(row):
    size = row.shape[1]
    across = lax.broadcasted_iota(jnp.int32, (size, size), 0)
    along = lax.broadcasted_iota(jnp.int32, (size, size), 1)
    return jnp.sum(jnp.where(across == along, row, jnp.zeros_like(row)), axis=1, keepdims=True)


def choosers(pos, slots):
    line = lax.broadcasted_iota(jnp.int32, (pos[0].shape[0], slots), 1)
    return [(place == line).astype(jnp.bfloat16) for place in pos]


def earlier_count(hot):
    tokens = hot.shape[0]
    later = lax.broadcasted_iota(jnp.int32, (tokens, tokens), 0)
    earlier = lax.broadcasted_iota(jnp.int32, (tokens, tokens), 1)
    return dot((later > earlier).astype(jnp.bfloat16), hot.astype(jnp.bfloat16))


def select_body(n_ctx, groups, capacity, ready, outs):
    wide_ref = ready(0)
    width = outs[0].shape[1]
    me_ctx, me_group = lax.axis_index("ctx"), lax.axis_index("group")
    shift = groups.bit_length() - 1
    picks = [[] for _ in range(n_ctx)]
    gates = [[] for _ in range(n_ctx)]
    for source in range(groups):
        tokens = wide_ref.shape[0] // groups
        extra = wide_ref[source * tokens : (source + 1) * tokens, width:].astype(jnp.float32)
        info = [extra[:, n : n + 1] for n in range(8)]
        ids = [info[k].astype(jnp.int32) for k in range(2)]
        both = [info[n] + info[n + 1] + info[n + 2] for n in (2, 5)]
        lanes = lax.broadcasted_iota(jnp.int32, (tokens, 128), 1)
        expert = (((me_ctx + lanes) & (n_ctx - 1)) << shift) + me_group
        hot = [((ids[k] == expert) & (lanes < n_ctx)).astype(jnp.float32) for k in range(2)]
        named = hot[0] + hot[1]
        before = earlier_count(named)
        gate = hot[0] * both[0] + hot[1] * both[1]
        line = lax.broadcasted_iota(jnp.int32, (tokens, groups * capacity), 1)
        start = source * capacity
        for step in range(n_ctx):
            place = before[:, step : step + 1].astype(jnp.int32) + start
            place = jnp.where(named[:, step : step + 1] > 0.0, place, -1)
            picks[step].append((place == line).astype(jnp.bfloat16))
            gates[step].append(gate[:, step : step + 1])
    grads = wide_ref[:, :width].astype(jnp.float32)
    for step, out_ref in enumerate(outs):
        scaled = (jnp.concatenate(gates[step], axis=0) * grads).astype(jnp.bfloat16)
        placed = dot(jnp.concatenate(picks[step], axis=0), scaled, TN)
        out_ref[...] = placed.astype(jnp.bfloat16)


def chunk_position(pos, capacity, first, count):
    expert = pos // capacity
    slot = pos - expert * capacity - first
    return jnp.where((slot >= 0) & (slot < count), expert * count + slot, -1)


def begin_body(capacity, ready, outs):
    pos_ref, wide_ref = outs
    ids_ref, gates_ref = ready(0), ready(1)
    ids = [column(ids_ref[k : k + 1]) for k in range(2)]
    tokens = ids[0].shape[0]
    lanes = lax.broadcasted_iota(jnp.int32, (tokens, 128), 1)
    hot = [(ids[k] == lanes).astype(jnp.float32) for k in range(2)]
    before = earlier_count(hot[0] + hot[1])
    pos, values = [], [ids[k].astype(jnp.float32) for k in range(2)]
    for k in range(2):
        slot = jnp.sum(hot[k] * before, axis=1, keepdims=True).astype(jnp.int32)
        pos.append(ids[k] * capacity + slot)
        left = column(gates_ref[k : k + 1])
        for _ in range(3):
            values.append(left.astype(jnp.bfloat16).astype(jnp.float32))
            left = left - values[-1]
    pair = lax.broadcasted_iota(jnp.int32, (tokens, 2), 1)
    pos_ref[...] = jnp.where(pair == 0, pos[0], pos[1])
    extra = jnp.zeros((tokens, 128), jnp.float32)
    for n, value in enumerate(values):
        extra = jnp.where(lanes == n, value, extra)
    width = wide_ref.shape[1] - 128
    wide_ref[:, width:] = extra.astype(jnp.bfloat16)
    wide_ref[:, :width] = ready(2)[...]


def pack_body(ready, outs):
    size = outs[0].shape[0] // 3
    for n in range(3):
        outs[0][n * size : (n + 1) * size] = ready(n)[...]


def attend_body(capacity, firsts, ready, outs):
    mixed_ref, *chunk_refs = outs
    query_ref, key_ref, value_ref = ready(0), ready(1), ready(2)
    parts = []
    for head in range(HEADS):
        cols = slice(head * HD, (head + 1) * HD)
        scores = dot(query_ref[:, cols], key_ref[:, cols], NT) * (HD ** (-0.5))
        weights = jnp.exp(scores - jnp.max(scores, axis=1, keepdims=True))
        total = jnp.sum(weights, axis=1, keepdims=True)
        accum = dot(weights.astype(jnp.bfloat16), value_ref[:, cols])
        parts.append((accum / total).astype(jnp.bfloat16))
    attended = jnp.concatenate(parts, axis=1)
    token_ref, proj_ref = ready(3), ready(4)
    mixed = token_ref[...].astype(jnp.float32) + dot(attended, proj_ref[...])
    mixed_ref[...] = mixed
    mean_square = jnp.mean(mixed * mixed, axis=1, keepdims=True)
    scale_ref, shift_ref = ready(5), ready(6)
    normed = mixed * lax.rsqrt(mean_square + 1e-06) * (1.0 + scale_ref[...]) + shift_ref[...]
    normed = normed.astype(jnp.bfloat16)
    pos_ref = ready(7)
    pos = [pos_ref[:, k : k + 1] for k in range(2)]
    for first, out_ref in zip(firsts, chunk_refs):
        blocks, count, _ = out_ref.shape
        piece = count if blocks > 1 else capacity
        pick = choosers(
            [chunk_position(place, capacity, first, piece) for place in pos], blocks * count
        )
        placed = dot(pick[0] + pick[1], normed, TN).astype(jnp.bfloat16)
        out_ref[...] = placed.reshape(out_ref.shape)


def forward_body(ready, outs):
    keep_ref, send_ref, gate_pre_ref, up_pre_ref = outs
    row_ref = ready(0)
    rows = row_ref[...].reshape(-1, row_ref.shape[-1])
    gate_pre = dot(ready(1)[...], rows, NT)
    gate_pre_ref[...] = gate_pre
    up_pre = dot(ready(2)[...], rows, NT)
    up_pre_ref[...] = up_pre
    hidden = (gate_pre * jax.nn.sigmoid(gate_pre) * up_pre).astype(jnp.bfloat16)
    half = rows.shape[0] // 2
    partial = dot(hidden, ready(3)[...], TN).astype(jnp.bfloat16)
    keep_ref[...] = partial[:half]
    send_ref[...] = partial[half:]


def add_body(ready, outs):
    for n, out_ref in enumerate(outs):
        total = ready(2 * n)[...].astype(jnp.float32) + ready(2 * n + 1)[...].astype(jnp.float32)
        out_ref[...] = total.astype(jnp.bfloat16).reshape(out_ref.shape)


def finish_body(ready, outs):
    sent_ref = ready(3)
    size = outs[0].shape[0]
    for n, out_ref in enumerate(outs):
        total = ready(n)[...] + sent_ref[n * size : (n + 1) * size].astype(jnp.float32)
        out_ref[...] = total.astype(jnp.bfloat16)


def backward_body(ready, outs):
    kept, sent_ref = outs[:3], outs[3]
    cot_ref, down_ref = ready(0), ready(1)
    cots = cot_ref[...]
    hidden_grad = dot(down_ref[...], cots, NT)
    gate_pre = ready(2)[...]
    up_pre = ready(3)[...]
    sigmoid = jax.nn.sigmoid(gate_pre)
    active = gate_pre * sigmoid
    gate_cot = hidden_grad * up_pre * sigmoid * (1.0 + gate_pre * (1.0 - sigmoid))
    up_cot = hidden_grad * active
    half = kept[0].shape[0]
    both = jnp.concatenate([gate_cot.astype(jnp.bfloat16), up_cot.astype(jnp.bfloat16)], axis=0)
    grads = dot(both, ready(4)[...])
    for n in range(2):
        kept[n][...] = grads[2 * n * half : (2 * n + 1) * half]
        sent = grads[(2 * n + 1) * half : (2 * n + 2) * half].astype(jnp.bfloat16)
        sent_ref[n * half : (n + 1) * half] = sent
    grads = dot((active * up_pre).astype(jnp.bfloat16), cots)
    kept[2][...] = grads[:half]
    sent_ref[2 * half :] = grads[half:].astype(jnp.bfloat16)


def combine_body(ready, outs):
    pos_ref, gates_ref = ready(0), ready(1)
    row_ref = ready(2)
    rows = row_ref[...].reshape(-1, row_ref.shape[-1])
    pick = choosers([pos_ref[:, 0:1], pos_ref[:, 1:2]], rows.shape[0])
    picked = dot(jnp.concatenate(pick, axis=0), rows)
    total = ready(3)[...]
    tokens = total.shape[0]
    for k in range(2):
        total = total + column(gates_ref[k : k + 1]) * picked[k * tokens : (k + 1) * tokens]
    outs[0][...] = total.astype(jnp.bfloat16)


def per_device(
    tokens,
    queries,
    keys,
    values,
    out_proj,
    mod_scale,
    mod_shift,
    expert_ids,
    gates,
    w_gate,
    w_up,
    w_down,
    out_grad,
):
    n_ctx = lax.axis_size("ctx")
    groups = lax.axis_size("group")
    experts = n_ctx * groups
    local = tokens.shape[1]
    width = tokens.shape[2]
    hidden = w_gate.shape[0]
    capacity = 3 * local // experts
    slots = experts * capacity
    if capacity % PIECE == 0 and capacity > PIECE:
        blocks, height = experts, capacity
        row_cuts = [(0, capacity - PIECE), (capacity - PIECE, PIECE)]
    else:
        blocks, height = 1, slots
        row_cuts = [(0, slots)]

    def swapped(value, axis):
        return lax.ppermute(value, axis, [(n, n ^ 1) for n in range(lax.axis_size(axis))])

    def exchanged(value):
        shaped = value if blocks > 1 else value.reshape(experts, capacity, width)
        moved = lax.all_to_all(shaped, ("ctx", "group"), split_axis=0, concat_axis=0, tiled=True)
        return moved.reshape(value.shape)

    def turned(value, step):
        size = lax.axis_size("ctx")
        return lax.ppermute(value, "ctx", [(n, (n + step) % size) for n in range(size)])

    def chunk_shapes(cuts):
        return [shape_of(blocks, count, width) for _, count in cuts]

    key_pieces = [keys[0]] + [turned(keys[0], step) for step in range(1, n_ctx)]
    value_pieces = [values[0]] + [turned(values[0], step) for step in range(1, n_ctx)]

    gate_rows = jnp.transpose(gates[0])
    pos, wide_grads = call(
        functools.partial(begin_body, capacity),
        "begin",
        [whole(jnp.transpose(expert_ids[0])), whole(gate_rows), whole(out_grad[0])],
        [shape_of(local, 2, dtype=jnp.int32), shape_of(local, width + 128)],
        1,
    )
    all_grads = lax.all_gather(wide_grads, "group", tiled=True)
    (packed,) = call(
        pack_body,
        "pack",
        [whole(w_gate), whole(w_up), whole(w_down)],
        [shape_of(3 * hidden, width)],
        1,
    )
    other_weights = swapped(packed, "core")

    mixed, *placed = call(
        functools.partial(attend_body, capacity, [first for first, _ in row_cuts]),
        "attend",
        [
            whole(queries[0]),
            rows_of(key_pieces),
            rows_of(value_pieces),
            whole(tokens[0]),
            whole(out_proj),
            whole(mod_scale),
            whole(mod_shift),
            whole(pos),
        ],
        [shape_of(local, width, dtype=jnp.float32)] + chunk_shapes(row_cuts),
        1,
    )
    rows = [exchanged(value) for value in placed]
    rows_across = [swapped(value, "side") for value in rows]

    picked = call(
        functools.partial(select_body, n_ctx, groups, capacity),
        "select",
        [whole(all_grads)],
        [shape_of(groups * capacity, width)] * n_ctx,
        1,
    )
    cots = [picked[0]] + [turned(value, step) for step, value in enumerate(picked) if step]
    cots_across = [swapped(value, "side") for value in cots]

    pairs = []
    for n, weight in enumerate((w_gate, w_up, w_down)):
        second = (other_weights, pl.ds(n * hidden, hidden), pl.ds(hidden, hidden))
        pairs.append(([(weight, None, pl.ds(0, hidden)), second], (2 * hidden, width)))
    gate_pres, up_pres, partials = [], [], []
    after = []
    for (_, count), own, across in zip(row_cuts, rows, rows_across):
        half = blocks * count
        pre = shape_of(2 * hidden, 2 * half, dtype=jnp.float32)
        keep, send, gate_pre, up_pre = call(
            forward_body,
            "forward",
            [([(own, None, 0), (across, None, 1)], (2,) + own.shape)]
            + pairs,
            [shape_of(half, width)] * 2 + [pre] * 2,
            0.1,
            after=after,
        )
        after = [keep]
        gate_pres.append(gate_pre)
        up_pres.append(up_pre)
        partials.append((keep, swapped(send, "side"), count))

    def summed(keep, other, count):
        (sums,) = call(
            add_body,
            "add",
            [whole(keep), whole(other)],
            [shape_of(blocks, count, width)],
            2,
        )
        return sums

    totals = [summed(*partial) for partial in partials]

    total_rows = 2 * slots
    row_pieces, cot_pieces, pre_pieces, line = [], [], [[], []], 0

    def cot_target(start, size, stride, step):
        ctx = (lax.axis_index("ctx") - step) & (n_ctx - 1)
        return pl.ds(pl.multiple_of(start + ctx * stride, 16), size)

    for n, (first, count) in enumerate(row_cuts):
        for side, (own, other) in enumerate(((rows, cots), (rows_across, cots_across))):
            start = line + side * blocks * count
            for block in range(blocks):
                row_pieces.append((own[n], block, pl.ds(start + block * count, count)))
            for step, value in enumerate(other):
                if blocks == 1:
                    size = groups * capacity
                    target = functools.partial(cot_target, start, size, size, step)
                    cot_pieces.append((value, None, target))
                    continue
                for group in range(groups):
                    target = functools.partial(
                        cot_target, start + group * count, count, groups * count, step
                    )
                    source = pl.ds(group * capacity + first, count)
                    cot_pieces.append((value, source, target))
        for pieces, pres in zip(pre_pieces, (gate_pres, up_pres)):
            target = (slice(None), pl.ds(line, 2 * blocks * count))
            pieces.append((pres[n], None, target))
        line += 2 * blocks * count
    *kept, sent = call(
        backward_body,
        "backward",
        [
            (cot_pieces, (total_rows, width)),
            pairs[2],
            (pre_pieces[0], (2 * hidden, total_rows)),
            (pre_pieces[1], (2 * hidden, total_rows)),
            (row_pieces, (total_rows, width)),
        ],
        [shape_of(hidden, width, dtype=jnp.float32)] * 3 + [shape_of(3 * hidden, width)],
        0.1,
        after=totals,
    )
    returned = [exchanged(total) for total in totals]
    grad_gate, grad_up, grad_down = call(
        finish_body,
        "finish",
        [whole(value) for value in kept] + [whole(swapped(sent, "core"))],
        [shape_of(hidden, width)] * 3,
        0.1,
    )

    returned_pieces = []
    for (first, count), value in zip(row_cuts, returned):
        returned_pieces.append((value, None, (slice(None), pl.ds(first, count))))
    (layer_out,) = call(
        combine_body,
        "combine",
        [
            whole(pos),
            whole(gate_rows),
            (returned_pieces, (blocks, height, width)),
            whole(mixed),
        ],
        [shape_of(local, width)],
        3,
        after=[grad_gate],
    )
    return (layer_out[None], grad_gate, grad_up, grad_down)


def solution(mesh):
    n_ctx = mesh.shape["ctx"]
    cut = (n_ctx, mesh.shape["exp"] // SHARDS, SHARDS // 2, 2)
    mesh = jax.sharding.Mesh(mesh.devices.reshape(cut), ("ctx",) + EXP)
    rows = P(EXP, "ctx", None)
    weight = P(("ctx",) + EXP, None)
    return jax.shard_map(
        per_device,
        mesh=mesh,
        in_specs=(rows, rows, rows, rows, P(), P(EXP, None), P(EXP, None), rows, rows)
        + (weight, weight, weight, rows),
        out_specs=(rows, weight, weight, weight),
        check_vma=False,
    )
```

```python
import functools

import jax
import jax.numpy as jnp
from jax import lax
from jax.experimental import pallas as pl
from jax.experimental.pallas import tpu as pltpu
from jax.sharding import PartitionSpec as P

HEADS = 8
HD = 128
SHARDS = 4
PIECE = 16
VMEM_LIMIT = 63 * 1024 * 1024
EXP = ("group", "side", "core")

NT = (((1,), (1,)), ((), ()))
TN = (((0,), (0,)), ((), ()))

VMEM = pl.BlockSpec(memory_space=pltpu.VMEM)
ANY = pl.BlockSpec(memory_space=pl.ANY)


def dot(a, b, dims=(((1,), (0,)), ((), ()))):
    return lax.dot_general(a, b, dims, preferred_element_type=jnp.float32)


def shape_of(*shape, dtype=jnp.bfloat16):
    return jax.ShapeDtypeStruct(shape, dtype)


def call(body, name, operands, outs, micros=1, after=()):
    pieces = [piece for group, _ in operands for piece in group]
    values = []
    for value, _, _ in pieces:
        if not any(value is known for known in values):
            values.append(value)
    where = [[value is known for known in values].index(True) for value, _, _ in pieces]
    n_in, n_outs = len(values) + len(after), len(outs)

    def kernel(*refs):
        out_refs = refs[n_in : n_in + n_outs]
        targets = refs[n_in + n_outs : -1]
        sem = refs[-1]
        waits, at = [], 0
        for (group, _), target in zip(operands, targets):
            copies = []
            for _, source_index, target_index in group:
                source = refs[where[at]]
                copies.append(
                    pltpu.make_async_copy(
                        source if source_index is None else source.at[source_index],
                        target if target_index is None else target.at[target_index],
                        sem.at[at],
                    )
                )
                at += 1
            waits.append(copies)
        for copies in waits:
            for copy in copies:
                copy.start()

        def ready(n):
            for copy in waits[n]:
                copy.wait()
            return targets[n]

        body(ready, out_refs)

    return pl.pallas_call(
        kernel,
        out_shape=tuple(outs),
        in_specs=[ANY] * n_in,
        out_specs=(VMEM,) * n_outs,
        scratch_shapes=[pltpu.VMEM(shape, group[0][0].dtype) for group, shape in operands]
        + [pltpu.SemaphoreType.DMA((len(pieces),))],
        compiler_params=pltpu.CompilerParams(vmem_limit_bytes=VMEM_LIMIT),
        cost_estimate=pl.CostEstimate(
            flops=int(micros * 1.15e9), bytes_accessed=0, transcendentals=0
        ),
        name=name,
    )(*values, *after)


def whole(value):
    return [(value, None, None)], value.shape


def rows_of(values):
    pieces, row = [], 0
    for value in values:
        pieces.append((value, None, pl.ds(row, value.shape[0])))
        row += value.shape[0]
    return pieces, (row, values[0].shape[1])


def column(row):
    size = row.shape[1]
    across = lax.broadcasted_iota(jnp.int32, (size, size), 0)
    along = lax.broadcasted_iota(jnp.int32, (size, size), 1)
    return jnp.sum(jnp.where(across == along, row, jnp.zeros_like(row)), axis=1, keepdims=True)


def choosers(pos, slots):
    line = lax.broadcasted_iota(jnp.int32, (pos[0].shape[0], slots), 1)
    return [(place == line).astype(jnp.bfloat16) for place in pos]


def positions(capacity, ids):
    tokens = ids[0].shape[0]
    lanes = lax.broadcasted_iota(jnp.int32, (tokens, 128), 1)
    hot = [(ids[k] == lanes).astype(jnp.float32) for k in range(2)]
    later = lax.broadcasted_iota(jnp.int32, (tokens, tokens), 0)
    earlier = lax.broadcasted_iota(jnp.int32, (tokens, tokens), 1)
    lower = (later > earlier).astype(jnp.bfloat16)
    before = dot(lower, (hot[0] + hot[1]).astype(jnp.bfloat16))
    pos = []
    for k in range(2):
        slot = jnp.sum(hot[k] * before, axis=1, keepdims=True).astype(jnp.int32)
        pos.append(ids[k] * capacity + slot)
    return pos


def chunk_position(pos, capacity, first, count):
    expert = pos // capacity
    slot = pos - expert * capacity - first
    return jnp.where((slot >= 0) & (slot < count), expert * count + slot, -1)


def place_cots(capacity, first, ready, grad_at, gates, pos, out_ref):
    blocks, count, _ = out_ref.shape
    piece = count if blocks > 1 else capacity
    pick = choosers(
        [chunk_position(place, capacity, first, piece) for place in pos], blocks * count
    )
    grad = ready(grad_at)[...].astype(jnp.float32)
    placed = 0.0
    for k in range(2):
        placed = placed + dot(pick[k], (gates[k] * grad).astype(jnp.bfloat16), TN)
    out_ref[...] = placed.astype(jnp.bfloat16).reshape(out_ref.shape)


def slots_body(capacity, ready, outs):
    pos_ref, cot_ref = outs
    ids_ref = ready(0)
    pos = positions(capacity, [column(ids_ref[k : k + 1]) for k in range(2)])
    pair = lax.broadcasted_iota(jnp.int32, (pos[0].shape[0], 2), 1)
    pos_ref[...] = jnp.where(pair == 0, pos[0], pos[1])
    gates_ref = ready(1)
    gates = [column(gates_ref[k : k + 1]) for k in range(2)]
    place_cots(capacity, 0, ready, 2, gates, pos, cot_ref)


def late_slots_body(capacity, first, ready, outs):
    pos_ref, gates_ref = ready(0), ready(1)
    gates = [column(gates_ref[k : k + 1]) for k in range(2)]
    pos = [pos_ref[:, k : k + 1] for k in range(2)]
    place_cots(capacity, first, ready, 2, gates, pos, outs[0])


def attend_body(ready, outs):
    mixed_ref, normed_ref = outs
    query_ref, key_ref, value_ref = ready(0), ready(1), ready(2)
    parts = []
    for head in range(HEADS):
        cols = slice(head * HD, (head + 1) * HD)
        scores = dot(query_ref[:, cols], key_ref[:, cols], NT) * (HD ** (-0.5))
        weights = jnp.exp(scores - jnp.max(scores, axis=1, keepdims=True))
        total = jnp.sum(weights, axis=1, keepdims=True)
        accum = dot(weights.astype(jnp.bfloat16), value_ref[:, cols])
        parts.append((accum / total).astype(jnp.bfloat16))
    attended = jnp.concatenate(parts, axis=1)
    token_ref, proj_ref = ready(3), ready(4)
    mixed = token_ref[...].astype(jnp.float32) + dot(attended, proj_ref[...])
    mixed_ref[...] = mixed
    mean_square = jnp.mean(mixed * mixed, axis=1, keepdims=True)
    scale_ref, shift_ref = ready(5), ready(6)
    normed = mixed * lax.rsqrt(mean_square + 1e-06) * (1.0 + scale_ref[...]) + shift_ref[...]
    normed_ref[...] = normed.astype(jnp.bfloat16)


def place_body(capacity, firsts, ready, outs):
    pos_ref = ready(0)
    pos = [pos_ref[:, k : k + 1] for k in range(2)]
    normed = ready(1)[...]
    for first, out_ref in zip(firsts, outs):
        blocks, count, _ = out_ref.shape
        piece = count if blocks > 1 else capacity
        pick = choosers(
            [chunk_position(place, capacity, first, piece) for place in pos], blocks * count
        )
        placed = dot(pick[0] + pick[1], normed, TN).astype(jnp.bfloat16)
        out_ref[...] = placed.reshape(out_ref.shape)


def forward_body(ready, outs):
    keep_ref, send_ref, gate_pre_ref, up_pre_ref = outs
    row_ref = ready(0)
    rows = row_ref[...].reshape(-1, row_ref.shape[-1])
    gate_pre = dot(ready(1)[...], rows, NT)
    gate_pre_ref[...] = gate_pre
    up_pre = dot(ready(2)[...], rows, NT)
    up_pre_ref[...] = up_pre
    hidden = (gate_pre * jax.nn.sigmoid(gate_pre) * up_pre).astype(jnp.bfloat16)
    half = rows.shape[0] // 2
    partial = dot(hidden, ready(3)[...], TN).astype(jnp.bfloat16)
    keep_ref[...] = partial[:half]
    send_ref[...] = partial[half:]


def add_body(ready, outs):
    for n, out_ref in enumerate(outs):
        total = ready(2 * n)[...].astype(jnp.float32) + ready(2 * n + 1)[...].astype(jnp.float32)
        out_ref[...] = total.astype(jnp.bfloat16).reshape(out_ref.shape)


def finish_body(ready, outs):
    sent_ref = ready(3)
    size = outs[0].shape[0]
    for n, out_ref in enumerate(outs):
        total = ready(n)[...] + sent_ref[n * size : (n + 1) * size].astype(jnp.float32)
        out_ref[...] = total.astype(jnp.bfloat16)


def backward_body(ready, outs):
    kept, sent_ref = outs[:3], outs[3]
    cot_ref, down_ref = ready(0), ready(1)
    cots = cot_ref[...]
    hidden_grad = dot(down_ref[...], cots, NT)
    gate_pre = ready(2)[...]
    up_pre = ready(3)[...]
    sigmoid = jax.nn.sigmoid(gate_pre)
    active = gate_pre * sigmoid
    gate_cot = hidden_grad * up_pre * sigmoid * (1.0 + gate_pre * (1.0 - sigmoid))
    up_cot = hidden_grad * active
    half = kept[0].shape[0]
    both = jnp.concatenate([gate_cot.astype(jnp.bfloat16), up_cot.astype(jnp.bfloat16)], axis=0)
    grads = dot(both, ready(4)[...])
    for n in range(2):
        kept[n][...] = grads[2 * n * half : (2 * n + 1) * half]
        sent = grads[(2 * n + 1) * half : (2 * n + 2) * half].astype(jnp.bfloat16)
        sent_ref[n * half : (n + 1) * half] = sent
    grads = dot((active * up_pre).astype(jnp.bfloat16), cots)
    kept[2][...] = grads[:half]
    sent_ref[2 * half :] = grads[half:].astype(jnp.bfloat16)


def pack_body(ready, outs):
    size = outs[0].shape[0] // 3
    for n in range(3):
        outs[0][n * size : (n + 1) * size] = ready(n)[...]


def combine_body(ready, outs):
    pos_ref, gates_ref = ready(0), ready(1)
    row_ref = ready(2)
    rows = row_ref[...].reshape(-1, row_ref.shape[-1])
    pick = choosers([pos_ref[:, 0:1], pos_ref[:, 1:2]], rows.shape[0])
    picked = dot(jnp.concatenate(pick, axis=0), rows)
    total = ready(3)[...]
    tokens = total.shape[0]
    for k in range(2):
        total = total + column(gates_ref[k : k + 1]) * picked[k * tokens : (k + 1) * tokens]
    outs[0][...] = total.astype(jnp.bfloat16)


def per_device(
    tokens,
    queries,
    keys,
    values,
    out_proj,
    mod_scale,
    mod_shift,
    expert_ids,
    gates,
    w_gate,
    w_up,
    w_down,
    out_grad,
):
    n_ctx = lax.axis_size("ctx")
    experts = n_ctx * lax.axis_size("group")
    local = tokens.shape[1]
    width = tokens.shape[2]
    hidden = w_gate.shape[0]
    capacity = 3 * local // experts
    slots = experts * capacity
    if capacity % PIECE == 0 and capacity > PIECE:
        blocks, height = experts, capacity
        row_cuts = [(0, capacity - PIECE), (capacity - PIECE, PIECE)]
        cot_cuts = [(0, PIECE), (PIECE, capacity - PIECE)]
    else:
        blocks, height = 1, slots
        row_cuts = cot_cuts = [(0, slots)]

    def swapped(value, axis):
        return lax.ppermute(value, axis, [(n, n ^ 1) for n in range(lax.axis_size(axis))])

    def exchanged(value):
        shaped = value if blocks > 1 else value.reshape(experts, capacity, width)
        moved = lax.all_to_all(shaped, ("ctx", "group"), split_axis=0, concat_axis=0, tiled=True)
        return moved.reshape(value.shape)

    def turned(value, step):
        size = lax.axis_size("ctx")
        return lax.ppermute(value, "ctx", [(n, (n + step) % size) for n in range(size)])

    def chunk_shapes(cuts):
        return [shape_of(blocks, count, width) for _, count in cuts]

    key_pieces = [keys[0]] + [turned(keys[0], step) for step in range(1, n_ctx)]
    value_pieces = [values[0]] + [turned(values[0], step) for step in range(1, n_ctx)]

    ids_rows = jnp.transpose(expert_ids[0])
    gate_rows = jnp.transpose(gates[0])
    pos, first_cots = call(
        functools.partial(slots_body, capacity),
        "slots",
        [whole(ids_rows), whole(gate_rows), whole(out_grad[0])],
        [shape_of(local, 2, dtype=jnp.int32)] + chunk_shapes(cot_cuts[:1]),
        0.35,
    )
    cots = [exchanged(first_cots)]
    cots_across = [swapped(cots[0], "side")]

    (packed,) = call(
        pack_body,
        "pack",
        [whole(w_gate), whole(w_up), whole(w_down)],
        [shape_of(3 * hidden, width)],
        0,
    )
    other_weights = swapped(packed, "core")

    mixed, normed = call(
        attend_body,
        "attend",
        [
            whole(queries[0]),
            rows_of(key_pieces),
            rows_of(value_pieces),
            whole(tokens[0]),
            whole(out_proj),
            whole(mod_scale),
            whole(mod_shift),
        ],
        [shape_of(local, width, dtype=jnp.float32), shape_of(local, width)],
        0.93,
    )
    placed = call(
        functools.partial(place_body, capacity, [first for first, _ in row_cuts]),
        "place",
        [whole(pos), whole(normed)],
        chunk_shapes(row_cuts),
        0.2,
        after=cots + [other_weights],
    )
    rows = [exchanged(value) for value in placed]
    rows_across = [swapped(value, "side") for value in rows]

    for first, count in cot_cuts[1:]:
        (late_cots,) = call(
            functools.partial(late_slots_body, capacity, first),
            "late_slots",
            [whole(pos), whole(gate_rows), whole(out_grad[0])],
            [shape_of(blocks, count, width)],
            0.35,
            after=rows,
        )
        cots.append(exchanged(late_cots))
        cots_across.append(swapped(cots[-1], "side"))

    pairs = []
    for n, weight in enumerate((w_gate, w_up, w_down)):
        second = (other_weights, pl.ds(n * hidden, hidden), pl.ds(hidden, hidden))
        pairs.append(([(weight, None, pl.ds(0, hidden)), second], (2 * hidden, width)))
    gate_pres, up_pres, partials = [], [], []
    after = []
    for (_, count), own, across in zip(row_cuts, rows, rows_across):
        half = blocks * count
        pre = shape_of(2 * hidden, 2 * half, dtype=jnp.float32)
        keep, send, gate_pre, up_pre = call(
            forward_body,
            "forward",
            [([(own, None, 0), (across, None, 1)], (2,) + own.shape)]
            + pairs,
            [shape_of(half, width)] * 2 + [pre] * 2,
            24e-6 * half * hidden * width / 1150,
            after=after,
        )
        after = [keep]
        gate_pres.append(gate_pre)
        up_pres.append(up_pre)
        partials.append((keep, swapped(send, "side"), count))

    def summed(keep, other, count):
        (sums,) = call(
            add_body,
            "add",
            [whole(keep), whole(other)],
            [shape_of(blocks, count, width)],
            0,
        )
        return sums

    returned = [exchanged(summed(*partial)) for partial in partials]

    total_rows = 2 * slots
    row_pieces, cot_pieces, pre_pieces, line = [], [], [[], []], 0
    for n, (first, count) in enumerate(row_cuts):
        for side, both in enumerate(((rows, cots), (rows_across, cots_across))):
            for block in range(blocks):
                start = line + (side * blocks + block) * count
                row_pieces.append((both[0][n], block, pl.ds(start, count)))
                for (cot_first, cot_count), value in zip(cot_cuts, both[1]):
                    low = max(first, cot_first)
                    high = min(first + count, cot_first + cot_count)
                    if low < high:
                        source = (block, pl.ds(low - cot_first, high - low))
                        cot_pieces.append((value, source, pl.ds(start + low - first, high - low)))
        for pieces, pres in zip(pre_pieces, (gate_pres, up_pres)):
            target = (slice(None), pl.ds(line, 2 * blocks * count))
            pieces.append((pres[n], None, target))
        line += 2 * blocks * count
    *kept, sent = call(
        backward_body,
        "backward",
        [
            (cot_pieces, (total_rows, width)),
            pairs[2],
            (pre_pieces[0], (2 * hidden, total_rows)),
            (pre_pieces[1], (2 * hidden, total_rows)),
            (row_pieces, (total_rows, width)),
        ],
        [shape_of(hidden, width, dtype=jnp.float32)] * 3 + [shape_of(3 * hidden, width)],
        16e-6 * total_rows * hidden * width / 1150,
    )
    grad_gate, grad_up, grad_down = call(
        finish_body,
        "finish",
        [whole(value) for value in kept] + [whole(swapped(sent, "core"))],
        [shape_of(hidden, width)] * 3,
        0,
    )

    returned_pieces = []
    for (first, count), value in zip(row_cuts, returned):
        returned_pieces.append((value, None, (slice(None), pl.ds(first, count))))
    (layer_out,) = call(
        combine_body,
        "combine",
        [
            whole(pos),
            whole(gate_rows),
            (returned_pieces, (blocks, height, width)),
            whole(mixed),
        ],
        [shape_of(local, width)],
        0.35,
    )
    return (layer_out[None], grad_gate, grad_up, grad_down)


def solution(mesh):
    n_ctx = mesh.shape["ctx"]
    cut = (n_ctx, mesh.shape["exp"] // SHARDS, SHARDS // 2, 2)
    mesh = jax.sharding.Mesh(mesh.devices.reshape(cut), ("ctx",) + EXP)
    rows = P(EXP, "ctx", None)
    weight = P(("ctx",) + EXP, None)
    return jax.shard_map(
        per_device,
        mesh=mesh,
        in_specs=(rows, rows, rows, rows, P(), P(EXP, None), P(EXP, None), rows, rows)
        + (weight, weight, weight, rows),
        out_specs=(rows, weight, weight, weight),
        check_vma=False,
    )
```

```python
import functools

import jax
import jax.numpy as jnp
from jax import lax
from jax.experimental import pallas as pl
from jax.experimental.pallas import tpu as pltpu
from jax.sharding import PartitionSpec as P

HEADS = 8
HD = 128
SHARDS = 4
PIECE = 16
VMEM_LIMIT = 60 * 1024 * 1024
EXP = ("group", "side", "core")

NT = (((1,), (1,)), ((), ()))
TN = (((0,), (0,)), ((), ()))

VMEM = pl.BlockSpec(memory_space=pltpu.VMEM)
ANY = pl.BlockSpec(memory_space=pl.ANY)


def dot(a, b, dims=(((1,), (0,)), ((), ()))):
    return lax.dot_general(a, b, dims, preferred_element_type=jnp.float32)


def shape_of(*shape, dtype=jnp.bfloat16):
    return jax.ShapeDtypeStruct(shape, dtype)


def call(body, name, operands, outs, flops=0, after=()):
    pieces = [piece for group, _ in operands for piece in group]
    values = []
    for value, _, _ in pieces:
        if not any(value is known for known in values):
            values.append(value)
    where = [[value is known for known in values].index(True) for value, _, _ in pieces]
    n_in, n_outs = len(values) + len(after), len(outs)

    def kernel(*refs):
        out_refs = refs[n_in : n_in + n_outs]
        targets = refs[n_in + n_outs : -1]
        sem = refs[-1]
        waits, at = [], 0
        for (group, _), target in zip(operands, targets):
            copies = []
            for _, source_index, target_index in group:
                source = refs[where[at]]
                copies.append(
                    pltpu.make_async_copy(
                        source if source_index is None else source.at[source_index],
                        target if target_index is None else target.at[target_index],
                        sem.at[at],
                    )
                )
                at += 1
            waits.append(copies)
        for copies in waits:
            for copy in copies:
                copy.start()

        def ready(n):
            for copy in waits[n]:
                copy.wait()
            return targets[n]

        body(ready, out_refs)

    moved = sum(v.size * v.dtype.itemsize for v in values)
    return pl.pallas_call(
        kernel,
        out_shape=tuple(outs),
        in_specs=[ANY] * n_in,
        out_specs=(VMEM,) * n_outs,
        scratch_shapes=[pltpu.VMEM(shape, group[0][0].dtype) for group, shape in operands]
        + [pltpu.SemaphoreType.DMA((len(pieces),))],
        compiler_params=pltpu.CompilerParams(vmem_limit_bytes=VMEM_LIMIT),
        cost_estimate=pl.CostEstimate(flops=flops, bytes_accessed=moved, transcendentals=0),
        name=name,
    )(*values, *after)


def whole(value):
    return [(value, None, None)], value.shape


def rows_of(values):
    pieces, row = [], 0
    for value in values:
        pieces.append((value, None, pl.ds(row, value.shape[0])))
        row += value.shape[0]
    return pieces, (row, values[0].shape[1])


def column(row):
    size = row.shape[1]
    across = lax.broadcasted_iota(jnp.int32, (size, size), 0)
    along = lax.broadcasted_iota(jnp.int32, (size, size), 1)
    return jnp.sum(jnp.where(across == along, row, jnp.zeros_like(row)), axis=1, keepdims=True)


def choosers(pos, slots):
    line = lax.broadcasted_iota(jnp.int32, (pos[0].shape[0], slots), 1)
    return [(place == line).astype(jnp.bfloat16) for place in pos]


def positions(capacity, ids):
    tokens = ids[0].shape[0]
    lanes = lax.broadcasted_iota(jnp.int32, (tokens, 128), 1)
    hot = [(ids[k] == lanes).astype(jnp.float32) for k in range(2)]
    later = lax.broadcasted_iota(jnp.int32, (tokens, tokens), 0)
    earlier = lax.broadcasted_iota(jnp.int32, (tokens, tokens), 1)
    lower = (later > earlier).astype(jnp.bfloat16)
    before = dot(lower, (hot[0] + hot[1]).astype(jnp.bfloat16))
    pos = []
    for k in range(2):
        slot = jnp.sum(hot[k] * before, axis=1, keepdims=True).astype(jnp.int32)
        pos.append(ids[k] * capacity + slot)
    return pos


def chunk_position(pos, capacity, first, count):
    expert = pos // capacity
    slot = pos - expert * capacity - first
    return jnp.where((slot >= 0) & (slot < count), expert * count + slot, -1)


def place_cots(capacity, first, ready, grad_at, gates, pos, out_ref):
    blocks, count, _ = out_ref.shape
    piece = count if blocks > 1 else capacity
    pick = choosers(
        [chunk_position(place, capacity, first, piece) for place in pos], blocks * count
    )
    grad = ready(grad_at)[...].astype(jnp.float32)
    placed = 0.0
    for k in range(2):
        placed = placed + dot(pick[k], (gates[k] * grad).astype(jnp.bfloat16), TN)
    out_ref[...] = placed.astype(jnp.bfloat16).reshape(out_ref.shape)


def slots_body(capacity, ready, outs):
    pos_ref, cot_ref = outs
    ids_ref = ready(0)
    pos = positions(capacity, [column(ids_ref[k : k + 1]) for k in range(2)])
    pair = lax.broadcasted_iota(jnp.int32, (pos[0].shape[0], 2), 1)
    pos_ref[...] = jnp.where(pair == 0, pos[0], pos[1])
    gates_ref = ready(1)
    gates = [column(gates_ref[k : k + 1]) for k in range(2)]
    place_cots(capacity, 0, ready, 2, gates, pos, cot_ref)


def late_slots_body(capacity, first, ready, outs):
    pos_ref, gates_ref = ready(0), ready(1)
    gates = [column(gates_ref[k : k + 1]) for k in range(2)]
    pos = [pos_ref[:, k : k + 1] for k in range(2)]
    place_cots(capacity, first, ready, 2, gates, pos, outs[0])


def attend_body(ready, outs):
    mixed_ref, normed_ref = outs
    query_ref, key_ref, value_ref = ready(0), ready(1), ready(2)
    parts = []
    for head in range(HEADS):
        cols = slice(head * HD, (head + 1) * HD)
        scores = dot(query_ref[:, cols], key_ref[:, cols], NT) * (HD ** (-0.5))
        weights = jnp.exp(scores - jnp.max(scores, axis=1, keepdims=True))
        total = jnp.sum(weights, axis=1, keepdims=True)
        accum = dot(weights.astype(jnp.bfloat16), value_ref[:, cols])
        parts.append((accum / total).astype(jnp.bfloat16))
    attended = jnp.concatenate(parts, axis=1)
    token_ref, proj_ref = ready(3), ready(4)
    mixed = token_ref[...].astype(jnp.float32) + dot(attended, proj_ref[...])
    mixed_ref[...] = mixed
    mean_square = jnp.mean(mixed * mixed, axis=1, keepdims=True)
    scale_ref, shift_ref = ready(5), ready(6)
    normed = mixed * lax.rsqrt(mean_square + 1e-06) * (1.0 + scale_ref[...]) + shift_ref[...]
    normed_ref[...] = normed.astype(jnp.bfloat16)


def place_body(capacity, firsts, ready, outs):
    pos_ref = ready(0)
    pos = [pos_ref[:, k : k + 1] for k in range(2)]
    normed = ready(1)[...]
    for first, out_ref in zip(firsts, outs):
        blocks, count, _ = out_ref.shape
        piece = count if blocks > 1 else capacity
        pick = choosers(
            [chunk_position(place, capacity, first, piece) for place in pos], blocks * count
        )
        placed = dot(pick[0] + pick[1], normed, TN).astype(jnp.bfloat16)
        out_ref[...] = placed.reshape(out_ref.shape)


def forward_body(ready, outs):
    keep_ref, send_ref, gate_pre_ref, up_pre_ref = outs
    row_ref = ready(0)
    rows = row_ref[...].reshape(-1, row_ref.shape[-1])
    gate_pre = dot(ready(1)[...], rows, NT)
    gate_pre_ref[...] = gate_pre
    up_pre = dot(ready(2)[...], rows, NT)
    up_pre_ref[...] = up_pre
    hidden = (gate_pre * jax.nn.sigmoid(gate_pre) * up_pre).astype(jnp.bfloat16)
    half = rows.shape[0] // 2
    partial = dot(hidden, ready(3)[...], TN).astype(jnp.bfloat16)
    keep_ref[...] = partial[:half]
    send_ref[...] = partial[half:]


def add_body(ready, outs):
    for n, out_ref in enumerate(outs):
        total = ready(2 * n)[...].astype(jnp.float32) + ready(2 * n + 1)[...].astype(jnp.float32)
        out_ref[...] = total.astype(jnp.bfloat16).reshape(out_ref.shape)


def backward_body(ready, outs):
    kept, sent = outs[:3], outs[3:]
    cot_ref, down_ref = ready(0), ready(1)
    cots = cot_ref[...]
    hidden_grad = dot(down_ref[...], cots, NT)
    gate_pre = ready(2)[...]
    up_pre = ready(3)[...]
    sigmoid = jax.nn.sigmoid(gate_pre)
    active = gate_pre * sigmoid
    gate_cot = hidden_grad * up_pre * sigmoid * (1.0 + gate_pre * (1.0 - sigmoid))
    up_cot = hidden_grad * active
    half = kept[0].shape[0]
    both = jnp.concatenate([gate_cot.astype(jnp.bfloat16), up_cot.astype(jnp.bfloat16)], axis=0)
    grads = dot(both, ready(4)[...])
    for n in range(2):
        kept[n][...] = grads[2 * n * half : (2 * n + 1) * half].astype(jnp.bfloat16)
        sent[n][...] = grads[(2 * n + 1) * half : (2 * n + 2) * half].astype(jnp.bfloat16)
    grads = dot((active * up_pre).astype(jnp.bfloat16), cots)
    kept[2][...] = grads[:half].astype(jnp.bfloat16)
    sent[2][...] = grads[half:].astype(jnp.bfloat16)


def combine_body(ready, outs):
    pos_ref, gates_ref = ready(0), ready(1)
    row_ref = ready(2)
    rows = row_ref[...].reshape(-1, row_ref.shape[-1])
    pick = choosers([pos_ref[:, 0:1], pos_ref[:, 1:2]], rows.shape[0])
    picked = dot(jnp.concatenate(pick, axis=0), rows)
    total = ready(3)[...]
    tokens = total.shape[0]
    for k in range(2):
        total = total + column(gates_ref[k : k + 1]) * picked[k * tokens : (k + 1) * tokens]
    outs[0][...] = total.astype(jnp.bfloat16)


def per_device(
    tokens,
    queries,
    keys,
    values,
    out_proj,
    mod_scale,
    mod_shift,
    expert_ids,
    gates,
    w_gate,
    w_up,
    w_down,
    out_grad,
):
    n_ctx = lax.axis_size("ctx")
    experts = n_ctx * lax.axis_size("group")
    local = tokens.shape[1]
    width = tokens.shape[2]
    hidden = w_gate.shape[0]
    capacity = 3 * local // experts
    slots = experts * capacity
    if capacity % PIECE == 0 and capacity > PIECE:
        blocks, height = experts, capacity
        row_cuts = [(0, capacity - PIECE), (capacity - PIECE, PIECE)]
        cot_cuts = [(0, PIECE), (PIECE, capacity - PIECE)]
    else:
        blocks, height = 1, slots
        row_cuts = cot_cuts = [(0, slots)]

    def swapped(value, axis):
        return lax.ppermute(value, axis, [(n, n ^ 1) for n in range(lax.axis_size(axis))])

    def exchanged(value):
        shaped = value if blocks > 1 else value.reshape(experts, capacity, width)
        moved = lax.all_to_all(shaped, ("ctx", "group"), split_axis=0, concat_axis=0, tiled=True)
        return moved.reshape(value.shape)

    def turned(value, step):
        size = lax.axis_size("ctx")
        return lax.ppermute(value, "ctx", [(n, (n + step) % size) for n in range(size)])

    def chunk_shapes(cuts):
        return [shape_of(blocks, count, width) for _, count in cuts]

    key_pieces = [keys[0]] + [turned(keys[0], step) for step in range(1, n_ctx)]
    value_pieces = [values[0]] + [turned(values[0], step) for step in range(1, n_ctx)]

    ids_rows = jnp.transpose(expert_ids[0])
    gate_rows = jnp.transpose(gates[0])
    pos, first_cots = call(
        functools.partial(slots_body, capacity),
        "slots",
        [whole(ids_rows), whole(gate_rows), whole(out_grad[0])],
        [shape_of(local, 2, dtype=jnp.int32)] + chunk_shapes(cot_cuts[:1]),
        flops=4 * slots * local * width,
    )
    cots = [exchanged(first_cots)]
    cots_across = [swapped(cots[0], "side")]

    mixed, normed = call(
        attend_body,
        "attend",
        [
            whole(queries[0]),
            rows_of(key_pieces),
            rows_of(value_pieces),
            whole(tokens[0]),
            whole(out_proj),
            whole(mod_scale),
            whole(mod_shift),
        ],
        [shape_of(local, width, dtype=jnp.float32), shape_of(local, width)],
        flops=4 * local * HEADS * HD * width,
    )
    placed = call(
        functools.partial(place_body, capacity, [first for first, _ in row_cuts]),
        "place",
        [whole(pos), whole(normed)],
        chunk_shapes(row_cuts),
        flops=2 * slots * local * width,
        after=cots,
    )
    rows = [exchanged(value) for value in placed]
    rows_across = [swapped(value, "side") for value in rows]

    for first, count in cot_cuts[1:]:
        (late_cots,) = call(
            functools.partial(late_slots_body, capacity, first),
            "late_slots",
            [whole(pos), whole(gate_rows), whole(out_grad[0])],
            [shape_of(blocks, count, width)],
            flops=4 * slots * local * width,
            after=rows,
        )
        cots.append(exchanged(late_cots))
        cots_across.append(swapped(cots[-1], "side"))

    pairs = [[weight, swapped(weight, "core")] for weight in (w_gate, w_up, w_down)]
    gate_pres, up_pres, returned = [], [], []
    after = []
    for (_, count), own, across in zip(row_cuts, rows, rows_across):
        half = blocks * count
        pre = shape_of(2 * hidden, 2 * half, dtype=jnp.float32)
        keep, send, gate_pre, up_pre = call(
            forward_body,
            "forward",
            [([(own, None, 0), (across, None, 1)], (2,) + own.shape)]
            + [rows_of(pair) for pair in pairs],
            [shape_of(half, width)] * 2 + [pre] * 2,
            flops=24 * half * hidden * width,
            after=after,
        )
        after = [keep] + cots_across[:1]
        gate_pres.append(gate_pre)
        up_pres.append(up_pre)
        (sums,) = call(
            add_body,
            "add",
            [whole(keep), whole(swapped(send, "side"))],
            [shape_of(blocks, count, width)],
        )
        returned.append(exchanged(sums))

    total_rows = 2 * slots
    row_pieces, cot_pieces, pre_pieces, line = [], [], [[], []], 0
    for n, (first, count) in enumerate(row_cuts):
        for side, both in enumerate(((rows, cots), (rows_across, cots_across))):
            for block in range(blocks):
                start = line + (side * blocks + block) * count
                row_pieces.append((both[0][n], block, pl.ds(start, count)))
                for (cot_first, cot_count), value in zip(cot_cuts, both[1]):
                    low = max(first, cot_first)
                    high = min(first + count, cot_first + cot_count)
                    if low < high:
                        source = (block, pl.ds(low - cot_first, high - low))
                        cot_pieces.append((value, source, pl.ds(start + low - first, high - low)))
        for pieces, pres in zip(pre_pieces, (gate_pres, up_pres)):
            target = (slice(None), pl.ds(line, 2 * blocks * count))
            pieces.append((pres[n], None, target))
        line += 2 * blocks * count
    grads = call(
        backward_body,
        "backward",
        [
            (cot_pieces, (total_rows, width)),
            rows_of(pairs[2]),
            (pre_pieces[0], (2 * hidden, total_rows)),
            (pre_pieces[1], (2 * hidden, total_rows)),
            (row_pieces, (total_rows, width)),
        ],
        [shape_of(hidden, width)] * 6,
        flops=16 * total_rows * hidden * width,
    )
    operands = []
    for kept, sent in zip(grads[:3], grads[3:]):
        operands += [whole(kept), whole(swapped(sent, "core"))]
    grad_gate, grad_up, grad_down = call(
        add_body, "finish", operands, [shape_of(hidden, width)] * 3
    )

    returned_pieces = []
    for (first, count), value in zip(row_cuts, returned):
        returned_pieces.append((value, None, (slice(None), pl.ds(first, count))))
    (layer_out,) = call(
        combine_body,
        "combine",
        [
            whole(pos),
            whole(gate_rows),
            (returned_pieces, (blocks, height, width)),
            whole(mixed),
        ],
        [shape_of(local, width)],
        flops=4 * slots * local * width,
    )
    return (layer_out[None], grad_gate, grad_up, grad_down)


def solution(mesh):
    n_ctx = mesh.shape["ctx"]
    cut = (n_ctx, mesh.shape["exp"] // SHARDS, SHARDS // 2, 2)
    mesh = jax.sharding.Mesh(mesh.devices.reshape(cut), ("ctx",) + EXP)
    rows = P(EXP, "ctx", None)
    weight = P(("ctx",) + EXP, None)
    return jax.shard_map(
        per_device,
        mesh=mesh,
        in_specs=(rows, rows, rows, rows, P(), P(EXP, None), P(EXP, None), rows, rows)
        + (weight, weight, weight, rows),
        out_specs=(rows, weight, weight, weight),
        check_vma=False,
    )
```

```python
import functools

import jax
import jax.numpy as jnp
from jax import lax
from jax.experimental import pallas as pl
from jax.experimental.pallas import tpu as pltpu
from jax.sharding import PartitionSpec as P

HEADS = 8
HD = 128
SHARDS = 4
PIECE = 16
VMEM_LIMIT = 60 * 1024 * 1024
EXP = ("group", "side", "core")

NT = (((1,), (1,)), ((), ()))
TN = (((0,), (0,)), ((), ()))

VMEM = pl.BlockSpec(memory_space=pltpu.VMEM)
ANY = pl.BlockSpec(memory_space=pl.ANY)


def dot(a, b, dims=(((1,), (0,)), ((), ()))):
    return lax.dot_general(a, b, dims, preferred_element_type=jnp.float32)


def shape_of(*shape, dtype=jnp.bfloat16):
    return jax.ShapeDtypeStruct(shape, dtype)


def call(body, name, operands, outs, flops=0, after=()):
    pieces = [piece for group, _ in operands for piece in group]
    values = []
    for value, _, _ in pieces:
        if not any(value is known for known in values):
            values.append(value)
    where = [[value is known for known in values].index(True) for value, _, _ in pieces]
    n_in, n_outs = len(values) + len(after), len(outs)

    def kernel(*refs):
        out_refs = refs[n_in : n_in + n_outs]
        targets = refs[n_in + n_outs : -1]
        sem = refs[-1]
        waits, at = [], 0
        for (group, _), target in zip(operands, targets):
            copies = []
            for _, source_index, target_index in group:
                source = refs[where[at]]
                copies.append(
                    pltpu.make_async_copy(
                        source if source_index is None else source.at[source_index],
                        target if target_index is None else target.at[target_index],
                        sem.at[at],
                    )
                )
                at += 1
            waits.append(copies)
        for copies in waits:
            for copy in copies:
                copy.start()

        def ready(n):
            for copy in waits[n]:
                copy.wait()
            return targets[n]

        body(ready, out_refs)

    moved = sum(v.size * v.dtype.itemsize for v in values)
    return pl.pallas_call(
        kernel,
        out_shape=tuple(outs),
        in_specs=[ANY] * n_in,
        out_specs=(VMEM,) * n_outs,
        scratch_shapes=[pltpu.VMEM(shape, group[0][0].dtype) for group, shape in operands]
        + [pltpu.SemaphoreType.DMA((len(pieces),))],
        compiler_params=pltpu.CompilerParams(vmem_limit_bytes=VMEM_LIMIT),
        cost_estimate=pl.CostEstimate(flops=flops, bytes_accessed=moved, transcendentals=0),
        name=name,
    )(*values, *after)


def whole(value):
    return [(value, None, None)], value.shape


def rows_of(values):
    pieces, row = [], 0
    for value in values:
        pieces.append((value, None, pl.ds(row, value.shape[0])))
        row += value.shape[0]
    return pieces, (row, values[0].shape[1])


def column(row):
    size = row.shape[1]
    across = lax.broadcasted_iota(jnp.int32, (size, size), 0)
    along = lax.broadcasted_iota(jnp.int32, (size, size), 1)
    return jnp.sum(jnp.where(across == along, row, jnp.zeros_like(row)), axis=1, keepdims=True)


def choosers(pos, slots):
    line = lax.broadcasted_iota(jnp.int32, (pos[0].shape[0], slots), 1)
    return [(place == line).astype(jnp.bfloat16) for place in pos]


def positions(capacity, ids):
    tokens = ids[0].shape[0]
    lanes = lax.broadcasted_iota(jnp.int32, (tokens, 128), 1)
    hot = [(ids[k] == lanes).astype(jnp.float32) for k in range(2)]
    later = lax.broadcasted_iota(jnp.int32, (tokens, tokens), 0)
    earlier = lax.broadcasted_iota(jnp.int32, (tokens, tokens), 1)
    lower = (later > earlier).astype(jnp.bfloat16)
    before = dot(lower, (hot[0] + hot[1]).astype(jnp.bfloat16))
    pos = []
    for k in range(2):
        slot = jnp.sum(hot[k] * before, axis=1, keepdims=True).astype(jnp.int32)
        pos.append(ids[k] * capacity + slot)
    return pos


def chunk_position(pos, capacity, first, count):
    expert = pos // capacity
    slot = pos - expert * capacity - first
    return jnp.where((slot >= 0) & (slot < count), expert * count + slot, -1)


def place_cots(capacity, first, ready, grad_at, gates, pos, out_ref):
    blocks, count, _ = out_ref.shape
    piece = count if blocks > 1 else capacity
    pick = choosers(
        [chunk_position(place, capacity, first, piece) for place in pos], blocks * count
    )
    grad = ready(grad_at)[...].astype(jnp.float32)
    placed = 0.0
    for k in range(2):
        placed = placed + dot(pick[k], (gates[k] * grad).astype(jnp.bfloat16), TN)
    out_ref[...] = placed.astype(jnp.bfloat16).reshape(out_ref.shape)


def slots_body(capacity, ready, outs):
    pos_ref, cot_ref = outs
    ids_ref = ready(0)
    pos = positions(capacity, [column(ids_ref[k : k + 1]) for k in range(2)])
    pair = lax.broadcasted_iota(jnp.int32, (pos[0].shape[0], 2), 1)
    pos_ref[...] = jnp.where(pair == 0, pos[0], pos[1])
    gates_ref = ready(1)
    gates = [column(gates_ref[k : k + 1]) for k in range(2)]
    place_cots(capacity, 0, ready, 2, gates, pos, cot_ref)


def late_slots_body(capacity, first, ready, outs):
    pos_ref, gates_ref = ready(0), ready(1)
    gates = [column(gates_ref[k : k + 1]) for k in range(2)]
    pos = [pos_ref[:, k : k + 1] for k in range(2)]
    place_cots(capacity, first, ready, 2, gates, pos, outs[0])


def attend_body(ready, outs):
    mixed_ref, normed_ref = outs
    query_ref, key_ref, value_ref = ready(0), ready(1), ready(2)
    parts = []
    for head in range(HEADS):
        cols = slice(head * HD, (head + 1) * HD)
        scores = dot(query_ref[:, cols], key_ref[:, cols], NT) * (HD ** (-0.5))
        weights = jnp.exp(scores - jnp.max(scores, axis=1, keepdims=True))
        total = jnp.sum(weights, axis=1, keepdims=True)
        accum = dot(weights.astype(jnp.bfloat16), value_ref[:, cols])
        parts.append((accum / total).astype(jnp.bfloat16))
    attended = jnp.concatenate(parts, axis=1)
    token_ref, proj_ref = ready(3), ready(4)
    mixed = token_ref[...].astype(jnp.float32) + dot(attended, proj_ref[...])
    mixed_ref[...] = mixed
    mean_square = jnp.mean(mixed * mixed, axis=1, keepdims=True)
    scale_ref, shift_ref = ready(5), ready(6)
    normed = mixed * lax.rsqrt(mean_square + 1e-06) * (1.0 + scale_ref[...]) + shift_ref[...]
    normed_ref[...] = normed.astype(jnp.bfloat16)


def place_body(capacity, firsts, ready, outs):
    pos_ref = ready(0)
    pos = [pos_ref[:, k : k + 1] for k in range(2)]
    normed = ready(1)[...]
    for first, out_ref in zip(firsts, outs):
        blocks, count, _ = out_ref.shape
        piece = count if blocks > 1 else capacity
        pick = choosers(
            [chunk_position(place, capacity, first, piece) for place in pos], blocks * count
        )
        placed = dot(pick[0] + pick[1], normed, TN).astype(jnp.bfloat16)
        out_ref[...] = placed.reshape(out_ref.shape)


def forward_body(ready, outs):
    keep_ref, send_ref, gate_pre_ref, up_pre_ref = outs
    row_ref = ready(0)
    rows = row_ref[...].reshape(-1, row_ref.shape[-1])
    gate_pre = dot(ready(1)[...], rows, NT)
    gate_pre_ref[...] = gate_pre
    up_pre = dot(ready(2)[...], rows, NT)
    up_pre_ref[...] = up_pre
    hidden = (gate_pre * jax.nn.sigmoid(gate_pre) * up_pre).astype(jnp.bfloat16)
    half = rows.shape[0] // 2
    partial = dot(hidden, ready(3)[...], TN).astype(jnp.bfloat16)
    keep_ref[...] = partial[:half]
    send_ref[...] = partial[half:]


def add_body(ready, outs):
    for n, out_ref in enumerate(outs):
        total = ready(2 * n)[...].astype(jnp.float32) + ready(2 * n + 1)[...].astype(jnp.float32)
        out_ref[...] = total.astype(jnp.bfloat16).reshape(out_ref.shape)


def backward_body(ready, outs):
    kept, sent = outs[:3], outs[3:]
    cot_ref, down_ref = ready(0), ready(1)
    cots = cot_ref[...]
    hidden_grad = dot(down_ref[...], cots, NT)
    gate_pre = ready(2)[...]
    up_pre = ready(3)[...]
    sigmoid = jax.nn.sigmoid(gate_pre)
    active = gate_pre * sigmoid
    gate_cot = hidden_grad * up_pre * sigmoid * (1.0 + gate_pre * (1.0 - sigmoid))
    up_cot = hidden_grad * active
    half = kept[0].shape[0]
    both = jnp.concatenate([gate_cot.astype(jnp.bfloat16), up_cot.astype(jnp.bfloat16)], axis=0)
    grads = dot(both, ready(4)[...])
    for n in range(2):
        kept[n][...] = grads[2 * n * half : (2 * n + 1) * half].astype(jnp.bfloat16)
        sent[n][...] = grads[(2 * n + 1) * half : (2 * n + 2) * half].astype(jnp.bfloat16)
    grads = dot((active * up_pre).astype(jnp.bfloat16), cots)
    kept[2][...] = grads[:half].astype(jnp.bfloat16)
    sent[2][...] = grads[half:].astype(jnp.bfloat16)


def combine_body(ready, outs):
    pos_ref, gates_ref = ready(0), ready(1)
    row_ref = ready(2)
    rows = row_ref[...].reshape(-1, row_ref.shape[-1])
    pick = choosers([pos_ref[:, 0:1], pos_ref[:, 1:2]], rows.shape[0])
    picked = dot(jnp.concatenate(pick, axis=0), rows)
    total = ready(3)[...]
    tokens = total.shape[0]
    for k in range(2):
        total = total + column(gates_ref[k : k + 1]) * picked[k * tokens : (k + 1) * tokens]
    outs[0][...] = total.astype(jnp.bfloat16)


def per_device(
    tokens,
    queries,
    keys,
    values,
    out_proj,
    mod_scale,
    mod_shift,
    expert_ids,
    gates,
    w_gate,
    w_up,
    w_down,
    out_grad,
):
    n_ctx = lax.axis_size("ctx")
    experts = n_ctx * lax.axis_size("group")
    local = tokens.shape[1]
    width = tokens.shape[2]
    hidden = w_gate.shape[0]
    capacity = 3 * local // experts
    slots = experts * capacity
    if capacity % PIECE == 0 and capacity > PIECE:
        blocks, height = experts, capacity
        row_cuts = [(0, capacity - PIECE), (capacity - PIECE, PIECE)]
        cot_cuts = [(0, PIECE), (PIECE, capacity - PIECE)]
    else:
        blocks, height = 1, slots
        row_cuts = cot_cuts = [(0, slots)]

    def swapped(value, axis):
        return lax.ppermute(value, axis, [(n, n ^ 1) for n in range(lax.axis_size(axis))])

    def exchanged(value):
        shaped = value if blocks > 1 else value.reshape(experts, capacity, width)
        moved = lax.all_to_all(shaped, ("ctx", "group"), split_axis=0, concat_axis=0, tiled=True)
        return moved.reshape(value.shape)

    def turned(value, step):
        size = lax.axis_size("ctx")
        return lax.ppermute(value, "ctx", [(n, (n + step) % size) for n in range(size)])

    def chunk_shapes(cuts):
        return [shape_of(blocks, count, width) for _, count in cuts]

    key_pieces = [keys[0]] + [turned(keys[0], step) for step in range(1, n_ctx)]
    value_pieces = [values[0]] + [turned(values[0], step) for step in range(1, n_ctx)]

    ids_rows = jnp.transpose(expert_ids[0])
    gate_rows = jnp.transpose(gates[0])
    pos, first_cots = call(
        functools.partial(slots_body, capacity),
        "slots",
        [whole(ids_rows), whole(gate_rows), whole(out_grad[0])],
        [shape_of(local, 2, dtype=jnp.int32)] + chunk_shapes(cot_cuts[:1]),
        flops=4 * slots * local * width,
    )
    cots = [exchanged(first_cots)]
    cots_across = [swapped(cots[0], "side")]

    mixed, normed = call(
        attend_body,
        "attend",
        [
            whole(queries[0]),
            rows_of(key_pieces),
            rows_of(value_pieces),
            whole(tokens[0]),
            whole(out_proj),
            whole(mod_scale),
            whole(mod_shift),
        ],
        [shape_of(local, width, dtype=jnp.float32), shape_of(local, width)],
        flops=4 * local * HEADS * HD * width,
    )
    placed = call(
        functools.partial(place_body, capacity, [first for first, _ in row_cuts]),
        "place",
        [whole(pos), whole(normed)],
        chunk_shapes(row_cuts),
        flops=2 * slots * local * width,
        after=cots,
    )
    rows = [exchanged(value) for value in placed]
    rows_across = [swapped(value, "side") for value in rows]

    for first, count in cot_cuts[1:]:
        (late_cots,) = call(
            functools.partial(late_slots_body, capacity, first),
            "late_slots",
            [whole(pos), whole(gate_rows), whole(out_grad[0])],
            [shape_of(blocks, count, width)],
            flops=4 * slots * local * width,
            after=rows,
        )
        cots.append(exchanged(late_cots))
        cots_across.append(swapped(cots[-1], "side"))

    pairs = [[weight, swapped(weight, "core")] for weight in (w_gate, w_up, w_down)]
    gate_pres, up_pres, returned = [], [], []
    after = []
    for (_, count), own, across in zip(row_cuts, rows, rows_across):
        half = blocks * count
        pre = shape_of(2 * hidden, 2 * half, dtype=jnp.float32)
        keep, send, gate_pre, up_pre = call(
            forward_body,
            "forward",
            [([(own, None, 0), (across, None, 1)], (2,) + own.shape)]
            + [rows_of(pair) for pair in pairs],
            [shape_of(half, width)] * 2 + [pre] * 2,
            flops=24 * half * hidden * width,
            after=after,
        )
        gate_pres.append(gate_pre)
        up_pres.append(up_pre)
        (sums,) = call(
            add_body,
            "add",
            [whole(keep), whole(swapped(send, "side"))],
            [shape_of(blocks, count, width)],
        )
        after = [sums] + cots_across[:1]
        returned.append(exchanged(sums))

    total_rows = 2 * slots
    row_pieces, cot_pieces, pre_pieces, line = [], [], [[], []], 0
    for n, (first, count) in enumerate(row_cuts):
        for side, both in enumerate(((rows, cots), (rows_across, cots_across))):
            for block in range(blocks):
                start = line + (side * blocks + block) * count
                row_pieces.append((both[0][n], block, pl.ds(start, count)))
                for (cot_first, cot_count), value in zip(cot_cuts, both[1]):
                    low = max(first, cot_first)
                    high = min(first + count, cot_first + cot_count)
                    if low < high:
                        source = (block, pl.ds(low - cot_first, high - low))
                        cot_pieces.append((value, source, pl.ds(start + low - first, high - low)))
        for pieces, pres in zip(pre_pieces, (gate_pres, up_pres)):
            target = (slice(None), pl.ds(line, 2 * blocks * count))
            pieces.append((pres[n], None, target))
        line += 2 * blocks * count
    grads = call(
        backward_body,
        "backward",
        [
            (cot_pieces, (total_rows, width)),
            rows_of(pairs[2]),
            (pre_pieces[0], (2 * hidden, total_rows)),
            (pre_pieces[1], (2 * hidden, total_rows)),
            (row_pieces, (total_rows, width)),
        ],
        [shape_of(hidden, width)] * 6,
        flops=16 * total_rows * hidden * width,
    )
    operands = []
    for kept, sent in zip(grads[:3], grads[3:]):
        operands += [whole(kept), whole(swapped(sent, "core"))]
    grad_gate, grad_up, grad_down = call(
        add_body, "finish", operands, [shape_of(hidden, width)] * 3
    )

    returned_pieces = []
    for (first, count), value in zip(row_cuts, returned):
        returned_pieces.append((value, None, (slice(None), pl.ds(first, count))))
    (layer_out,) = call(
        combine_body,
        "combine",
        [
            whole(pos),
            whole(gate_rows),
            (returned_pieces, (blocks, height, width)),
            whole(mixed),
        ],
        [shape_of(local, width)],
        flops=4 * slots * local * width,
    )
    return (layer_out[None], grad_gate, grad_up, grad_down)


def solution(mesh):
    n_ctx = mesh.shape["ctx"]
    cut = (n_ctx, mesh.shape["exp"] // SHARDS, SHARDS // 2, 2)
    mesh = jax.sharding.Mesh(mesh.devices.reshape(cut), ("ctx",) + EXP)
    rows = P(EXP, "ctx", None)
    weight = P(("ctx",) + EXP, None)
    return jax.shard_map(
        per_device,
        mesh=mesh,
        in_specs=(rows, rows, rows, rows, P(), P(EXP, None), P(EXP, None), rows, rows)
        + (weight, weight, weight, rows),
        out_specs=(rows, weight, weight, weight),
        check_vma=False,
    )
```
